32 devices in a mesh: gx: 2 (over x), gy: 4 (over y, core), gz: 4 (over z).
Axes of the slice: x: 2, y: 2, z: 4, core: 2. Of those that a mesh axis runs over, the one named last changes fastest.
Arguments:
- positions: float32 [3, 16384], P(None, ('gx', 'gy', 'gz')), may hold values from 0 to 1
- features: bfloat16 [64, 16384], P(None, ('gx', 'gy', 'gz')), may hold values from -6 to 6
- species: int32 [16384], P(('gx', 'gy', 'gz')), may hold values from 0 to 3
- species_scale: bfloat16 [4], replicated, may hold values from 0.5 to 2
- w_first: bfloat16 [64, 64], replicated, may hold values from -0.75 to 0.75
- w_second: bfloat16 [64, 64], replicated, may hold values from -0.75 to 0.75
- w_radial: float32 [64, 8], replicated, may hold values from -4 to 4
- w_mid: bfloat16 [64, 64], replicated, may hold values from -0.75 to 0.75
- w_last: bfloat16 [64, 64], replicated, may hold values from -0.75 to 0.75
- w_out: float32 [64], replicated, may hold values from -0.75 to 0.75
- ghost_send: int32 [8192], P(('gx', 'gy', 'gz')), may hold values from 0 to 511
- local_first: int32 [655360], P(('gx', 'gy', 'gz')), may hold values from 0 to 511
- local_second: int32 [655360], P(('gx', 'gy', 'gz')), may hold values from 0 to 511
- local_mask: int32 [655360], P(('gx', 'gy', 'gz')), may hold values 0 or 1
- ghost_owner: int32 [393216], P(('gx', 'gy', 'gz')), may hold values from 0 to 511
- ghost_index: int32 [393216], P(('gx', 'gy', 'gz')), may hold values from 0 to 1791
- ghost_mask: int32 [393216], P(('gx', 'gy', 'gz')), may hold values 0 or 1
Outputs:
- forces: float32 [3, 16384], P(None, ('gx', 'gy', 'gz'))
- atom_energy: float32 [16384], P(('gx', 'gy', 'gz'))
The draws below stay inside these ranges and needn't reach their ends.
Inputs may be any that keep to these rules, and one draw needn't show every extreme that they name: `ghost_send`: rows of the domain's own atoms. `local_first`: owned atoms of the domain. `local_second`: owned atoms of the domain. `ghost_owner`: owned atoms of the domain. `ghost_index`: ghost rows of the domain.
All inputs are finite; a program needn't handle non-finite values. No bound on the sum of `local_mask` or of `ghost_mask` on one device may be relied on, other than what follows from the above.
Results may differ from the reference program's by a relative error of at most 0.0085.
Values may be sent and summed in bfloat16 or wider, within the bound.
No kernel may reach another device: no remote copies, remote signals or barrier semaphores. Data moves between devices by JAX's collectives and lax.ppermute only.
A program may use at most 64 MiB of HBM per device.

```python
import math
import jax
import jax.numpy as jnp
from jax import lax

C = 64
NB = 8
K = 4
A_DEV = 512
G = 256
PL = 20480
PG = 12288
ATOMS = 16384
SENDS = 8192
LOCAL_SLOTS = 655360
GHOST_SLOTS = 393216
N_GX = 2
N_GY = 4
N_GZ = 4


def place_ends(values, stream_key, low, largest):
    longest = values.shape.index(max(values.shape))
    spots = []
    for shift in (0, 1):
        where = [jax.random.randint(jax.random.fold_in(stream_key, axis), (), 0, length) for axis, length in enumerate(values.shape)]
        where[longest] = (where[longest] + shift) % values.shape[longest]
        spots.append(tuple(where))
    return values.at[spots[0]].set(low).at[spots[1]].set(largest)


def shard_levels(key, dims, cuts, low, high):
    gain, own = 1.0, jax.random.fold_in(key, 6)
    for position, blocks in cuts:
        heights = jnp.exp(jax.random.uniform(jax.random.fold_in(own, position), (blocks,), jnp.float32, low / len(cuts), high / len(cuts)))
        gain = gain * jnp.repeat(heights, dims[position] // blocks).reshape([-1 if axis == position else 1 for axis in range(len(dims))])
    return gain


def scatter_about(rng, extent, scale, reach, shards=(), kind=jnp.bfloat16):
    gain = shard_levels(rng, extent, shards, -0.22, 0.18) if shards else 1.0
    values = jax.random.normal(rng, extent, jnp.float32) * scale * gain
    return jnp.minimum(jnp.maximum(values, -reach), reach).astype(kind)


def setup_inputs(seed: int = 0) -> dict:
    key_of = jax.random.split(jax.random.key(seed), 18)
    positions = jnp.clip(1.0 * jax.random.uniform(key_of[0], (3, ATOMS), jnp.float32) ** shard_levels(key_of[0], (3, ATOMS), ((1, 32),), -0.2, 0.2), 0.0, 1.0)
    features = scatter_about(key_of[1], (C, ATOMS), 1.0, 6.0, ((1, 32),))
    species = place_ends(jax.random.randint(key_of[2], (ATOMS,), 0, K), jax.random.fold_in(key_of[2], 1), 0, K - 1).astype(jnp.int32)
    species_scale = jnp.clip(jnp.exp(jax.random.uniform(key_of[3], (K,), jnp.float32, math.log(0.5), math.log(2.0))), 0.5, 2.0).astype(jnp.bfloat16)
    w_first = scatter_about(key_of[4], (C, C), C ** -0.5, 0.75)
    w_second = scatter_about(key_of[5], (C, C), C ** -0.5, 0.75)
    w_radial = scatter_about(key_of[6], (C, NB), 2 ** -0.5, 4.0, (), jnp.float32)
    w_mid = scatter_about(key_of[7], (C, C), C ** -0.5, 0.75)
    w_last = scatter_about(key_of[8], (C, C), C ** -0.5, 0.75)
    w_out = scatter_about(key_of[9], (C,), C ** -0.5, 0.75, (), jnp.float32)
    ghost_send = place_ends(jax.random.randint(key_of[10], (SENDS,), 0, A_DEV), jax.random.fold_in(key_of[10], 1), 0, A_DEV - 1).astype(jnp.int32)
    local_first = place_ends(jax.random.randint(key_of[11], (LOCAL_SLOTS,), 0, A_DEV), jax.random.fold_in(key_of[11], 1), 0, A_DEV - 1).astype(jnp.int32)
    local_second = place_ends(jax.random.randint(key_of[12], (LOCAL_SLOTS,), 0, A_DEV), jax.random.fold_in(key_of[12], 1), 0, A_DEV - 1).astype(jnp.int32)
    local_mask = place_ends((jax.random.randint(key_of[13], (LOCAL_SLOTS,), 0, 4) < 3).astype(jnp.int32), jax.random.fold_in(key_of[13], 1), 0, 1)
    ghost_owner = place_ends(jax.random.randint(key_of[14], (GHOST_SLOTS,), 0, A_DEV), jax.random.fold_in(key_of[14], 1), 0, A_DEV - 1).astype(jnp.int32)
    ghost_index = place_ends(jax.random.randint(key_of[15], (GHOST_SLOTS,), 0, 7 * G), jax.random.fold_in(key_of[15], 1), 0, (7 * G) - 1).astype(jnp.int32)
    ghost_mask = place_ends((jax.random.randint(key_of[16], (GHOST_SLOTS,), 0, 4) < 3).astype(jnp.int32), jax.random.fold_in(key_of[16], 1), 0, 1)
    return dict(positions=positions, features=features, species=species, species_scale=species_scale, w_first=w_first, w_second=w_second, w_radial=w_radial, w_mid=w_mid, w_last=w_last, w_out=w_out, ghost_send=ghost_send, local_first=local_first, local_second=local_second, local_mask=local_mask, ghost_owner=ghost_owner, ghost_index=ghost_index, ghost_mask=ghost_mask)


basis_width = 24.0
domain_edge = 1.0
ghost_offsets = ((1, 0, 0), (0, 1, 0), (0, 0, 1), (1, 1, 0), (1, 0, 1), (0, 1, 1), (1, 1, 1))

def pair_energy(squared, left_proj, right_proj, weights, w_radial, w_mid, w_last, w_out):
    basis_count = w_radial.shape[1]
    centers = jnp.arange(basis_count, dtype=jnp.float32) / (basis_count - 1)
    radial_basis = jnp.exp(-basis_width * (squared[None, :] - centers[:, None]) ** 2)
    radial = jnp.dot(w_radial, radial_basis, precision=lax.Precision.HIGHEST, preferred_element_type=jnp.float32)
    hidden_one = jax.nn.silu(left_proj.astype(jnp.float32) + right_proj.astype(jnp.float32) + radial).astype(jnp.bfloat16)
    hidden_two = jax.nn.silu(jnp.dot(w_mid, hidden_one, preferred_element_type=jnp.float32)).astype(jnp.bfloat16)
    hidden_three = jax.nn.silu(jnp.dot(w_last, hidden_two, preferred_element_type=jnp.float32))
    readout = jnp.dot(w_out, hidden_three, precision=lax.Precision.HIGHEST, preferred_element_type=jnp.float32)
    envelope = jnp.maximum(1.0 - squared, 0.0) ** 2
    return weights * envelope * readout

def pair_terms(owners, partners, slot_mask, own_coords, own_gain, left_all, right_table, right_coords, right_gain, w_radial, w_mid, w_last, w_out):
    total = owners.shape[0]
    block_size = math.gcd(total, 8192)
    step_count = total // block_size

    def one_block(pieces):
        owner_rows, partner_rows, live = pieces
        displace = jnp.take(right_coords, partner_rows, axis=1) - jnp.take(own_coords, owner_rows, axis=1)
        squared = lax.optimization_barrier(jnp.sum(displace * displace, axis=0))
        weights = live.astype(jnp.float32) * jnp.take(own_gain, owner_rows) * jnp.take(right_gain, partner_rows)
        left_proj = jnp.take(left_all, owner_rows, axis=1)
        right_proj = jnp.take(right_table, partner_rows, axis=1)

        def energy_of(squared_in):
            return pair_energy(squared_in, left_proj, right_proj, weights, w_radial, w_mid, w_last, w_out)
        energy, pullback = jax.vjp(energy_of, squared)
        slope = pullback(jnp.ones_like(energy))[0]
        return (energy, 2.0 * displace * slope[None, :])
    energies, pushes = lax.map(one_block, (owners.reshape(step_count, block_size), partners.reshape(step_count, block_size), slot_mask.reshape(step_count, block_size)))
    return (energies.reshape(total), jnp.moveaxis(pushes, 1, 0).reshape(3, total))

def reference(positions, features, species, species_scale, w_first, w_second, w_radial, w_mid, w_last, w_out, ghost_send, local_first, local_second, local_mask, ghost_owner, ghost_index, ghost_mask):
    device_count = N_GX * N_GY * N_GZ
    channels = features.shape[0]
    atom_gain = species_scale.astype(jnp.float32)[species]
    coord_high = positions.astype(jnp.bfloat16)
    coord_low = (positions - coord_high.astype(jnp.float32)).astype(jnp.bfloat16)
    payload = jnp.concatenate([features, coord_high, coord_low, atom_gain.astype(jnp.bfloat16)[None, :]], 0)
    payload_dev = payload.reshape(channels + 7, device_count, A_DEV)
    send_dev = ghost_send.reshape(device_count, G)
    picked = jax.vmap(lambda table, rows_in: jnp.take(table, rows_in, axis=1), in_axes=(1, 0), out_axes=1)(payload_dev, send_dev)
    picked_grid = picked.reshape(channels + 7, N_GX, N_GY, N_GZ, G)
    blocks = [jnp.roll(picked_grid, (-offset[0], -offset[1], -offset[2]), axis=(1, 2, 3)) for offset in ghost_offsets]
    ghosts = jnp.stack(blocks, 4).reshape(channels + 7, device_count, 7 * G)
    shifts = domain_edge * jnp.array(ghost_offsets, dtype=jnp.float32).T

    def device_terms(pieces):
        own_pos, own_feat, own_gain, ghost_rows, first_l, second_l, mask_l, owner_g, index_g, mask_g = pieces
        ghost_feat = ghost_rows[:channels]
        ghost_high = ghost_rows[channels:channels + 3].astype(jnp.float32)
        ghost_low = ghost_rows[channels + 3:channels + 6].astype(jnp.float32)
        ghost_coords = ((ghost_high + ghost_low).reshape(3, 7, G) + shifts[:, :, None]).reshape(3, 7 * G)
        ghost_gain = ghost_rows[channels + 6].astype(jnp.float32)
        left_all = jnp.dot(w_first, own_feat, preferred_element_type=jnp.float32).astype(jnp.bfloat16)
        right_own = jnp.dot(w_second, own_feat, preferred_element_type=jnp.float32).astype(jnp.bfloat16)
        right_ghost = jnp.dot(w_second, ghost_feat, preferred_element_type=jnp.float32).astype(jnp.bfloat16)
        local_energy, local_push = pair_terms(first_l, second_l, mask_l, own_pos, own_gain, left_all, right_own, own_pos, own_gain, w_radial, w_mid, w_last, w_out)
        ghost_energy, ghost_push = pair_terms(owner_g, index_g, mask_g, own_pos, own_gain, left_all, right_ghost, ghost_coords, ghost_gain, w_radial, w_mid, w_last, w_out)
        energy_out = jnp.zeros((A_DEV,), jnp.float32).at[first_l].add(local_energy).at[owner_g].add(ghost_energy)
        force_out = jnp.zeros((3, A_DEV), jnp.float32).at[:, first_l].add(local_push).at[:, second_l].add(-local_push).at[:, owner_g].add(ghost_push)
        ghost_force = jnp.zeros((3, 7 * G), jnp.float32).at[:, index_g].add(-ghost_push)
        return (force_out, energy_out, ghost_force)
    pieces = (jnp.moveaxis(positions.reshape(3, device_count, A_DEV), 1, 0), jnp.moveaxis(features.reshape(channels, device_count, A_DEV), 1, 0), atom_gain.reshape(device_count, A_DEV), jnp.moveaxis(ghosts, 1, 0), local_first.reshape(device_count, PL), local_second.reshape(device_count, PL), local_mask.reshape(device_count, PL), ghost_owner.reshape(device_count, PG), ghost_index.reshape(device_count, PG), ghost_mask.reshape(device_count, PG))
    force_dev, energy_dev, ghost_dev = lax.map(device_terms, pieces)
    ghost_grid = ghost_dev.reshape(N_GX, N_GY, N_GZ, 3, 7, G)
    incoming = jnp.zeros((N_GX, N_GY, N_GZ, 3, G), jnp.float32)
    for slot in range(7):
        offset = ghost_offsets[slot]
        incoming = incoming + jnp.roll(ghost_grid[:, :, :, :, slot, :], (offset[0], offset[1], offset[2]), axis=(0, 1, 2))
    incoming = incoming.reshape(device_count, 3, G)
    force_dev = jax.vmap(lambda table, rows_in, values: table.at[:, rows_in].add(values))(force_dev, send_dev, incoming)
    forces = jnp.moveaxis(force_dev, 0, 1).reshape(3, device_count * A_DEV)
    atom_energy = energy_dev.reshape(device_count * A_DEV)
    return (forces, atom_energy)
```

```python
import functools
import math

import jax
import jax.numpy as jnp
from jax import lax
from jax.experimental import pallas as pl
from jax.experimental.pallas import tpu as pltpu
from jax.sharding import PartitionSpec as P

basis_width = 24.0
domain_edge = 1.0
ghost_offsets = ((1, 0, 0), (0, 1, 0), (0, 0, 1), (1, 1, 0), (1, 0, 1), (0, 1, 1), (1, 1, 1))

EXTRA = 16
GROUP = 256
LANES = 128
CHUNK = 256
VMEM_LIMIT = 48 * 1024 * 1024

NT = (((1,), (1,)), ((), ()))
f32 = jnp.float32
bf16 = jnp.bfloat16


def dot(left, right):
    return jnp.dot(left, right, preferred_element_type=f32)


def dot_nt(left, right):
    return lax.dot_general(left, right, NT, preferred_element_type=f32)


def iota(shape, dim):
    return lax.broadcasted_iota(jnp.int32, shape, dim)


def one_hot(row, count):
    return jnp.where(iota((count, row.shape[1]), 0) == row, 1.0, 0.0).astype(bf16)


def split_two(value):
    high = value.astype(bf16).astype(f32)
    return high, value - high


def coord_rows(coords, gain):
    high, low = split_two(coords)
    none = jnp.zeros((1, coords.shape[1]), f32)
    return jnp.concatenate([high, none, gain, none, none, none, low, none, none, none, none, none], 0)


def eye(count):
    return (iota((count, count), 0) == iota((count, count), 1)).astype(bf16)


def prep_kernel(
    positions_ref,
    features_ref,
    species_ref,
    scale_ref,
    w_first_ref,
    w_second_ref,
    w_radial_ref,
    w_mid_ref,
    w_last_ref,
    w_out_ref,
    send_ref,
    own_ref,
    right_ref,
    offered_ref,
    mats_ref,
    radial_ref,
    radial_t_ref,
    out_ref,
):
    channels = features_ref.shape[0]
    count = features_ref.shape[1]
    rows = channels + EXTRA
    species = species_ref[...]
    gain = jnp.zeros((1, count), f32)
    for kind in range(scale_ref.shape[1]):
        scale = scale_ref[:, kind : kind + 1].astype(f32)
        gain = jnp.where(species == kind, scale, gain)
    extra = coord_rows(positions_ref[...], gain).astype(bf16)
    left = dot(w_first_ref[...], features_ref[...]).astype(bf16).astype(f32)
    right = dot(w_second_ref[...], features_ref[...]).astype(bf16).astype(f32)
    left = (0.5 * left).astype(bf16)
    right = (0.5 * right).astype(bf16)
    groups = count // GROUP
    for group in range(groups):
        cols = slice(group * GROUP, (group + 1) * GROUP)
        own_ref[group * rows : group * rows + channels, :] = left[:, cols]
        own_ref[group * rows + channels : (group + 1) * rows, :] = extra[:, cols]
        right_ref[group * rows : group * rows + channels, :] = right[:, cols]
        right_ref[group * rows + channels : (group + 1) * rows, :] = extra[:, cols]
    send = send_ref[...]
    picked = dot(right_ref[...], one_hot(send & (GROUP - 1), GROUP))
    chosen = picked[:rows]
    for group in range(1, groups):
        chosen = jnp.where(send // GROUP == group, picked[group * rows : (group + 1) * rows], chosen)
    offered_ref[...] = chosen.astype(bf16)

    unit = eye(channels)
    mid = w_mid_ref[...].astype(f32)
    last = w_last_ref[...].astype(f32)
    mats_ref[0:channels, :] = (0.5 * mid).astype(bf16)
    mats_ref[channels : 2 * channels, :] = (0.5 * last).astype(bf16)
    mats_ref[2 * channels : 3 * channels, :] = (0.5 * dot_nt(unit, w_last_ref[...])).astype(bf16)
    mats_ref[3 * channels : 4 * channels, :] = (0.5 * dot_nt(unit, w_mid_ref[...])).astype(bf16)
    bases = w_radial_ref.shape[1]
    high, low = split_two(w_radial_ref[...])
    spread = (iota((bases, 4 * bases), 0) == iota((bases, 4 * bases), 1) % bases).astype(bf16)
    wide_high = dot(high.astype(bf16), spread)
    wide_low = dot(low.astype(bf16), spread)
    lane = iota((channels, 4 * bases), 1)
    radial_ref[...] = (0.5 * jnp.where(lane < 2 * bases, wide_high, wide_low)).astype(bf16)
    unit = eye(bases)
    radial_t_ref[0:bases, :] = dot_nt(unit, high.astype(bf16))
    radial_t_ref[bases : 2 * bases, :] = dot_nt(unit, low.astype(bf16))
    w_out = w_out_ref[...]
    diagonal = jnp.where(iota((channels, channels), 0) == iota((channels, channels), 1), w_out, 0.0)
    out_ref[...] = jnp.broadcast_to(jnp.sum(diagonal, axis=1, keepdims=True), (channels, LANES))


def group_pick(values, high, rows, groups):
    chosen = values[:rows]
    for group in range(1, groups):
        chosen = jnp.where(high == group, values[group * rows : (group + 1) * rows], chosen)
    return chosen


def spread_groups(values, high, groups):
    pieces = [jnp.where(high == group, values, 0.0) for group in range(groups)]
    if groups % 2:
        pieces.append(jnp.zeros_like(values))
    return jnp.concatenate(pieces, 0).astype(bf16)


def pair_body(
    per_step,
    own_groups,
    partner_groups,
    channels,
    bases,
    owner_ref,
    partner_ref,
    mask_ref,
    own_ref,
    right_ref,
    mats_ref,
    radial_ref,
    radial_t_ref,
    out_ref,
    own_acc,
    partner_acc,
    hot_own,
    hot_partner,
    slope_one,
    slope_two,
):
    rows = channels + EXTRA
    steps = owner_ref.shape[0] * LANES // (per_step * CHUNK)
    line = CHUNK // LANES
    w_mid = mats_ref[0:channels, :]
    w_last = mats_ref[channels : 2 * channels, :]
    w_last_t = mats_ref[2 * channels : 3 * channels, :]
    w_mid_t = mats_ref[3 * channels : 4 * channels, :]
    w_radial = radial_ref[...]
    w_radial_t = radial_t_ref[...].astype(bf16)
    w_out = jnp.concatenate([out_ref[...]] * line, 1)
    centers = iota((bases, CHUNK), 0).astype(f32) * (1.0 / (bases - 1))
    sub = iota((8, CHUNK), 0)

    def chunk(base, number):
        def row_of(ref):
            block = ref[pl.ds(base, per_step * line), :]
            return jnp.concatenate(
                [block[number * line + part : number * line + part + 1, :] for part in range(line)], 1
            )

        owner = row_of(owner_ref)
        partner = row_of(partner_ref)
        live = row_of(mask_ref).astype(f32)
        own_high = owner // GROUP
        partner_high = partner // GROUP
        hot_own[number] = one_hot(owner & (GROUP - 1), GROUP)
        hot_partner[number] = one_hot(partner & (GROUP - 1), GROUP)
        yield
        own_vals = group_pick(dot(own_ref[...], hot_own[number]), own_high, rows, own_groups)
        partner_vals = group_pick(
            dot(right_ref[...], hot_partner[number]), partner_high, rows, partner_groups
        )
        yield
        projected = own_vals[:channels] + partner_vals[:channels]
        own_coords = own_vals[channels : channels + 8] + own_vals[channels + 8 :]
        partner_coords = partner_vals[channels : channels + 8] + partner_vals[channels + 8 :]
        shift = partner_coords - own_coords
        square = shift * shift
        squared = square[0:1] + square[1:2] + square[2:3]
        weight = live * own_coords[4:5] * partner_coords[4:5]
        away = squared - centers
        basis = jnp.exp(-basis_width * (away * away))
        basis_slope = (-2.0 * basis_width) * away * basis
        basis_high, basis_low = split_two(basis)
        stacked = jnp.concatenate([basis_high, basis_low, basis_high, basis_low], 0).astype(bf16)
        radial = dot(w_radial, stacked)
        yield
        half = projected + radial
        grow = jnp.tanh(half)
        plus = 1.0 + grow
        hidden = half * plus
        slope_one[number] = plus + hidden * (1.0 - grow)
        hidden = hidden.astype(bf16)
        yield
        half = dot(w_mid, hidden)
        yield
        grow = jnp.tanh(half)
        plus = 1.0 + grow
        hidden = half * plus
        slope_two[number] = plus + hidden * (1.0 - grow)
        hidden = hidden.astype(bf16)
        yield
        half = dot(w_last, hidden)
        yield
        grow = jnp.tanh(half)
        plus = 1.0 + grow
        hidden = half * plus
        readout = jnp.sum(w_out * hidden, axis=0, keepdims=True)
        back = ((0.5 * w_out) * (plus + hidden * (1.0 - grow))).astype(bf16)
        yield
        back = dot(w_last_t, back)
        yield
        back = (back * slope_two[number]).astype(bf16)
        yield
        back = dot(w_mid_t, back)
        yield
        back = (back * slope_one[number]).astype(bf16)
        yield
        back = dot(w_radial_t, back)
        back = back[:bases] + back[bases:]
        yield
        readout_slope = jnp.sum(back * basis_slope, axis=0, keepdims=True)
        near = jnp.maximum(1.0 - squared, 0.0)
        weight_near = weight * near
        energy = weight_near * near * readout
        slope = weight_near * (near * readout_slope - 2.0 * readout)
        push = (2.0 * slope) * shift
        high, low = split_two(jnp.where(sub == 3, energy, push))
        values = jnp.concatenate([high[:4], low[:4]], 0)
        own_part = spread_groups(values, own_high, own_groups)
        partner_part = spread_groups(values, partner_high, partner_groups)
        yield
        own_acc[...] += dot_nt(own_part, hot_own[number])
        partner_acc[...] += dot_nt(partner_part, hot_partner[number])

    def step(index, unused):
        base = pl.multiple_of(index * (per_step * line), per_step * line)
        running = []
        waiting = [chunk(base, number) for number in range(per_step)]
        while running or waiting:
            if waiting:
                running.append(waiting.pop(0))
            running = [task for task in running if next(task, task) is not task]
        return unused

    lax.fori_loop(0, steps, step, 0)


def local_kernel(per_step, channels, bases, with_start, *refs):
    if with_start:
        (owner, partner, mask, own, right, mats, radial, radial_t, out, own_in, partner_in) = refs[:11]
        own_acc, partner_acc, *scratch = refs[11:]
        own_acc[...] = own_in[...]
        partner_acc[...] = partner_in[...]
    else:
        (owner, partner, mask, own, right, mats, radial, radial_t, out) = refs[:9]
        own_acc, partner_acc, *scratch = refs[9:]
        own_acc[...] = jnp.zeros_like(own_acc)
        partner_acc[...] = jnp.zeros_like(partner_acc)
    groups = own.shape[0] // (channels + EXTRA)
    pair_body(
        per_step,
        groups,
        groups,
        channels,
        bases,
        owner,
        partner,
        mask,
        own,
        right,
        mats,
        radial,
        radial_t,
        out,
        own_acc,
        partner_acc,
        *scratch,
    )


def ghost_kernel(per_step, channels, bases, *refs):
    blocks = len(ghost_offsets)
    (owner, partner, mask, own, mats, radial, radial_t, out, own_in) = refs[:9]
    arrived = refs[9 : 9 + blocks]
    own_acc = refs[9 + blocks]
    forces = refs[10 + blocks : 10 + 2 * blocks]
    table, partner_acc, *scratch = refs[10 + 2 * blocks :]
    rows = channels + EXTRA
    groups = own.shape[0] // rows
    own_acc[...] = own_in[...]
    partner_acc[...] = jnp.zeros_like(partner_acc)
    for block, offset in enumerate(ghost_offsets):
        start = block * rows
        table[start : start + channels, :] = arrived[block][0:channels, :]
        extra = arrived[block][channels:rows, :].astype(f32)
        coords = extra[0:8] + extra[8:16]
        moved = jnp.concatenate(
            [coords[axis : axis + 1] + domain_edge * offset[axis] for axis in range(3)], 0
        )
        table[start + channels : start + rows, :] = coord_rows(moved, coords[4:5]).astype(bf16)
    pair_body(
        per_step,
        groups,
        blocks,
        channels,
        bases,
        owner,
        partner,
        mask,
        own,
        table,
        mats,
        radial,
        radial_t,
        out,
        own_acc,
        partner_acc,
        *scratch,
    )
    for block in range(blocks):
        part = partner_acc[block * 8 : block * 8 + 8, :]
        forces[block][...] = -(part + jnp.concatenate([part[4:], part[:4]], 0))


def final_kernel(blocks, *refs):
    own_ref, partner_ref, send_ref = refs[:3]
    arrived = refs[3 : 3 + blocks]
    forces_ref, energy_ref = refs[3 + blocks :]
    incoming = arrived[0][...]
    for block in range(1, blocks):
        incoming = incoming + arrived[block][...]
    high, low = split_two(incoming)
    send = send_ref[...]
    groups = own_ref.shape[0] // 8
    values = spread_groups(jnp.concatenate([high[:4], low[:4]], 0), send // GROUP, groups)
    back = dot_nt(values, one_hot(send & (GROUP - 1), GROUP))
    for group in range(groups):
        part = slice(group * 8, group * 8 + 8)
        total = own_ref[part, :] - partner_ref[part, :] + back[part]
        total = total[:4] + total[4:]
        cols = slice(group * GROUP, (group + 1) * GROUP)
        forces_ref[:, cols] = total[:3]
        energy = own_ref[group * 8 + 3 : group * 8 + 4, :] + own_ref[group * 8 + 7 : group * 8 + 8, :]
        energy_ref[:, cols] = energy


def whole(shape, dtype):
    return jax.ShapeDtypeStruct(shape, dtype)


def call(kernel, outs, name, scratch=(), specs=None, cost=None):
    more = {} if specs is None else dict(in_specs=specs, grid=(1,))
    if cost is not None:
        more["cost_estimate"] = cost
    return pl.pallas_call(
        kernel,
        out_shape=outs,
        scratch_shapes=list(scratch),
        compiler_params=pltpu.CompilerParams(vmem_limit_bytes=VMEM_LIMIT),
        name=name,
        **more,
    )


def shifted(value, offset, sizes, sign):
    names = ("gx", "gy", "gz")
    used = tuple(name for name, step in zip(names, offset) if step)
    dims = [sizes[name] for name in used]
    pairs = []
    for flat in range(math.prod(dims)):
        place, rest = [], flat
        for size in reversed(dims):
            place.insert(0, rest % size)
            rest //= size
        target = 0
        for at, size in zip(place, dims):
            target = target * size + (at - sign) % size
        pairs.append((flat, target))
    return lax.ppermute(value, used, pairs)


def on_device(
    sizes,
    positions,
    features,
    species,
    species_scale,
    w_first,
    w_second,
    w_radial,
    w_mid,
    w_last,
    w_out,
    ghost_send,
    local_first,
    local_second,
    local_mask,
    ghost_owner,
    ghost_index,
    ghost_mask,
):
    channels, own_count = features.shape
    send_count = ghost_send.shape[0]
    bases = w_radial.shape[1]
    rows = channels + EXTRA
    groups = own_count // GROUP
    blocks = len(ghost_offsets)
    send = ghost_send.reshape(1, send_count)
    own, right, offered, mats, radial, radial_t, out = call(
        prep_kernel,
        (
            whole((groups * rows, GROUP), bf16),
            whole((groups * rows, GROUP), bf16),
            whole((rows, send_count), bf16),
            whole((4 * channels, channels), bf16),
            whole((channels, 4 * bases), bf16),
            whole((2 * bases, channels), f32),
            whole((channels, LANES), f32),
        ),
        "tables",
    )(
        positions,
        features,
        species.reshape(1, own_count),
        species_scale.reshape(1, species_scale.shape[0]),
        w_first,
        w_second,
        w_radial,
        w_mid,
        w_last,
        w_out.reshape(1, channels),
        send,
    )
    arrived = [shifted(offered, offset, sizes, 1) for offset in ghost_offsets]

    def tiles(value):
        return value.reshape(value.shape[0] // LANES, LANES)

    per_step = 8

    def scratch(partner_groups):
        return [
            pltpu.VMEM((per_step, GROUP, CHUNK), bf16),
            pltpu.VMEM((per_step, GROUP, CHUNK), bf16),
            pltpu.VMEM((per_step, channels, CHUNK), f32),
            pltpu.VMEM((per_step, channels, CHUNK), f32),
        ]

    def cost(slots):
        return pl.CostEstimate(
            flops=slots * 400000, bytes_accessed=slots * 12, transcendentals=slots * 200
        )

    local = [tiles(value) for value in (local_first, local_second, local_mask)]
    parts = 2
    part_rows = local[0].shape[0] // parts
    weights = (mats, radial, radial_t, out)
    whole_spec = pl.BlockSpec(memory_space=pltpu.VMEM)

    def local_call(part, start):
        cut = pl.BlockSpec((part_rows, LANES), lambda step: (part, 0))
        operands = [*local, own, right, *weights, *start]
        return call(
            functools.partial(local_kernel, per_step, channels, bases, bool(start)),
            (whole((groups * 8, GROUP), f32), whole((groups * 8, GROUP), f32)),
            "local_pairs",
            scratch(groups),
            [cut] * 3 + [whole_spec] * (len(operands) - 3),
            cost(part_rows * LANES),
        )(*operands)

    own_sum, partner_sum = local_call(0, ())
    own_sum, *ghost_forces = call(
        functools.partial(ghost_kernel, per_step, channels, bases),
        (whole((groups * 8, GROUP), f32),) + (whole((8, send_count), f32),) * blocks,
        "ghost_pairs",
        [pltpu.VMEM((blocks * rows, GROUP), bf16), pltpu.VMEM(((blocks + blocks % 2) * 8, GROUP), f32)]
        + scratch(blocks),
        None,
        cost(ghost_owner.shape[0]),
    )(*[tiles(value) for value in (ghost_owner, ghost_index, ghost_mask)], own, *weights, own_sum, *arrived)
    returned = [
        shifted(force, offset, sizes, -1) for force, offset in zip(ghost_forces, ghost_offsets)
    ]
    own_sum, partner_sum = local_call(1, (own_sum, partner_sum))
    forces, energy = call(
        functools.partial(final_kernel, blocks),
        (whole((3, own_count), f32), whole((1, own_count), f32)),
        "totals",
    )(own_sum, partner_sum, send, *returned)
    return forces, energy.reshape(own_count)


def solution(mesh):
    names = ("gx", "gy", "gz")
    sizes = {name: mesh.shape[name] for name in names}
    split = P(names)
    cols = P(None, names)
    in_specs = (
        (cols, cols, split) + (P(),) * 7 + (split,) * 7
    )
    return jax.shard_map(
        functools.partial(on_device, sizes),
        mesh=mesh,
        in_specs=in_specs,
        out_specs=(cols, split),
        check_vma=False,
    )
```

```python
import functools
import math

import jax
import jax.numpy as jnp
from jax import lax
from jax.experimental import pallas as pl
from jax.experimental.pallas import tpu as pltpu
from jax.sharding import PartitionSpec as P

basis_width = 24.0
domain_edge = 1.0
ghost_offsets = ((1, 0, 0), (0, 1, 0), (0, 0, 1), (1, 1, 0), (1, 0, 1), (0, 1, 1), (1, 1, 1))

EXTRA = 16
GROUP = 256
LANES = 128
CHUNK = 256
QUAD = 4
VMEM_LIMIT = 48 * 1024 * 1024

NT = (((1,), (1,)), ((), ()))
f32 = jnp.float32
bf16 = jnp.bfloat16


def dot(left, right):
    return jnp.dot(left, right, preferred_element_type=f32)


def dot_nt(left, right):
    return lax.dot_general(left, right, NT, preferred_element_type=f32)


def iota(shape, dim):
    return lax.broadcasted_iota(jnp.int32, shape, dim)


def one_hot(row, count):
    return jnp.where(iota((count, row.shape[1]), 0) == row, 1.0, 0.0).astype(bf16)


def split_two(value):
    high = value.astype(bf16).astype(f32)
    return high, value - high


def coord_rows(coords, gain):
    high, low = split_two(coords)
    none = jnp.zeros((1, coords.shape[1]), f32)
    return jnp.concatenate([high, none, gain, none, none, none, low, none, none, none, none, none], 0)


def eye(count):
    return (iota((count, count), 0) == iota((count, count), 1)).astype(bf16)


def prep_kernel(
    positions_ref,
    features_ref,
    species_ref,
    scale_ref,
    w_first_ref,
    w_second_ref,
    radial_w_ref,
    w_mid_ref,
    w_last_ref,
    w_out_ref,
    send_ref,
    own_ref,
    right_ref,
    offered_ref,
    mats_ref,
    radial_ref,
    radial_t_ref,
    out_ref,
):
    channels = features_ref.shape[0]
    count = features_ref.shape[1]
    rows = channels + EXTRA
    species = species_ref[...]
    gain = jnp.zeros((1, count), f32)
    for kind in range(scale_ref.shape[1]):
        scale = scale_ref[:, kind : kind + 1].astype(f32)
        gain = jnp.where(species == kind, scale, gain)
    extra = coord_rows(positions_ref[...], gain).astype(bf16)
    left = dot(w_first_ref[...], features_ref[...]).astype(bf16).astype(f32)
    right = dot(w_second_ref[...], features_ref[...]).astype(bf16).astype(f32)
    left = (0.5 * left).astype(bf16)
    right = (0.5 * right).astype(bf16)
    groups = count // GROUP
    for group in range(groups):
        cols = slice(group * GROUP, (group + 1) * GROUP)
        own_ref[group * rows : group * rows + channels, :] = left[:, cols]
        own_ref[group * rows + channels : (group + 1) * rows, :] = extra[:, cols]
        right_ref[group * rows : group * rows + channels, :] = right[:, cols]
        right_ref[group * rows + channels : (group + 1) * rows, :] = extra[:, cols]
    send = send_ref[...]
    picked = dot(right_ref[...], one_hot(send & (GROUP - 1), GROUP))
    chosen = picked[:rows]
    for group in range(1, groups):
        chosen = jnp.where(send // GROUP == group, picked[group * rows : (group + 1) * rows], chosen)
    offered_ref[...] = chosen.astype(bf16)

    unit = eye(channels)
    w_mid = w_mid_ref[...]
    w_last = w_last_ref[...]
    last_t = dot_nt(unit, w_last).astype(bf16)
    mid_t = dot_nt(unit, w_mid).astype(bf16)
    wide = QUAD * channels
    for place, matrix in enumerate((w_mid, w_last, last_t, mid_t)):
        mats_ref[place * wide : (place + 1) * wide, :] = (0.5 * diagonal_copies(matrix)).astype(bf16)
    bases = radial_w_ref.shape[0]
    high, low = split_two(radial_w_ref[...])
    high = high.astype(bf16)
    low = low.astype(bf16)
    spread = dot_nt(unit, jnp.concatenate([high, high, low, low], 0)).astype(bf16)
    radial_ref[...] = (0.5 * diagonal_copies(spread)).astype(bf16)
    radial_t_ref[...] = diagonal_copies(jnp.concatenate([high, low], 0)).astype(bf16)
    w_out = w_out_ref[...]
    diagonal = jnp.where(iota((channels, channels), 0) == iota((channels, channels), 1), w_out, 0.0)
    out_ref[...] = jnp.broadcast_to(jnp.sum(diagonal, axis=1, keepdims=True), (channels, LANES))


def diagonal_copies(matrix):
    high, wide = matrix.shape
    repeat = (iota((wide, QUAD * wide), 0) == iota((wide, QUAD * wide), 1) % wide).astype(bf16)
    row = dot(matrix, repeat)
    full = jnp.concatenate([row] * QUAD, 0)
    return jnp.where(iota(full.shape, 0) // high == iota(full.shape, 1) // wide, full, 0.0)


def group_pick(values, high, rows, groups):
    chosen = values[:rows]
    for group in range(1, groups):
        chosen = jnp.where(high == group, values[group * rows : (group + 1) * rows], chosen)
    return chosen


def spread_groups(values, high, groups):
    pieces = [jnp.where(high == group, values, 0.0) for group in range(groups)]
    if groups % 2:
        pieces.append(jnp.zeros_like(values))
    return jnp.concatenate(pieces, 0).astype(bf16)


def pair_body(
    per_step,
    own_groups,
    partner_groups,
    channels,
    bases,
    owner_ref,
    partner_ref,
    mask_ref,
    own_ref,
    right_ref,
    mats_ref,
    radial_ref,
    radial_t_ref,
    out_ref,
    own_acc,
    partner_acc,
    hot_own,
    hot_partner,
    slope_one,
    slope_two,
):
    rows = channels + EXTRA
    line = CHUNK // LANES
    block = QUAD * line
    wide = QUAD * channels
    steps = owner_ref.shape[0] // (per_step * block)
    w_out = jnp.concatenate([out_ref[...]] * line, 1)
    centers = iota((bases, CHUNK), 0).astype(f32) * (1.0 / (bases - 1))
    sub = iota((8, CHUNK), 0)
    quads = range(QUAD)

    def matrix(place):
        return mats_ref[place * wide : (place + 1) * wide, :]

    def part(values, number, size=channels):
        return values[number * size : (number + 1) * size]

    def silu_pair(half):
        grow = jnp.tanh(half)
        plus = 1.0 + grow
        hidden = half * plus
        return hidden, plus + hidden * (1.0 - grow)

    def chunk(base, number):
        at = pl.multiple_of(base + number * block, block)
        owner_rows = owner_ref[pl.ds(at, block), :]
        partner_rows = partner_ref[pl.ds(at, block), :]
        live_rows = mask_ref[pl.ds(at, block), :].astype(f32)

        def row_of(values, quad):
            return jnp.concatenate(
                [values[quad * line + piece : quad * line + piece + 1, :] for piece in range(line)], 1
            )

        own_high, partner_high, projected, shifts, squares, weights, stacks, slopes = ([] for _ in range(8))
        for quad in quads:
            cols = slice(quad * CHUNK, (quad + 1) * CHUNK)
            owner = row_of(owner_rows, quad)
            partner = row_of(partner_rows, quad)
            own_high.append(owner // GROUP)
            partner_high.append(partner // GROUP)
            hot_own[number, :, cols] = one_hot(owner & (GROUP - 1), GROUP)
            hot_partner[number, :, cols] = one_hot(partner & (GROUP - 1), GROUP)
            yield
        for quad in quads:
            cols = slice(quad * CHUNK, (quad + 1) * CHUNK)
            own_vals = group_pick(
                dot(own_ref[...], hot_own[number, :, cols]), own_high[quad], rows, own_groups
            )
            partner_vals = group_pick(
                dot(right_ref[...], hot_partner[number, :, cols]), partner_high[quad], rows, partner_groups
            )
            projected.append(own_vals[:channels] + partner_vals[:channels])
            own_coords = own_vals[channels : channels + 8] + own_vals[channels + 8 :]
            partner_coords = partner_vals[channels : channels + 8] + partner_vals[channels + 8 :]
            shift = partner_coords - own_coords
            square = shift * shift
            squared = square[0:1] + square[1:2] + square[2:3]
            weights.append(row_of(live_rows, quad) * own_coords[4:5] * partner_coords[4:5])
            away = squared - centers
            basis = jnp.exp(-basis_width * (away * away))
            basis_high, basis_low = split_two(basis)
            stacks.append(jnp.concatenate([basis_high, basis_low, basis_high, basis_low], 0).astype(bf16))
            slopes.append((-2.0 * basis_width) * away * basis)
            shifts.append(shift)
            squares.append(squared)
            yield
        radial = dot(radial_ref[...], jnp.concatenate(stacks, 0))
        yield
        pieces = []
        for quad in quads:
            hidden, slope_one[number, quad] = silu_pair(projected[quad] + part(radial, quad))
            pieces.append(hidden.astype(bf16))
        yield
        half = dot(matrix(0), jnp.concatenate(pieces, 0))
        yield
        pieces = []
        for quad in quads:
            hidden, slope_two[number, quad] = silu_pair(part(half, quad))
            pieces.append(hidden.astype(bf16))
        yield
        half = dot(matrix(1), jnp.concatenate(pieces, 0))
        yield
        pieces = []
        readouts = []
        for quad in quads:
            hidden, slope = silu_pair(part(half, quad))
            readouts.append(jnp.sum(w_out * hidden, axis=0, keepdims=True))
            pieces.append(((0.5 * w_out) * slope).astype(bf16))
        yield
        back = dot(matrix(2), jnp.concatenate(pieces, 0))
        yield
        pieces = [(part(back, quad) * slope_two[number, quad]).astype(bf16) for quad in quads]
        back = dot(matrix(3), jnp.concatenate(pieces, 0))
        yield
        pieces = [(part(back, quad) * slope_one[number, quad]).astype(bf16) for quad in quads]
        back = dot(radial_t_ref[...], jnp.concatenate(pieces, 0))
        yield
        own_parts = []
        partner_parts = []
        for quad in quads:
            two = part(back, quad, 2 * bases)
            readout_slope = jnp.sum((two[:bases] + two[bases:]) * slopes[quad], axis=0, keepdims=True)
            near = jnp.maximum(1.0 - squares[quad], 0.0)
            weight_near = weights[quad] * near
            energy = weight_near * near * readouts[quad]
            slope = weight_near * (near * readout_slope - 2.0 * readouts[quad])
            push = (2.0 * slope) * shifts[quad]
            high, low = split_two(jnp.where(sub == 3, energy, push))
            values = jnp.concatenate([high[:4], low[:4]], 0)
            own_parts.append(spread_groups(values, own_high[quad], own_groups))
            partner_parts.append(spread_groups(values, partner_high[quad], partner_groups))
        yield
        own_acc[...] += dot_nt(jnp.concatenate(own_parts, 1), hot_own[number])
        partner_acc[...] += dot_nt(jnp.concatenate(partner_parts, 1), hot_partner[number])

    def step(index, unused):
        base = pl.multiple_of(index * (per_step * block), per_step * block)
        running = []
        waiting = [chunk(base, number) for number in range(per_step)]
        while running or waiting:
            if waiting:
                running.append(waiting.pop(0))
            for _ in range(2):
                running = [task for task in running if next(task, task) is not task]
        return unused

    lax.fori_loop(0, steps, step, 0)


def local_kernel(per_step, channels, bases, with_start, *refs):
    if with_start:
        (owner, partner, mask, own, right, mats, radial, radial_t, out, own_in, partner_in) = refs[:11]
        own_acc, partner_acc, *scratch = refs[11:]
        own_acc[...] = own_in[...]
        partner_acc[...] = partner_in[...]
    else:
        (owner, partner, mask, own, right, mats, radial, radial_t, out) = refs[:9]
        own_acc, partner_acc, *scratch = refs[9:]
        own_acc[...] = jnp.zeros_like(own_acc)
        partner_acc[...] = jnp.zeros_like(partner_acc)
    groups = own.shape[0] // (channels + EXTRA)
    pair_body(
        per_step,
        groups,
        groups,
        channels,
        bases,
        owner,
        partner,
        mask,
        own,
        right,
        mats,
        radial,
        radial_t,
        out,
        own_acc,
        partner_acc,
        *scratch,
    )


def neighbour(sizes, offset, sign):
    flat = 0
    for (name, size), step in zip(sizes, offset):
        place = lax.axis_index(name)
        if step:
            place = lax.rem(place + (sign % size), size)
        flat = flat * size + place
    return flat


def fetch(sizes, sign, gathered, landed, arrived):
    copies = [
        pltpu.make_async_copy(
            gathered.at[neighbour(sizes, offset, sign)], landed.at[block], arrived.at[block]
        )
        for block, offset in enumerate(ghost_offsets)
    ]
    for copy in copies:
        copy.start()
    for copy in copies:
        copy.wait()


def ghost_kernel(per_step, channels, bases, sizes, *refs):
    blocks = len(ghost_offsets)
    (owner, partner, mask, own, mats, radial, radial_t, out, own_in, gathered) = refs[:10]
    own_acc, forces, landed, arrived, table, partner_acc, *scratch = refs[10:]
    rows = channels + EXTRA
    groups = own.shape[0] // rows
    fetch(sizes, 1, gathered, landed, arrived)
    own_acc[...] = own_in[...]
    partner_acc[...] = jnp.zeros_like(partner_acc)
    for block, offset in enumerate(ghost_offsets):
        start = block * rows
        table[start : start + channels, :] = landed[block, 0:channels, :]
        extra = landed[block, channels:rows, :].astype(f32)
        coords = extra[0:8] + extra[8:16]
        moved = jnp.concatenate(
            [coords[axis : axis + 1] + domain_edge * offset[axis] for axis in range(3)], 0
        )
        table[start + channels : start + rows, :] = coord_rows(moved, coords[4:5]).astype(bf16)
    pair_body(
        per_step,
        groups,
        blocks,
        channels,
        bases,
        owner,
        partner,
        mask,
        own,
        table,
        mats,
        radial,
        radial_t,
        out,
        own_acc,
        partner_acc,
        *scratch,
    )
    forces[...] = jnp.zeros_like(forces)
    for block in range(blocks):
        both = partner_acc[block * 8 : block * 8 + 8, :]
        forces[3 * block : 3 * block + 3, :] = -(both[:3] + both[4:7])


def final_kernel(sizes, *refs):
    own_ref, partner_ref, send_ref, gathered, forces_ref, energy_ref, landed, arrived = refs
    fetch(sizes, -1, gathered, landed, arrived)
    incoming = landed[0, 0:3, :]
    for block in range(1, len(ghost_offsets)):
        incoming = incoming + landed[block, 3 * block : 3 * block + 3, :]
    high, low = split_two(jnp.concatenate([incoming, jnp.zeros_like(incoming[:1])], 0))
    send = send_ref[...]
    groups = own_ref.shape[0] // 8
    values = spread_groups(jnp.concatenate([high, low], 0), send // GROUP, groups)
    back = dot_nt(values, one_hot(send & (GROUP - 1), GROUP))
    for group in range(groups):
        part = slice(group * 8, group * 8 + 8)
        total = own_ref[part, :] - partner_ref[part, :] + back[part]
        total = total[:4] + total[4:]
        cols = slice(group * GROUP, (group + 1) * GROUP)
        forces_ref[:, cols] = total[:3]
        energy = own_ref[group * 8 + 3 : group * 8 + 4, :] + own_ref[group * 8 + 7 : group * 8 + 8, :]
        energy_ref[:, cols] = energy


def whole(shape, dtype):
    return jax.ShapeDtypeStruct(shape, dtype)


def call(kernel, outs, name, scratch=(), specs=None, cost=None):
    more = {} if cost is None else dict(cost_estimate=cost)
    return pl.pallas_call(
        kernel,
        grid=(1,),
        in_specs=specs,
        out_specs=tuple(pl.BlockSpec(memory_space=pltpu.VMEM) for _ in outs),
        out_shape=outs,
        scratch_shapes=list(scratch),
        compiler_params=pltpu.CompilerParams(vmem_limit_bytes=VMEM_LIMIT),
        name=name,
        **more,
    )


def on_device(
    sizes,
    positions,
    features,
    species,
    species_scale,
    w_first,
    w_second,
    w_radial,
    w_mid,
    w_last,
    w_out,
    ghost_send,
    local_first,
    local_second,
    local_mask,
    ghost_owner,
    ghost_index,
    ghost_mask,
):
    channels, own_count = features.shape
    send_count = ghost_send.shape[0]
    bases = w_radial.shape[1]
    rows = channels + EXTRA
    groups = own_count // GROUP
    blocks = len(ghost_offsets)
    names = tuple(name for name, size in sizes)
    send = ghost_send.reshape(1, send_count)
    whole_spec = pl.BlockSpec(memory_space=pltpu.VMEM)
    remain = pl.BlockSpec(memory_space=pl.ANY)
    own, right, offered, mats, radial, radial_t, out = call(
        prep_kernel,
        (
            whole((groups * rows, GROUP), bf16),
            whole((groups * rows, GROUP), bf16),
            whole((rows, send_count), bf16),
            whole((4 * QUAD * channels, QUAD * channels), bf16),
            whole((QUAD * channels, QUAD * 4 * bases), bf16),
            whole((QUAD * 2 * bases, QUAD * channels), bf16),
            whole((channels, LANES), f32),
        ),
        "tables",
        specs=[whole_spec] * 11,
    )(
        positions,
        features,
        species.reshape(1, own_count),
        species_scale.reshape(1, species_scale.shape[0]),
        w_first,
        w_second,
        w_radial.T,
        w_mid,
        w_last,
        w_out.reshape(1, channels),
        send,
    )
    gathered = lax.all_gather(offered, names)

    def tiles(value):
        return value.reshape(value.shape[0] // LANES, LANES)

    def scratch(per_step):
        return [
            pltpu.VMEM((per_step, GROUP, QUAD * CHUNK), bf16),
            pltpu.VMEM((per_step, GROUP, QUAD * CHUNK), bf16),
            pltpu.VMEM((per_step, QUAD, channels, CHUNK), f32),
            pltpu.VMEM((per_step, QUAD, channels, CHUNK), f32),
        ]

    def cost(slots):
        return pl.CostEstimate(flops=slots * 400000, bytes_accessed=slots * 12, transcendentals=slots * 200)

    local = [tiles(value) for value in (local_first, local_second, local_mask)]
    parts = 2
    part_rows = local[0].shape[0] // parts
    weights = (mats, radial, radial_t, out)
    local_step = math.gcd(part_rows * LANES // (QUAD * CHUNK), 5)

    def local_call(part, start):
        cut = pl.BlockSpec((part_rows, LANES), lambda step: (part, 0))
        operands = [*local, own, right, *weights, *start]
        return call(
            functools.partial(local_kernel, local_step, channels, bases, bool(start)),
            (whole((groups * 8, GROUP), f32), whole((groups * 8, GROUP), f32)),
            "local_pairs",
            scratch(local_step),
            [cut] * 3 + [whole_spec] * (len(operands) - 3),
            cost(part_rows * LANES),
        )(*operands)

    own_sum, partner_sum = local_call(0, ())
    ghost_lists = [tiles(value) for value in (ghost_owner, ghost_index, ghost_mask)]
    ghost_step = math.gcd(ghost_owner.shape[0] // (QUAD * CHUNK), 4)
    fetched = [pltpu.SemaphoreType.DMA((blocks,))]
    own_sum, ghost_forces = call(
        functools.partial(ghost_kernel, ghost_step, channels, bases, sizes),
        (whole((groups * 8, GROUP), f32), whole((3 * (blocks + 1), send_count), f32)),
        "ghost_pairs",
        [pltpu.VMEM((blocks, rows, send_count), bf16)]
        + fetched
        + [
            pltpu.VMEM((blocks * rows, GROUP), bf16),
            pltpu.VMEM(((blocks + blocks % 2) * 8, GROUP), f32),
        ]
        + scratch(ghost_step),
        [whole_spec] * 9 + [remain],
        cost(ghost_owner.shape[0]),
    )(*ghost_lists, own, *weights, own_sum, gathered)
    returned = lax.all_gather(ghost_forces, names)
    own_sum, partner_sum = local_call(1, (own_sum, partner_sum))
    forces, energy = call(
        functools.partial(final_kernel, sizes),
        (whole((3, own_count), f32), whole((1, own_count), f32)),
        "totals",
        [pltpu.VMEM((blocks, 3 * (blocks + 1), send_count), f32)] + fetched,
        [whole_spec] * 3 + [remain],
    )(own_sum, partner_sum, send, returned)
    return forces, energy.reshape(own_count)


def solution(mesh):
    names = ("gx", "gy", "gz")
    sizes = tuple((name, mesh.shape[name]) for name in names)
    split = P(names)
    cols = P(None, names)
    in_specs = (cols, cols, split) + (P(),) * 7 + (split,) * 7
    return jax.shard_map(
        functools.partial(on_device, sizes),
        mesh=mesh,
        in_specs=in_specs,
        out_specs=(cols, split),
        check_vma=False,
    )
```

```python
import functools
import math

import jax
import jax.numpy as jnp
from jax import lax
from jax.experimental import pallas as pl
from jax.experimental.pallas import tpu as pltpu
from jax.sharding import PartitionSpec as P

basis_width = 24.0
domain_edge = 1.0
ghost_offsets = ((1, 0, 0), (0, 1, 0), (0, 0, 1), (1, 1, 0), (1, 0, 1), (0, 1, 1), (1, 1, 1))

EXTRA = 16
GROUP = 256
LANES = 128
CHUNK = 256
QUAD = 4
VMEM_LIMIT = 48 * 1024 * 1024

NT = (((1,), (1,)), ((), ()))
f32 = jnp.float32
bf16 = jnp.bfloat16


def dot(left, right):
    return jnp.dot(left, right, preferred_element_type=f32)


def dot_nt(left, right):
    return lax.dot_general(left, right, NT, preferred_element_type=f32)


def iota(shape, dim):
    return lax.broadcasted_iota(jnp.int32, shape, dim)


def one_hot(row, count):
    return jnp.where(iota((count, row.shape[1]), 0) == row, 1.0, 0.0).astype(bf16)


def split_two(value):
    high = value.astype(bf16).astype(f32)
    return high, value - high


def coord_rows(coords, gain):
    high, low = split_two(coords)
    none = jnp.zeros((1, coords.shape[1]), f32)
    return jnp.concatenate([high, none, gain, none, none, none, low, none, none, none, none, none], 0)


def eye(count):
    return (iota((count, count), 0) == iota((count, count), 1)).astype(bf16)


def prep_kernel(*refs):
    sources = refs[:14]
    own_ref, right_ref, offered_ref, mats_ref, radial_ref, radial_t_ref, out_ref = refs[14:21]
    targets = refs[25:35] + refs[21:25]
    landed = refs[35]
    copies = [
        pltpu.make_async_copy(source, target, landed.at[place])
        for place, (source, target) in enumerate(zip(sources, targets))
    ]
    for copy in copies:
        copy.start()
    for copy in copies:
        copy.wait()
    (
        positions_ref,
        features_ref,
        species_ref,
        scale_ref,
        w_first_ref,
        w_second_ref,
        radial_w_ref,
        w_mid_ref,
        w_last_ref,
        w_out_ref,
        send_ref,
    ) = targets[:11]
    channels = features_ref.shape[0]
    count = features_ref.shape[1]
    rows = channels + EXTRA
    species = species_ref[...]
    gain = jnp.zeros((1, count), f32)
    for kind in range(scale_ref.shape[1]):
        scale = scale_ref[:, kind : kind + 1].astype(f32)
        gain = jnp.where(species == kind, scale, gain)
    extra = coord_rows(positions_ref[...], gain).astype(bf16)
    left = dot(w_first_ref[...], features_ref[...]).astype(bf16).astype(f32)
    right = dot(w_second_ref[...], features_ref[...]).astype(bf16).astype(f32)
    left = (0.5 * left).astype(bf16)
    right = (0.5 * right).astype(bf16)
    groups = count // GROUP
    for group in range(groups):
        cols = slice(group * GROUP, (group + 1) * GROUP)
        own_ref[group * rows : group * rows + channels, :] = left[:, cols]
        own_ref[group * rows + channels : (group + 1) * rows, :] = extra[:, cols]
        right_ref[group * rows : group * rows + channels, :] = right[:, cols]
        right_ref[group * rows + channels : (group + 1) * rows, :] = extra[:, cols]
    send = send_ref[...]
    picked = dot(right_ref[...], one_hot(send & (GROUP - 1), GROUP))
    chosen = picked[:rows]
    for group in range(1, groups):
        chosen = jnp.where(send // GROUP == group, picked[group * rows : (group + 1) * rows], chosen)
    offered_ref[...] = chosen.astype(bf16)

    unit = eye(channels)
    w_mid = w_mid_ref[...]
    w_last = w_last_ref[...]
    last_t = dot_nt(unit, w_last).astype(bf16)
    mid_t = dot_nt(unit, w_mid).astype(bf16)
    wide = QUAD * channels
    for place, matrix in enumerate((w_mid, w_last, last_t, mid_t)):
        mats_ref[place * wide : (place + 1) * wide, :] = (0.5 * diagonal_copies(matrix)).astype(bf16)
    bases = radial_w_ref.shape[0]
    high, low = split_two(radial_w_ref[...])
    high = high.astype(bf16)
    low = low.astype(bf16)
    spread = dot_nt(unit, jnp.concatenate([high, high, low, low], 0)).astype(bf16)
    radial_ref[...] = (0.5 * diagonal_copies(spread)).astype(bf16)
    radial_t_ref[...] = diagonal_copies(jnp.concatenate([high, low], 0)).astype(bf16)
    w_out = w_out_ref[...]
    diagonal = jnp.where(iota((channels, channels), 0) == iota((channels, channels), 1), w_out, 0.0)
    out_ref[...] = jnp.broadcast_to(jnp.sum(diagonal, axis=1, keepdims=True), (channels, LANES))


def diagonal_copies(matrix):
    high, wide = matrix.shape
    repeat = (iota((wide, QUAD * wide), 0) == iota((wide, QUAD * wide), 1) % wide).astype(bf16)
    row = dot(matrix, repeat)
    full = jnp.concatenate([row] * QUAD, 0)
    return jnp.where(iota(full.shape, 0) // high == iota(full.shape, 1) // wide, full, 0.0)


def group_pick(values, high, rows, groups):
    chosen = values[:rows]
    for group in range(1, groups):
        chosen = jnp.where(high == group, values[group * rows : (group + 1) * rows], chosen)
    return chosen


def spread_groups(values, high, groups):
    pieces = [jnp.where(high == group, values, 0.0) for group in range(groups)]
    if groups % 2:
        pieces.append(jnp.zeros_like(values))
    return jnp.concatenate(pieces, 0).astype(bf16)


def pair_body(
    per_step,
    first_row,
    row_count,
    own_groups,
    partner_groups,
    channels,
    bases,
    owner_ref,
    partner_ref,
    mask_ref,
    own_ref,
    right_ref,
    mats_ref,
    radial_ref,
    radial_t_ref,
    out_ref,
    own_acc,
    partner_acc,
    hot_own,
    hot_partner,
    slope_one,
    slope_two,
):
    rows = channels + EXTRA
    line = CHUNK // LANES
    block = QUAD * line
    wide = QUAD * channels
    steps = row_count // (per_step * block)
    w_out = jnp.concatenate([out_ref[...]] * line, 1)
    centers = iota((bases, CHUNK), 0).astype(f32) * (1.0 / (bases - 1))
    sub = iota((8, CHUNK), 0)
    quads = range(QUAD)

    def matrix(place):
        return mats_ref[place * wide : (place + 1) * wide, :]

    def part(values, number, size=channels):
        return values[number * size : (number + 1) * size]

    def silu_pair(half):
        grow = jnp.tanh(half)
        plus = 1.0 + grow
        hidden = half * plus
        return hidden, plus + hidden * (1.0 - grow)

    def chunk(base, number):
        at = pl.multiple_of(base + number * block, block)
        owner_rows = owner_ref[pl.ds(at, block), :]
        partner_rows = partner_ref[pl.ds(at, block), :]
        live_rows = mask_ref[pl.ds(at, block), :].astype(f32)

        def row_of(values, quad):
            return jnp.concatenate(
                [values[quad * line + piece : quad * line + piece + 1, :] for piece in range(line)], 1
            )

        own_high, partner_high, projected, shifts, squares, weights, stacks, slopes = ([] for _ in range(8))
        for quad in quads:
            cols = slice(quad * CHUNK, (quad + 1) * CHUNK)
            owner = row_of(owner_rows, quad)
            partner = row_of(partner_rows, quad)
            own_high.append(owner // GROUP)
            partner_high.append(partner // GROUP)
            hot_own[number, :, cols] = one_hot(owner & (GROUP - 1), GROUP)
            hot_partner[number, :, cols] = one_hot(partner & (GROUP - 1), GROUP)
            yield
        for quad in quads:
            cols = slice(quad * CHUNK, (quad + 1) * CHUNK)
            own_vals = group_pick(
                dot(own_ref[...], hot_own[number, :, cols]), own_high[quad], rows, own_groups
            )
            partner_vals = group_pick(
                dot(right_ref[...], hot_partner[number, :, cols]), partner_high[quad], rows, partner_groups
            )
            projected.append(own_vals[:channels] + partner_vals[:channels])
            own_coords = own_vals[channels : channels + 8] + own_vals[channels + 8 :]
            partner_coords = partner_vals[channels : channels + 8] + partner_vals[channels + 8 :]
            shift = partner_coords - own_coords
            square = shift * shift
            squared = square[0:1] + square[1:2] + square[2:3]
            weights.append(row_of(live_rows, quad) * own_coords[4:5] * partner_coords[4:5])
            away = squared - centers
            basis = jnp.exp(-basis_width * (away * away))
            basis_high, basis_low = split_two(basis)
            stacks.append(jnp.concatenate([basis_high, basis_low, basis_high, basis_low], 0).astype(bf16))
            slopes.append((-2.0 * basis_width) * away * basis)
            shifts.append(shift)
            squares.append(squared)
            yield
        radial = dot(radial_ref[...], jnp.concatenate(stacks, 0))
        yield
        pieces = []
        for quad in quads:
            hidden, slope_one[number, quad] = silu_pair(projected[quad] + part(radial, quad))
            pieces.append(hidden.astype(bf16))
        yield
        half = dot(matrix(0), jnp.concatenate(pieces, 0))
        yield
        pieces = []
        for quad in quads:
            hidden, slope_two[number, quad] = silu_pair(part(half, quad))
            pieces.append(hidden.astype(bf16))
        yield
        half = dot(matrix(1), jnp.concatenate(pieces, 0))
        yield
        pieces = []
        readouts = []
        for quad in quads:
            hidden, slope = silu_pair(part(half, quad))
            readouts.append(jnp.sum(w_out * hidden, axis=0, keepdims=True))
            pieces.append(((0.5 * w_out) * slope).astype(bf16))
        yield
        back = dot(matrix(2), jnp.concatenate(pieces, 0))
        yield
        pieces = [(part(back, quad) * slope_two[number, quad]).astype(bf16) for quad in quads]
        back = dot(matrix(3), jnp.concatenate(pieces, 0))
        yield
        pieces = [(part(back, quad) * slope_one[number, quad]).astype(bf16) for quad in quads]
        back = dot(radial_t_ref[...], jnp.concatenate(pieces, 0))
        yield
        own_parts = []
        partner_parts = []
        for quad in quads:
            two = part(back, quad, 2 * bases)
            readout_slope = jnp.sum((two[:bases] + two[bases:]) * slopes[quad], axis=0, keepdims=True)
            near = jnp.maximum(1.0 - squares[quad], 0.0)
            weight_near = weights[quad] * near
            energy = weight_near * near * readouts[quad]
            slope = weight_near * (near * readout_slope - 2.0 * readouts[quad])
            push = (2.0 * slope) * shifts[quad]
            high, low = split_two(jnp.where(sub == 3, energy, push))
            values = jnp.concatenate([high[:4], low[:4]], 0)
            own_parts.append(spread_groups(values, own_high[quad], own_groups))
            partner_parts.append(spread_groups(values, partner_high[quad], partner_groups))
        yield
        own_acc[...] += dot_nt(jnp.concatenate(own_parts, 1), hot_own[number])
        partner_acc[...] += dot_nt(jnp.concatenate(partner_parts, 1), hot_partner[number])

    def step(index, unused):
        base = pl.multiple_of(first_row + index * (per_step * block), block)
        running = []
        waiting = [chunk(base, number) for number in range(per_step)]
        while running or waiting:
            if waiting:
                running.append(waiting.pop(0))
            for _ in range(2):
                running = [task for task in running if next(task, task) is not task]
        return unused

    lax.fori_loop(0, steps, step, 0)


def local_kernel(per_step, channels, bases, first_row, row_count, with_start, *refs):
    if with_start:
        (owner, partner, mask, own, right, mats, radial, radial_t, out, own_in, partner_in) = refs[:11]
        own_acc, partner_acc, *scratch = refs[11:]
        own_acc[...] = own_in[...]
        partner_acc[...] = partner_in[...]
    else:
        (owner, partner, mask, own, right, mats, radial, radial_t, out) = refs[:9]
        own_acc, partner_acc, *scratch = refs[9:]
        own_acc[...] = jnp.zeros_like(own_acc)
        partner_acc[...] = jnp.zeros_like(partner_acc)
    groups = own.shape[0] // (channels + EXTRA)
    pair_body(
        per_step,
        first_row,
        row_count,
        groups,
        groups,
        channels,
        bases,
        owner,
        partner,
        mask,
        own,
        right,
        mats,
        radial,
        radial_t,
        out,
        own_acc,
        partner_acc,
        *scratch,
    )


def ghost_kernel(per_step, channels, bases, *refs):
    blocks = len(ghost_offsets)
    (owner, partner, mask, own, mats, radial, radial_t, out, own_in) = refs[:9]
    arrived = refs[9 : 9 + blocks]
    own_acc = refs[9 + blocks]
    forces = refs[10 + blocks : 10 + 2 * blocks]
    table, partner_acc, *scratch = refs[10 + 2 * blocks :]
    rows = channels + EXTRA
    groups = own.shape[0] // rows
    own_acc[...] = own_in[...]
    partner_acc[...] = jnp.zeros_like(partner_acc)
    for block, offset in enumerate(ghost_offsets):
        start = block * rows
        table[start : start + channels, :] = arrived[block][0:channels, :]
        extra = arrived[block][channels:rows, :].astype(f32)
        coords = extra[0:8] + extra[8:16]
        moved = jnp.concatenate(
            [coords[axis : axis + 1] + domain_edge * offset[axis] for axis in range(3)], 0
        )
        table[start + channels : start + rows, :] = coord_rows(moved, coords[4:5]).astype(bf16)
    pair_body(
        per_step,
        0,
        owner.shape[0],
        groups,
        blocks,
        channels,
        bases,
        owner,
        partner,
        mask,
        own,
        table,
        mats,
        radial,
        radial_t,
        out,
        own_acc,
        partner_acc,
        *scratch,
    )
    for block in range(blocks):
        both = partner_acc[block * 8 : block * 8 + 8, :]
        forces[block][...] = -(both + jnp.concatenate([both[4:], both[:4]], 0))


def final_kernel(blocks, *refs):
    own_ref, partner_ref, send_ref = refs[:3]
    arrived = refs[3 : 3 + blocks]
    forces_ref, energy_ref = refs[3 + blocks :]
    incoming = arrived[0][...]
    for block in range(1, blocks):
        incoming = incoming + arrived[block][...]
    high, low = split_two(incoming[:4])
    send = send_ref[...]
    groups = own_ref.shape[0] // 8
    values = spread_groups(jnp.concatenate([high, low], 0), send // GROUP, groups)
    back = dot_nt(values, one_hot(send & (GROUP - 1), GROUP))
    for group in range(groups):
        part = slice(group * 8, group * 8 + 8)
        total = own_ref[part, :] - partner_ref[part, :] + back[part]
        total = total[:4] + total[4:]
        cols = slice(group * GROUP, (group + 1) * GROUP)
        forces_ref[:, cols] = total[:3]
        energy = own_ref[group * 8 + 3 : group * 8 + 4, :] + own_ref[group * 8 + 7 : group * 8 + 8, :]
        energy_ref[:, cols] = energy


def whole(shape, dtype):
    return jax.ShapeDtypeStruct(shape, dtype)


def call(kernel, outs, name, scratch=(), specs=None, cost=None):
    more = {} if cost is None else dict(cost_estimate=cost)
    return pl.pallas_call(
        kernel,
        grid=(1,),
        in_specs=specs,
        out_specs=tuple(pl.BlockSpec(memory_space=pltpu.VMEM) for _ in outs),
        out_shape=outs,
        scratch_shapes=list(scratch),
        compiler_params=pltpu.CompilerParams(vmem_limit_bytes=VMEM_LIMIT),
        name=name,
        **more,
    )


def shifted(value, offset, sizes, sign):
    used = tuple(axis for axis, step in zip(sizes, offset) if step)
    dims = [size for name, size in used]
    pairs = []
    for flat in range(math.prod(dims)):
        place, rest = [], flat
        for size in reversed(dims):
            place.insert(0, rest % size)
            rest //= size
        target = 0
        for at, size in zip(place, dims):
            target = target * size + (at - sign) % size
        pairs.append((flat, target))
    return lax.ppermute(value, tuple(name for name, size in used), pairs)


def on_device(
    sizes,
    positions,
    features,
    species,
    species_scale,
    w_first,
    w_second,
    w_radial,
    w_mid,
    w_last,
    w_out,
    ghost_send,
    local_first,
    local_second,
    local_mask,
    ghost_owner,
    ghost_index,
    ghost_mask,
):
    channels, own_count = features.shape
    send_count = ghost_send.shape[0]
    bases = w_radial.shape[1]
    rows = channels + EXTRA
    groups = own_count // GROUP
    blocks = len(ghost_offsets)
    send = ghost_send.reshape(1, send_count)
    whole_spec = pl.BlockSpec(memory_space=pltpu.VMEM)
    def tiles(value):
        return value.reshape(value.shape[0] // LANES, LANES)

    small = (
        positions,
        features,
        species.reshape(1, own_count),
        species_scale.reshape(1, species_scale.shape[0]),
        w_first,
        w_second,
        w_radial.T,
        w_mid,
        w_last,
        w_out.reshape(1, channels),
    )
    lists = [send] + [tiles(value) for value in (local_first, local_second, local_mask)]
    own, right, offered, mats, radial, radial_t, out, send, *local = call(
        prep_kernel,
        (
            whole((groups * rows, GROUP), bf16),
            whole((groups * rows, GROUP), bf16),
            whole((rows, send_count), bf16),
            whole((4 * QUAD * channels, QUAD * channels), bf16),
            whole((QUAD * channels, QUAD * 4 * bases), bf16),
            whole((QUAD * 2 * bases, QUAD * channels), bf16),
            whole((channels, LANES), f32),
            *[whole(value.shape, value.dtype) for value in lists],
        ),
        "tables",
        [pltpu.VMEM(value.shape, value.dtype) for value in small]
        + [pltpu.SemaphoreType.DMA((len(small) + len(lists),))],
        [pl.BlockSpec(memory_space=pltpu.HBM)] * (len(small) + len(lists)),
    )(*[pltpu.with_memory_space_constraint(value, pltpu.HBM) for value in (*small, *lists)])
    arrived = [shifted(offered, offset, sizes, 1) for offset in ghost_offsets]

    def scratch(per_step):
        return [
            pltpu.VMEM((per_step, GROUP, QUAD * CHUNK), bf16),
            pltpu.VMEM((per_step, GROUP, QUAD * CHUNK), bf16),
            pltpu.VMEM((per_step, QUAD, channels, CHUNK), f32),
            pltpu.VMEM((per_step, QUAD, channels, CHUNK), f32),
        ]

    def cost(slots):
        return pl.CostEstimate(flops=slots * 400000, bytes_accessed=slots * 12, transcendentals=slots * 200)

    parts = 2
    part_rows = local[0].shape[0] // parts
    weights = (mats, radial, radial_t, out)
    local_step = part_rows * LANES // (QUAD * CHUNK)

    def local_call(part, start):
        operands = [*local, own, right, *weights, *start]
        return call(
            functools.partial(local_kernel, local_step, channels, bases, part * part_rows, part_rows, bool(start)),
            (whole((groups * 8, GROUP), f32), whole((groups * 8, GROUP), f32)),
            "local_pairs",
            scratch(local_step),
            [whole_spec] * len(operands),
            cost(part_rows * LANES),
        )(*operands)

    own_sum, partner_sum = local_call(0, ())
    ghost_lists = [tiles(value) for value in (ghost_owner, ghost_index, ghost_mask)]
    ghost_step = ghost_owner.shape[0] // (QUAD * CHUNK)
    own_sum, *ghost_forces = call(
        functools.partial(ghost_kernel, ghost_step, channels, bases),
        (whole((groups * 8, GROUP), f32),) + (whole((8, send_count), f32),) * blocks,
        "ghost_pairs",
        [
            pltpu.VMEM((blocks * rows, GROUP), bf16),
            pltpu.VMEM(((blocks + blocks % 2) * 8, GROUP), f32),
        ]
        + scratch(ghost_step),
        [whole_spec] * (9 + blocks),
        cost(ghost_owner.shape[0]),
    )(*ghost_lists, own, *weights, own_sum, *arrived)
    returned = [shifted(force, offset, sizes, -1) for force, offset in zip(ghost_forces, ghost_offsets)]
    own_sum, partner_sum = local_call(1, (own_sum, partner_sum))
    forces, energy = call(
        functools.partial(final_kernel, blocks),
        (whole((3, own_count), f32), whole((1, own_count), f32)),
        "totals",
        specs=[whole_spec] * (3 + blocks),
    )(own_sum, partner_sum, send, *returned)
    return forces, energy.reshape(own_count)


def solution(mesh):
    names = ("gx", "gy", "gz")
    sizes = tuple((name, mesh.shape[name]) for name in names)
    split = P(names)
    cols = P(None, names)
    in_specs = (cols, cols, split) + (P(),) * 7 + (split,) * 7
    return jax.shard_map(
        functools.partial(on_device, sizes),
        mesh=mesh,
        in_specs=in_specs,
        out_specs=(cols, split),
        check_vma=False,
    )
```

```python
import functools
import math

import jax
import jax.numpy as jnp
from jax import lax
from jax.experimental import pallas as pl
from jax.experimental.pallas import tpu as pltpu
from jax.sharding import PartitionSpec as P

basis_width = 24.0
domain_edge = 1.0
ghost_offsets = ((1, 0, 0), (0, 1, 0), (0, 0, 1), (1, 1, 0), (1, 0, 1), (0, 1, 1), (1, 1, 1))

EXTRA = 8
OFFERED = 16
GROUP = 256
LANES = 128
CHUNK = 256
QUAD = 4
VMEM_LIMIT = 48 * 1024 * 1024

NT = (((1,), (1,)), ((), ()))
f32 = jnp.float32
bf16 = jnp.bfloat16


def dot(left, right):
    return jnp.dot(left, right, preferred_element_type=f32)


def dot_nt(left, right):
    return lax.dot_general(left, right, NT, preferred_element_type=f32)


def iota(shape, dim):
    return lax.broadcasted_iota(jnp.int32, shape, dim)


def one_hot(row, codes):
    entry = jnp.broadcast_to(row.astype(f32), (16, row.shape[1])).astype(bf16)
    entry = jnp.concatenate([entry] * (codes.shape[0] // 16), 0)
    pieces = [
        jnp.where(codes == entry[:, start : start + LANES], bf16(1), bf16(0))
        for start in range(0, row.shape[1], LANES)
    ]
    return jnp.concatenate(pieces, 1)


def row_codes(count):
    return iota((count, LANES), 0).astype(f32).astype(bf16)


def split_two(value):
    high = value.astype(bf16).astype(f32)
    return high, value - high


def coord_rows(coords, gain):
    high, low = split_two(coords)
    return jnp.concatenate([high, gain, low, jnp.zeros_like(gain)], 0)


def eye(count):
    return (iota((count, count), 0) == iota((count, count), 1)).astype(bf16)


def prep_kernel(*refs):
    sources = refs[:14]
    own_ref, right_ref, offered_ref, mats_ref, radial_ref, radial_t_ref, out_ref = refs[14:21]
    targets = refs[25:35] + refs[21:25]
    landed = refs[35]
    copies = [
        pltpu.make_async_copy(source, target, landed.at[place])
        for place, (source, target) in enumerate(zip(sources, targets))
    ]
    for copy in copies:
        copy.start()
    for copy in copies:
        copy.wait()
    (
        positions_ref,
        features_ref,
        species_ref,
        scale_ref,
        w_first_ref,
        w_second_ref,
        radial_w_ref,
        w_mid_ref,
        w_last_ref,
        w_out_ref,
        send_ref,
    ) = targets[:11]
    channels = features_ref.shape[0]
    count = features_ref.shape[1]
    species = species_ref[...]
    gain = jnp.zeros((1, count), f32)
    for kind in range(scale_ref.shape[1]):
        scale = scale_ref[:, kind : kind + 1].astype(f32)
        gain = jnp.where(species == kind, scale, gain)
    positions = positions_ref[...]
    left = dot(w_first_ref[...], features_ref[...]).astype(bf16).astype(f32)
    right = dot(w_second_ref[...], features_ref[...]).astype(bf16).astype(f32)
    place = jnp.concatenate([positions, gain, jnp.zeros((EXTRA - 4, count), f32)], 0)
    own_ref[0:channels, :] = 0.5 * left
    own_ref[channels:, :] = place
    right_ref[0:channels, :] = 0.5 * right
    right_ref[channels:, :] = place
    parts = coord_rows(positions, gain)
    table = jnp.concatenate([0.5 * right, parts, jnp.zeros_like(parts)], 0).astype(bf16)
    send = send_ref[...]
    hot = one_hot(send & (GROUP - 1), row_codes(GROUP))
    chosen = dot(table[:, 0:GROUP], hot)
    for group in range(1, count // GROUP):
        picked = dot(table[:, group * GROUP : (group + 1) * GROUP], hot)
        chosen = jnp.where(send // GROUP == group, picked, chosen)
    offered_ref[...] = chosen.astype(bf16)

    unit = eye(channels)
    w_mid = w_mid_ref[...]
    w_last = w_last_ref[...]
    last_t = dot_nt(unit, w_last).astype(bf16)
    mid_t = dot_nt(unit, w_mid).astype(bf16)
    wide = QUAD * channels
    for place, matrix in enumerate((w_mid, w_last, last_t, mid_t)):
        mats_ref[place * wide : (place + 1) * wide, :] = (0.5 * diagonal_copies(matrix)).astype(bf16)
    bases = radial_w_ref.shape[0]
    high, low = split_two(radial_w_ref[...])
    high = high.astype(bf16)
    low = low.astype(bf16)
    spread = dot_nt(unit, jnp.concatenate([high, high, low, low], 0)).astype(bf16)
    radial_ref[...] = (0.5 * diagonal_copies(spread)).astype(bf16)
    radial_t_ref[...] = diagonal_copies(jnp.concatenate([high, low], 0)).astype(bf16)
    w_out = w_out_ref[...]
    diagonal = jnp.where(iota((channels, channels), 0) == iota((channels, channels), 1), w_out, 0.0)
    out_ref[...] = jnp.broadcast_to(jnp.sum(diagonal, axis=1, keepdims=True), (channels, LANES))


def diagonal_copies(matrix):
    high, wide = matrix.shape
    repeat = (iota((wide, QUAD * wide), 0) == iota((wide, QUAD * wide), 1) % wide).astype(bf16)
    row = dot(matrix, repeat)
    full = jnp.concatenate([row] * QUAD, 0)
    return jnp.where(iota(full.shape, 0) // high == iota(full.shape, 1) // wide, full, 0.0)


def group_pick(values, high, rows, groups):
    chosen = values[:rows]
    for group in range(1, groups):
        chosen = jnp.where(high == group, values[group * rows : (group + 1) * rows], chosen)
    return chosen


def spread_groups(values, high, groups):
    pieces = [jnp.where(high == group, values, 0.0) for group in range(groups)]
    return jnp.concatenate(pieces, 0).astype(bf16)


def lane_pick(table_ref, row):
    rows, count = table_ref.shape
    lane = jnp.broadcast_to(row & (LANES - 1), (rows, LANES))
    high = row // LANES
    chosen = None
    for group in range(count // LANES):
        part = table_ref[:, group * LANES : (group + 1) * LANES]
        picked = jnp.take_along_axis(part, lane, axis=1, mode="promise_in_bounds")
        chosen = picked if chosen is None else jnp.where(high == group, picked, chosen)
    return chosen


def pair_body(
    per_step,
    first_row,
    row_count,
    own_groups,
    partner_groups,
    channels,
    bases,
    owner_ref,
    partner_ref,
    mask_ref,
    own_ref,
    right_ref,
    mats_ref,
    radial_ref,
    radial_t_ref,
    out_ref,
    sums,
    hot,
    hot_wide,
    slope_one,
    slope_two,
    codes_ref,
):
    rows = channels + EXTRA
    line = CHUNK // LANES
    block = QUAD * line
    wide = QUAD * channels
    steps = row_count // (per_step * block)
    w_out = jnp.concatenate([out_ref[...]] * line, 1)
    centers = iota((bases, CHUNK), 0).astype(f32) * (1.0 / (bases - 1))
    sub = iota((8, CHUNK), 0)
    quads = range(QUAD)
    codes_ref[...] = row_codes(GROUP)

    def matrix(place):
        return mats_ref[place * wide : (place + 1) * wide, :]

    def part(values, number, size=channels):
        return values[number * size : (number + 1) * size]

    def silu_pair(half):
        grow = jnp.tanh(half)
        plus = 1.0 + grow
        hidden = half * plus
        return hidden, plus + hidden * (1.0 - grow)

    def chunk(base, number):
        at = pl.multiple_of(base + number * block, block)
        owner_rows = owner_ref[pl.ds(at, block), :]
        partner_rows = partner_ref[pl.ds(at, block), :]
        live_rows = mask_ref[pl.ds(at, block), :].astype(f32)

        def row_of(values, quad):
            return jnp.concatenate(
                [values[quad * line + piece : quad * line + piece + 1, :] for piece in range(line)], 1
            )

        own_high, partner_high, projected, shifts, squares, weights, stacks, slopes = ([] for _ in range(8))
        for quad in quads:
            cols = slice(quad * CHUNK, (quad + 1) * CHUNK)
            owner = row_of(owner_rows, quad)
            partner = row_of(partner_rows, quad)
            own_high.append(owner // LANES)
            partner_high.append(partner // LANES)
            hot[number, 0:LANES, cols] = one_hot(owner & (LANES - 1), codes_ref[0:LANES, :])
            if hot_wide is None:
                hot[number, LANES:, cols] = one_hot(partner & (LANES - 1), codes_ref[0:LANES, :])
            else:
                both = one_hot(partner & (GROUP - 1), codes_ref[...])
                hot_wide[number, :, cols] = both
                hot[number, LANES:, cols] = both[0:LANES] + both[LANES:]
            yield
        for quad in quads:
            cols = slice(quad * CHUNK, (quad + 1) * CHUNK)
            pieces = []
            for piece in range(line):
                at_row = quad * line + piece
                pieces.append(lane_pick(own_ref, owner_rows[at_row : at_row + 1, :]))
            own_vals = jnp.concatenate(pieces, 1)
            if hot_wide is None:
                pieces = []
                for piece in range(line):
                    at_row = quad * line + piece
                    pieces.append(lane_pick(right_ref, partner_rows[at_row : at_row + 1, :]))
                partner_vals = jnp.concatenate(pieces, 1)
                partner_coords = partner_vals[channels:]
            else:
                wide_high = row_of(partner_rows, quad) // GROUP
                partner_vals = group_pick(
                    dot(right_ref[...], hot_wide[number, :, cols]), wide_high, rows, partner_groups * LANES // GROUP
                )
                extra = partner_vals[channels:]
                partner_coords = extra + jnp.concatenate([extra[4:], extra[:4]], 0)
            projected.append(own_vals[:channels] + partner_vals[:channels])
            own_coords = own_vals[channels:]
            shift = partner_coords - own_coords
            square = shift * shift
            squared = square[0:1] + square[1:2] + square[2:3]
            weights.append(row_of(live_rows, quad) * own_coords[3:4] * partner_coords[3:4])
            away = squared - centers
            basis = jnp.exp(-basis_width * (away * away))
            basis_high, basis_low = split_two(basis)
            stacks.append(jnp.concatenate([basis_high, basis_low, basis_high, basis_low], 0).astype(bf16))
            slopes.append((-2.0 * basis_width) * away * basis)
            shifts.append(shift)
            squares.append(squared)
            yield
        radial = dot(radial_ref[...], jnp.concatenate(stacks, 0))
        yield
        pieces = []
        for quad in quads:
            hidden, slope_one[number, quad] = silu_pair(projected[quad] + part(radial, quad))
            pieces.append(hidden.astype(bf16))
        yield
        half = dot(matrix(0), jnp.concatenate(pieces, 0))
        yield
        pieces = []
        for quad in quads:
            hidden, slope_two[number, quad] = silu_pair(part(half, quad))
            pieces.append(hidden.astype(bf16))
        yield
        half = dot(matrix(1), jnp.concatenate(pieces, 0))
        yield
        pieces = []
        readouts = []
        for quad in quads:
            hidden, slope = silu_pair(part(half, quad))
            readouts.append(jnp.sum(w_out * hidden, axis=0, keepdims=True))
            pieces.append(((0.5 * w_out) * slope).astype(bf16))
        yield
        back = dot(matrix(2), jnp.concatenate(pieces, 0))
        yield
        pieces = [(part(back, quad) * slope_two[number, quad]).astype(bf16) for quad in quads]
        back = dot(matrix(3), jnp.concatenate(pieces, 0))
        yield
        pieces = [(part(back, quad) * slope_one[number, quad]).astype(bf16) for quad in quads]
        back = dot(radial_t_ref[...], jnp.concatenate(pieces, 0))
        yield
        parts = []
        for quad in quads:
            two = part(back, quad, 2 * bases)
            readout_slope = jnp.sum((two[:bases] + two[bases:]) * slopes[quad], axis=0, keepdims=True)
            near = jnp.maximum(1.0 - squares[quad], 0.0)
            weight_near = weights[quad] * near
            energy = weight_near * near * readouts[quad]
            slope = weight_near * (near * readout_slope - 2.0 * readouts[quad])
            push = (2.0 * slope) * shifts[quad]
            high, low = split_two(jnp.where(sub == 3, energy, push))
            values = jnp.concatenate([high[:4], low[:4]], 0)
            parts.append(
                jnp.concatenate(
                    [jnp.where(own_high[quad] == group, values, 0.0) for group in range(own_groups)]
                    + [jnp.where(partner_high[quad] == group, values, 0.0) for group in range(partner_groups)],
                    0,
                ).astype(bf16)
            )
        yield
        sums[...] += dot_nt(jnp.concatenate(parts, 1), hot[number])

    def step(index, unused):
        base = pl.multiple_of(first_row + index * (per_step * block), block)
        running = []
        waiting = [chunk(base, number) for number in range(per_step)]
        while running or waiting:
            if waiting:
                running.append(waiting.pop(0))
            for _ in range(2):
                running = [task for task in running if next(task, task) is not task]
        return unused

    lax.fori_loop(0, steps, step, 0)


def local_kernel(per_step, channels, bases, first_row, row_count, with_start, *refs):
    count = 9 + with_start
    owner, partner, mask, own, right, *weights = refs[:9]
    sums, hot, *scratch = refs[count:]
    sums[...] = refs[9][...] if with_start else jnp.zeros_like(sums)
    groups = own.shape[1] // LANES
    pair_body(
        per_step,
        first_row,
        row_count,
        groups,
        groups,
        channels,
        bases,
        owner,
        partner,
        mask,
        own,
        right,
        *weights,
        sums,
        hot,
        None,
        *scratch,
    )


def ghost_kernel(per_step, channels, bases, *refs):
    blocks = len(ghost_offsets)
    owner, partner, mask, own, *weights = refs[:8]
    sums_in = refs[8]
    arrived = refs[9 : 9 + blocks]
    sums_out = refs[9 + blocks]
    forces = refs[10 + blocks : 10 + 2 * blocks]
    table, sums, *scratch = refs[10 + 2 * blocks :]
    groups = own.shape[1] // LANES
    partner_groups = blocks * GROUP // LANES
    sums[...] = jnp.zeros_like(sums)
    pieces = []
    for block, offset in enumerate(ghost_offsets):
        extra = arrived[block][channels : channels + OFFERED, :].astype(f32)
        moved = jnp.concatenate(
            [extra[axis : axis + 1] + extra[axis + 4 : axis + 5] + domain_edge * offset[axis] for axis in range(3)], 0
        )
        pieces += [arrived[block][0:channels, :].astype(f32), coord_rows(moved, extra[3:4])]
    pieces.append(jnp.zeros((table.shape[0] - blocks * (channels + EXTRA), GROUP), f32))
    table[...] = jnp.concatenate(pieces, 0).astype(bf16)
    pair_body(
        per_step,
        0,
        owner.shape[0],
        groups,
        partner_groups,
        channels,
        bases,
        owner,
        partner,
        mask,
        own,
        table,
        *weights,
        sums,
        *scratch,
    )
    first = groups * 8
    sums_out[0:first, :] = sums_in[0:first, :] + sums[0:first, :]
    sums_out[first:, :] = sums_in[first:, :]
    for block in range(blocks):
        for half in range(GROUP // LANES):
            start = first + (block * (GROUP // LANES) + half) * 8
            both = sums[start : start + 8, LANES:]
            forces[block][:, half * LANES : (half + 1) * LANES] = -(
                both + jnp.concatenate([both[4:], both[:4]], 0)
            )


def final_kernel(blocks, *refs):
    sums_ref, send_ref = refs[:2]
    arrived = refs[2 : 2 + blocks]
    forces_ref, energy_ref = refs[2 + blocks :]
    incoming = arrived[0][...]
    for block in range(1, blocks):
        incoming = incoming + arrived[block][...]
    high, low = split_two(incoming[:4])
    send = send_ref[...]
    groups = sums_ref.shape[0] // 16
    values = spread_groups(jnp.concatenate([high, low], 0), send // LANES, groups)
    back = dot_nt(values, one_hot(send & (LANES - 1), row_codes(LANES)))
    for group in range(groups):
        own = sums_ref[group * 8 : group * 8 + 8, 0:LANES]
        partner = sums_ref[(groups + group) * 8 : (groups + group) * 8 + 8, LANES:]
        total = own - partner + back[group * 8 : group * 8 + 8]
        cols = slice(group * LANES, (group + 1) * LANES)
        forces_ref[:, cols] = total[0:3] + total[4:7]
        energy_ref[:, cols] = own[3:4] + own[7:8]


def whole(shape, dtype):
    return jax.ShapeDtypeStruct(shape, dtype)


def call(kernel, outs, name, scratch=(), specs=None, cost=None):
    more = {} if cost is None else dict(cost_estimate=cost)
    return pl.pallas_call(
        kernel,
        grid=(1,),
        in_specs=specs,
        out_specs=tuple(pl.BlockSpec(memory_space=pltpu.VMEM) for _ in outs),
        out_shape=outs,
        scratch_shapes=list(scratch),
        compiler_params=pltpu.CompilerParams(vmem_limit_bytes=VMEM_LIMIT),
        name=name,
        **more,
    )


def shifted(value, offset, sizes, sign):
    used = tuple(axis for axis, step in zip(sizes, offset) if step)
    dims = [size for name, size in used]
    pairs = []
    for flat in range(math.prod(dims)):
        place, rest = [], flat
        for size in reversed(dims):
            place.insert(0, rest % size)
            rest //= size
        target = 0
        for at, size in zip(place, dims):
            target = target * size + (at - sign) % size
        pairs.append((flat, target))
    return lax.ppermute(value, tuple(name for name, size in used), pairs)


def on_device(
    sizes,
    positions,
    features,
    species,
    species_scale,
    w_first,
    w_second,
    w_radial,
    w_mid,
    w_last,
    w_out,
    ghost_send,
    local_first,
    local_second,
    local_mask,
    ghost_owner,
    ghost_index,
    ghost_mask,
):
    channels, own_count = features.shape
    send_count = ghost_send.shape[0]
    bases = w_radial.shape[1]
    rows = channels + EXTRA
    groups = own_count // LANES
    blocks = len(ghost_offsets)
    send = ghost_send.reshape(1, send_count)
    whole_spec = pl.BlockSpec(memory_space=pltpu.VMEM)
    def tiles(value):
        return value.reshape(value.shape[0] // LANES, LANES)

    small = (
        positions,
        features,
        species.reshape(1, own_count),
        species_scale.reshape(1, species_scale.shape[0]),
        w_first,
        w_second,
        w_radial.T,
        w_mid,
        w_last,
        w_out.reshape(1, channels),
    )
    lists = [send] + [tiles(value) for value in (local_first, local_second, local_mask)]
    own, right, offered, mats, radial, radial_t, out, send, *local = call(
        prep_kernel,
        (
            whole((rows, own_count), f32),
            whole((rows, own_count), f32),
            whole((channels + OFFERED, send_count), bf16),
            whole((4 * QUAD * channels, QUAD * channels), bf16),
            whole((QUAD * channels, QUAD * 4 * bases), bf16),
            whole((QUAD * 2 * bases, QUAD * channels), bf16),
            whole((channels, LANES), f32),
            *[whole(value.shape, value.dtype) for value in lists],
        ),
        "tables",
        [pltpu.VMEM(value.shape, value.dtype) for value in small]
        + [pltpu.SemaphoreType.DMA((len(small) + len(lists),))],
        [pl.BlockSpec(memory_space=pltpu.HBM)] * (len(small) + len(lists)),
    )(*[pltpu.with_memory_space_constraint(value, pltpu.HBM) for value in (*small, *lists)])
    arrived = [shifted(offered, offset, sizes, 1) for offset in ghost_offsets]

    def scratch(per_step, hots):
        return [pltpu.VMEM((per_step, GROUP, QUAD * CHUNK), bf16) for _ in range(hots)] + [
            pltpu.VMEM((per_step, QUAD, channels, CHUNK), f32),
            pltpu.VMEM((per_step, QUAD, channels, CHUNK), f32),
            pltpu.VMEM((GROUP, LANES), bf16),
        ]

    def cost(slots):
        return pl.CostEstimate(flops=slots * 400000, bytes_accessed=slots * 12, transcendentals=slots * 200)

    parts = 2
    part_rows = local[0].shape[0] // parts
    weights = (mats, radial, radial_t, out)
    local_step = part_rows * LANES // (QUAD * CHUNK)

    def local_call(part, start):
        operands = [*local, own, right, *weights, *start]
        (sums,) = call(
            functools.partial(
                local_kernel, local_step, channels, bases, part * part_rows, part_rows, len(start)
            ),
            (whole((groups * 16, GROUP), f32),),
            "local_pairs",
            scratch(local_step, 1),
            [whole_spec] * len(operands),
            cost(part_rows * LANES),
        )(*operands)
        return sums

    sums = local_call(0, ())
    ghost_lists = [tiles(value) for value in (ghost_owner, ghost_index, ghost_mask)]
    ghost_step = ghost_owner.shape[0] // (QUAD * CHUNK)
    partner_rows = blocks * GROUP // LANES * 8
    table_rows = -(-blocks * rows // 16) * 16
    sums, *ghost_forces = call(
        functools.partial(ghost_kernel, ghost_step, channels, bases),
        (whole((groups * 16, GROUP), f32),) + (whole((8, send_count), f32),) * blocks,
        "ghost_pairs",
        [pltpu.VMEM((table_rows, GROUP), bf16), pltpu.VMEM((groups * 8 + partner_rows, GROUP), f32)]
        + scratch(ghost_step, 2),
        [whole_spec] * (9 + blocks),
        cost(ghost_owner.shape[0]),
    )(*ghost_lists, own, *weights, sums, *arrived)
    returned = [shifted(force, offset, sizes, -1) for force, offset in zip(ghost_forces, ghost_offsets)]
    sums = local_call(1, (sums,))
    forces, energy = call(
        functools.partial(final_kernel, blocks),
        (whole((3, own_count), f32), whole((1, own_count), f32)),
        "totals",
        specs=[whole_spec] * (2 + blocks),
    )(sums, send, *returned)
    return forces, energy.reshape(own_count)


def solution(mesh):
    names = ("gx", "gy", "gz")
    sizes = tuple((name, mesh.shape[name]) for name in names)
    split = P(names)
    cols = P(None, names)
    in_specs = (cols, cols, split) + (P(),) * 7 + (split,) * 7
    return jax.shard_map(
        functools.partial(on_device, sizes),
        mesh=mesh,
        in_specs=in_specs,
        out_specs=(cols, split),
        check_vma=False,
    )
```

```python
import functools
import math

import jax
import jax.numpy as jnp
from jax import lax
from jax.experimental import pallas as pl
from jax.experimental.pallas import tpu as pltpu
from jax.sharding import PartitionSpec as P

basis_width = 24.0
domain_edge = 1.0
ghost_offsets = ((1, 0, 0), (0, 1, 0), (0, 0, 1), (1, 1, 0), (1, 0, 1), (0, 1, 1), (1, 1, 1))

EXTRA = 8
OFFERED = 16
GROUP = 256
LANES = 128
CHUNK = 256
QUAD = 4
VMEM_LIMIT = 48 * 1024 * 1024

NT = (((1,), (1,)), ((), ()))
f32 = jnp.float32
bf16 = jnp.bfloat16


def dot(left, right):
    return jnp.dot(left, right, preferred_element_type=f32)


def dot_nt(left, right):
    return lax.dot_general(left, right, NT, preferred_element_type=f32)


def iota(shape, dim):
    return lax.broadcasted_iota(jnp.int32, shape, dim)


def one_hot(row, codes):
    entry = jnp.broadcast_to(row.astype(f32), (16, row.shape[1])).astype(bf16)
    entry = jnp.concatenate([entry] * (codes.shape[0] // 16), 0)
    pieces = [
        jnp.where(codes == entry[:, start : start + LANES], bf16(1), bf16(0))
        for start in range(0, row.shape[1], LANES)
    ]
    return jnp.concatenate(pieces, 1)


def row_codes(count):
    return iota((count, LANES), 0).astype(f32).astype(bf16)


def split_two(value):
    high = value.astype(bf16).astype(f32)
    return high, value - high


def coord_rows(coords, gain):
    high, low = split_two(coords)
    return jnp.concatenate([high, gain, low, jnp.zeros_like(gain)], 0)


def eye(count):
    return (iota((count, count), 0) == iota((count, count), 1)).astype(bf16)


def prep_kernel(*refs):
    sources = refs[:14]
    own_ref, right_ref, offered_ref, mats_ref, radial_ref, radial_t_ref, out_ref = refs[14:21]
    targets = refs[25:35] + refs[21:25]
    landed = refs[35]
    copies = [
        pltpu.make_async_copy(source, target, landed.at[place])
        for place, (source, target) in enumerate(zip(sources, targets))
    ]
    for copy in copies:
        copy.start()
    for copy in copies:
        copy.wait()
    (
        positions_ref,
        features_ref,
        species_ref,
        scale_ref,
        w_first_ref,
        w_second_ref,
        radial_w_ref,
        w_mid_ref,
        w_last_ref,
        w_out_ref,
        send_ref,
    ) = targets[:11]
    channels = features_ref.shape[0]
    count = features_ref.shape[1]
    species = species_ref[...]
    gain = jnp.zeros((1, count), f32)
    for kind in range(scale_ref.shape[1]):
        scale = scale_ref[:, kind : kind + 1].astype(f32)
        gain = jnp.where(species == kind, scale, gain)
    positions = positions_ref[...]
    left = dot(w_first_ref[...], features_ref[...]).astype(bf16).astype(f32)
    right = dot(w_second_ref[...], features_ref[...]).astype(bf16).astype(f32)
    own_ref[0:channels, :] = 0.5 * left
    own_ref[channels:, :] = jnp.concatenate([positions, gain, jnp.zeros((EXTRA - 4, count), f32)], 0)
    column = jnp.concatenate([0.5 * right, coord_rows(positions, gain)], 0)
    groups = count // GROUP
    rows = channels + EXTRA
    table = jnp.concatenate([column[:, group * GROUP : (group + 1) * GROUP] for group in range(groups)], 0)
    spare = right_ref.shape[0] - groups * rows
    if spare:
        table = jnp.concatenate([table, jnp.zeros((spare, GROUP), f32)], 0)
    table = table.astype(bf16)
    right_ref[...] = table
    send = send_ref[...]
    picked = dot(table, one_hot(send & (GROUP - 1), row_codes(GROUP)))
    chosen = group_pick(picked, send // GROUP, rows, groups)
    chosen = jnp.concatenate([chosen, jnp.zeros((OFFERED - EXTRA, chosen.shape[1]), f32)], 0)
    offered_ref[...] = chosen.astype(bf16)

    unit = eye(channels)
    w_mid = w_mid_ref[...]
    w_last = w_last_ref[...]
    last_t = dot_nt(unit, w_last).astype(bf16)
    mid_t = dot_nt(unit, w_mid).astype(bf16)
    wide = QUAD * channels
    for place, matrix in enumerate((w_mid, w_last, last_t, mid_t)):
        mats_ref[place * wide : (place + 1) * wide, :] = (0.5 * diagonal_copies(matrix)).astype(bf16)
    bases = radial_w_ref.shape[0]
    high, low = split_two(radial_w_ref[...])
    high = high.astype(bf16)
    low = low.astype(bf16)
    spread = dot_nt(unit, jnp.concatenate([high, high, low, low], 0)).astype(bf16)
    radial_ref[...] = (0.5 * diagonal_copies(spread)).astype(bf16)
    radial_t_ref[...] = diagonal_copies(jnp.concatenate([high, low], 0)).astype(bf16)
    w_out = w_out_ref[...]
    diagonal = jnp.where(iota((channels, channels), 0) == iota((channels, channels), 1), w_out, 0.0)
    out_ref[...] = jnp.broadcast_to(jnp.sum(diagonal, axis=1, keepdims=True), (channels, LANES))


def diagonal_copies(matrix):
    high, wide = matrix.shape
    repeat = (iota((wide, QUAD * wide), 0) == iota((wide, QUAD * wide), 1) % wide).astype(bf16)
    row = dot(matrix, repeat)
    full = jnp.concatenate([row] * QUAD, 0)
    return jnp.where(iota(full.shape, 0) // high == iota(full.shape, 1) // wide, full, 0.0)


def group_pick(values, high, rows, groups):
    chosen = values[:rows]
    for group in range(1, groups):
        chosen = jnp.where(high == group, values[group * rows : (group + 1) * rows], chosen)
    return chosen


def spread_groups(values, high, groups):
    pieces = [jnp.where(high == group, values, 0.0) for group in range(groups)]
    return jnp.concatenate(pieces, 0).astype(bf16)


def lane_pick(table_ref, row):
    rows, count = table_ref.shape
    lane = jnp.broadcast_to(row & (LANES - 1), (rows, LANES))
    high = row // LANES
    chosen = None
    for group in range(count // LANES):
        part = table_ref[:, group * LANES : (group + 1) * LANES]
        picked = jnp.take_along_axis(part, lane, axis=1, mode="promise_in_bounds")
        chosen = picked if chosen is None else jnp.where(high == group, picked, chosen)
    return chosen


def pair_body(
    per_step,
    first_row,
    row_count,
    own_groups,
    partner_groups,
    channels,
    bases,
    owner_ref,
    partner_ref,
    mask_ref,
    own_ref,
    right_ref,
    mats_ref,
    radial_ref,
    radial_t_ref,
    out_ref,
    sums,
    hot,
    hot_wide,
    slope_one,
    slope_two,
    codes_ref,
):
    rows = channels + EXTRA
    line = CHUNK // LANES
    block = QUAD * line
    wide = QUAD * channels
    steps = row_count // (per_step * block)
    w_out = jnp.concatenate([out_ref[...]] * line, 1)
    centers = iota((bases, CHUNK), 0).astype(f32) * (1.0 / (bases - 1))
    sub = iota((8, CHUNK), 0)
    quads = range(QUAD)
    codes_ref[...] = row_codes(GROUP)

    def matrix(place):
        return mats_ref[place * wide : (place + 1) * wide, :]

    def part(values, number, size=channels):
        return values[number * size : (number + 1) * size]

    def silu_pair(half):
        grow = jnp.tanh(half)
        plus = 1.0 + grow
        hidden = half * plus
        return hidden, plus + hidden * (1.0 - grow)

    def chunk(base, number):
        at = pl.multiple_of(base + number * block, block)
        owner_rows = owner_ref[pl.ds(at, block), :]
        partner_rows = partner_ref[pl.ds(at, block), :]
        live_rows = mask_ref[pl.ds(at, block), :].astype(f32)

        def row_of(values, quad):
            return jnp.concatenate(
                [values[quad * line + piece : quad * line + piece + 1, :] for piece in range(line)], 1
            )

        own_high, partner_high, projected, shifts, squares, weights, stacks, slopes = ([] for _ in range(8))
        for quad in quads:
            cols = slice(quad * CHUNK, (quad + 1) * CHUNK)
            owner = row_of(owner_rows, quad)
            partner = row_of(partner_rows, quad)
            own_high.append(owner // LANES)
            partner_high.append(partner // LANES)
            hot[number, 0:LANES, cols] = one_hot(owner & (LANES - 1), codes_ref[0:LANES, :])
            if hot_wide is None:
                hot[number, LANES:, cols] = one_hot(partner & (LANES - 1), codes_ref[0:LANES, :])
            else:
                both = one_hot(partner & (GROUP - 1), codes_ref[...])
                hot_wide[number, :, cols] = both
                hot[number, LANES:, cols] = both[0:LANES] + both[LANES:]
            yield
        for quad in quads:
            cols = slice(quad * CHUNK, (quad + 1) * CHUNK)
            pieces = []
            for piece in range(line):
                at_row = quad * line + piece
                pieces.append(lane_pick(own_ref, owner_rows[at_row : at_row + 1, :]))
            own_vals = jnp.concatenate(pieces, 1)
            if hot_wide is None:
                pieces = []
                for piece in range(line):
                    at_row = quad * line + piece
                    pieces.append(lane_pick(right_ref, partner_rows[at_row : at_row + 1, :]))
                partner_vals = jnp.concatenate(pieces, 1)
                partner_coords = partner_vals[channels:]
            else:
                wide_high = row_of(partner_rows, quad) // GROUP
                partner_vals = group_pick(
                    dot(right_ref[...], hot_wide[number, :, cols]), wide_high, rows, partner_groups * LANES // GROUP
                )
                extra = partner_vals[channels:]
                partner_coords = extra + jnp.concatenate([extra[4:], extra[:4]], 0)
            projected.append(own_vals[:channels] + partner_vals[:channels])
            own_coords = own_vals[channels:]
            shift = partner_coords - own_coords
            square = shift * shift
            squared = square[0:1] + square[1:2] + square[2:3]
            weights.append(row_of(live_rows, quad) * own_coords[3:4] * partner_coords[3:4])
            away = squared - centers
            basis = jnp.exp(-basis_width * (away * away))
            basis_high, basis_low = split_two(basis)
            stacks.append(jnp.concatenate([basis_high, basis_low, basis_high, basis_low], 0).astype(bf16))
            slopes.append((-2.0 * basis_width) * away * basis)
            shifts.append(shift)
            squares.append(squared)
            yield
        radial = dot(radial_ref[...], jnp.concatenate(stacks, 0))
        yield
        pieces = []
        for quad in quads:
            hidden, slope_one[number, quad] = silu_pair(projected[quad] + part(radial, quad))
            pieces.append(hidden.astype(bf16))
        yield
        half = dot(matrix(0), jnp.concatenate(pieces, 0))
        yield
        pieces = []
        for quad in quads:
            hidden, slope_two[number, quad] = silu_pair(part(half, quad))
            pieces.append(hidden.astype(bf16))
        yield
        half = dot(matrix(1), jnp.concatenate(pieces, 0))
        yield
        pieces = []
        readouts = []
        for quad in quads:
            hidden, slope = silu_pair(part(half, quad))
            readouts.append(jnp.sum(w_out * hidden, axis=0, keepdims=True))
            pieces.append(((0.5 * w_out) * slope).astype(bf16))
        yield
        back = dot(matrix(2), jnp.concatenate(pieces, 0))
        yield
        pieces = [(part(back, quad) * slope_two[number, quad]).astype(bf16) for quad in quads]
        back = dot(matrix(3), jnp.concatenate(pieces, 0))
        yield
        pieces = [(part(back, quad) * slope_one[number, quad]).astype(bf16) for quad in quads]
        back = dot(radial_t_ref[...], jnp.concatenate(pieces, 0))
        yield
        parts = []
        for quad in quads:
            two = part(back, quad, 2 * bases)
            readout_slope = jnp.sum((two[:bases] + two[bases:]) * slopes[quad], axis=0, keepdims=True)
            near = jnp.maximum(1.0 - squares[quad], 0.0)
            weight_near = weights[quad] * near
            energy = weight_near * near * readouts[quad]
            slope = weight_near * (near * readout_slope - 2.0 * readouts[quad])
            push = (2.0 * slope) * shifts[quad]
            high, low = split_two(jnp.where(sub == 3, energy, push))
            values = jnp.concatenate([high[:4], low[:4]], 0)
            parts.append(
                jnp.concatenate(
                    [jnp.where(own_high[quad] == group, values, 0.0) for group in range(own_groups)]
                    + [jnp.where(partner_high[quad] == group, values, 0.0) for group in range(partner_groups)],
                    0,
                ).astype(bf16)
            )
        yield
        sums[...] += dot_nt(jnp.concatenate(parts, 1), hot[number])

    def step(index, unused):
        base = pl.multiple_of(first_row + index * (per_step * block), block)
        running = []
        waiting = [chunk(base, number) for number in range(per_step)]
        while running or waiting:
            if waiting:
                running.append(waiting.pop(0))
            for _ in range(2):
                running = [task for task in running if next(task, task) is not task]
        return unused

    lax.fori_loop(0, steps, step, 0)


def local_kernel(per_step, channels, bases, first_row, row_count, with_start, *refs):
    count = 9 + with_start
    owner, partner, mask, own, right, *weights = refs[:9]
    sums, hot, *scratch = refs[count:]
    sums[...] = refs[9][...] if with_start else jnp.zeros_like(sums)
    groups = own.shape[1] // LANES
    pair_body(
        per_step,
        first_row,
        row_count,
        groups,
        groups,
        channels,
        bases,
        owner,
        partner,
        mask,
        own,
        right,
        *weights,
        sums,
        hot,
        *scratch,
    )


def ghost_kernel(per_step, channels, bases, *refs):
    blocks = len(ghost_offsets)
    owner, partner, mask, own, *weights = refs[:8]
    sums_in = refs[8]
    arrived = refs[9 : 9 + blocks]
    sums_out = refs[9 + blocks]
    forces = refs[10 + blocks : 10 + 2 * blocks]
    table, sums, *scratch = refs[10 + 2 * blocks :]
    groups = own.shape[1] // LANES
    partner_groups = blocks * GROUP // LANES
    sums[...] = jnp.zeros_like(sums)
    pieces = []
    for block, offset in enumerate(ghost_offsets):
        extra = arrived[block][channels : channels + OFFERED, :].astype(f32)
        moved = jnp.concatenate(
            [extra[axis : axis + 1] + extra[axis + 4 : axis + 5] + domain_edge * offset[axis] for axis in range(3)], 0
        )
        pieces += [arrived[block][0:channels, :].astype(f32), coord_rows(moved, extra[3:4])]
    pieces.append(jnp.zeros((table.shape[0] - blocks * (channels + EXTRA), GROUP), f32))
    table[...] = jnp.concatenate(pieces, 0).astype(bf16)
    pair_body(
        per_step,
        0,
        owner.shape[0],
        groups,
        partner_groups,
        channels,
        bases,
        owner,
        partner,
        mask,
        own,
        table,
        *weights,
        sums,
        *scratch,
    )
    first = groups * 8
    sums_out[0:first, :] = sums_in[0:first, :] + sums[0:first, :]
    sums_out[first:, :] = sums_in[first:, :]
    for block in range(blocks):
        for half in range(GROUP // LANES):
            start = first + (block * (GROUP // LANES) + half) * 8
            both = sums[start : start + 8, LANES:]
            forces[block][:, half * LANES : (half + 1) * LANES] = -(
                both + jnp.concatenate([both[4:], both[:4]], 0)
            )


def final_kernel(blocks, *refs):
    sums_ref, send_ref = refs[:2]
    arrived = refs[2 : 2 + blocks]
    forces_ref, energy_ref = refs[2 + blocks :]
    incoming = arrived[0][...]
    for block in range(1, blocks):
        incoming = incoming + arrived[block][...]
    high, low = split_two(incoming[:4])
    send = send_ref[...]
    groups = sums_ref.shape[0] // 16
    values = spread_groups(jnp.concatenate([high, low], 0), send // LANES, groups)
    back = dot_nt(values, one_hot(send & (LANES - 1), row_codes(LANES)))
    for group in range(groups):
        own = sums_ref[group * 8 : group * 8 + 8, 0:LANES]
        partner = sums_ref[(groups + group) * 8 : (groups + group) * 8 + 8, LANES:]
        total = own - partner + back[group * 8 : group * 8 + 8]
        cols = slice(group * LANES, (group + 1) * LANES)
        forces_ref[:, cols] = total[0:3] + total[4:7]
        energy_ref[:, cols] = own[3:4] + own[7:8]


def whole(shape, dtype):
    return jax.ShapeDtypeStruct(shape, dtype)


def call(kernel, outs, name, scratch=(), specs=None, cost=None):
    more = {} if cost is None else dict(cost_estimate=cost)
    return pl.pallas_call(
        kernel,
        grid=(1,),
        in_specs=specs,
        out_specs=tuple(pl.BlockSpec(memory_space=pltpu.VMEM) for _ in outs),
        out_shape=outs,
        scratch_shapes=list(scratch),
        compiler_params=pltpu.CompilerParams(vmem_limit_bytes=VMEM_LIMIT),
        name=name,
        **more,
    )


def shifted(value, offset, sizes, sign):
    used = tuple(axis for axis, step in zip(sizes, offset) if step)
    dims = [size for name, size in used]
    pairs = []
    for flat in range(math.prod(dims)):
        place, rest = [], flat
        for size in reversed(dims):
            place.insert(0, rest % size)
            rest //= size
        target = 0
        for at, size in zip(place, dims):
            target = target * size + (at - sign) % size
        pairs.append((flat, target))
    return lax.ppermute(value, tuple(name for name, size in used), pairs)


def on_device(
    sizes,
    positions,
    features,
    species,
    species_scale,
    w_first,
    w_second,
    w_radial,
    w_mid,
    w_last,
    w_out,
    ghost_send,
    local_first,
    local_second,
    local_mask,
    ghost_owner,
    ghost_index,
    ghost_mask,
):
    channels, own_count = features.shape
    send_count = ghost_send.shape[0]
    bases = w_radial.shape[1]
    rows = channels + EXTRA
    groups = own_count // LANES
    blocks = len(ghost_offsets)
    send = ghost_send.reshape(1, send_count)
    whole_spec = pl.BlockSpec(memory_space=pltpu.VMEM)
    def tiles(value):
        return value.reshape(value.shape[0] // LANES, LANES)

    small = (
        positions,
        features,
        species.reshape(1, own_count),
        species_scale.reshape(1, species_scale.shape[0]),
        w_first,
        w_second,
        w_radial.T,
        w_mid,
        w_last,
        w_out.reshape(1, channels),
    )
    lists = [send] + [tiles(value) for value in (local_first, local_second, local_mask)]
    own, right, offered, mats, radial, radial_t, out, send, *local = call(
        prep_kernel,
        (
            whole((rows, own_count), f32),
            whole((-(-own_count // GROUP * rows // 16) * 16, GROUP), bf16),
            whole((channels + OFFERED, send_count), bf16),
            whole((4 * QUAD * channels, QUAD * channels), bf16),
            whole((QUAD * channels, QUAD * 4 * bases), bf16),
            whole((QUAD * 2 * bases, QUAD * channels), bf16),
            whole((channels, LANES), f32),
            *[whole(value.shape, value.dtype) for value in lists],
        ),
        "tables",
        [pltpu.VMEM(value.shape, value.dtype) for value in small]
        + [pltpu.SemaphoreType.DMA((len(small) + len(lists),))],
        [pl.BlockSpec(memory_space=pltpu.HBM)] * (len(small) + len(lists)),
    )(*[pltpu.with_memory_space_constraint(value, pltpu.HBM) for value in (*small, *lists)])
    arrived = [shifted(offered, offset, sizes, 1) for offset in ghost_offsets]

    def scratch(per_step, hots):
        return [pltpu.VMEM((per_step, GROUP, QUAD * CHUNK), bf16) for _ in range(hots)] + [
            pltpu.VMEM((per_step, QUAD, channels, CHUNK), f32),
            pltpu.VMEM((per_step, QUAD, channels, CHUNK), f32),
            pltpu.VMEM((GROUP, LANES), bf16),
        ]

    def cost(slots):
        return pl.CostEstimate(flops=slots * 400000, bytes_accessed=slots * 12, transcendentals=slots * 200)

    parts = 2
    part_rows = local[0].shape[0] // parts
    weights = (mats, radial, radial_t, out)
    local_step = part_rows * LANES // (QUAD * CHUNK)

    def local_call(part, start):
        operands = [*local, own, right, *weights, *start]
        (sums,) = call(
            functools.partial(
                local_kernel, local_step, channels, bases, part * part_rows, part_rows, len(start)
            ),
            (whole((groups * 16, GROUP), f32),),
            "local_pairs",
            scratch(local_step, 2),
            [whole_spec] * len(operands),
            cost(part_rows * LANES),
        )(*operands)
        return sums

    sums = local_call(0, ())
    ghost_lists = [tiles(value) for value in (ghost_owner, ghost_index, ghost_mask)]
    ghost_step = ghost_owner.shape[0] // (QUAD * CHUNK)
    partner_rows = blocks * GROUP // LANES * 8
    table_rows = -(-blocks * rows // 16) * 16
    sums, *ghost_forces = call(
        functools.partial(ghost_kernel, ghost_step, channels, bases),
        (whole((groups * 16, GROUP), f32),) + (whole((8, send_count), f32),) * blocks,
        "ghost_pairs",
        [pltpu.VMEM((table_rows, GROUP), bf16), pltpu.VMEM((groups * 8 + partner_rows, GROUP), f32)]
        + scratch(ghost_step, 2),
        [whole_spec] * (9 + blocks),
        cost(ghost_owner.shape[0]),
    )(*ghost_lists, own, *weights, sums, *arrived)
    returned = [
        shifted(force, offset, sizes, -1) for force, offset in reversed(list(zip(ghost_forces, ghost_offsets)))
    ]
    sums = local_call(1, (sums,))
    forces, energy = call(
        functools.partial(final_kernel, blocks),
        (whole((3, own_count), f32), whole((1, own_count), f32)),
        "totals",
        specs=[whole_spec] * (2 + blocks),
    )(sums, send, *returned)
    return forces, energy.reshape(own_count)


def solution(mesh):
    names = ("gx", "gy", "gz")
    sizes = tuple((name, mesh.shape[name]) for name in names)
    split = P(names)
    cols = P(None, names)
    in_specs = (cols, cols, split) + (P(),) * 7 + (split,) * 7
    return jax.shard_map(
        functools.partial(on_device, sizes),
        mesh=mesh,
        in_specs=in_specs,
        out_specs=(cols, split),
        check_vma=False,
    )
```

```python
import functools
import math

import jax
import jax.numpy as jnp
from jax import lax
from jax.experimental import pallas as pl
from jax.experimental.pallas import tpu as pltpu
from jax.sharding import PartitionSpec as P

basis_width = 24.0
domain_edge = 1.0
ghost_offsets = ((1, 0, 0), (0, 1, 0), (0, 0, 1), (1, 1, 0), (1, 0, 1), (0, 1, 1), (1, 1, 1))

PLANAR = ((1, 0), (0, 1), (1, 1))
EXTRA = 8
OFFERED = 16
GROUP = 256
LANES = 128
CHUNK = 256
QUAD = 4
VMEM_LIMIT = 48 * 1024 * 1024

NT = (((1,), (1,)), ((), ()))
f32 = jnp.float32
bf16 = jnp.bfloat16


def dot(left, right):
    return jnp.dot(left, right, preferred_element_type=f32)


def dot_nt(left, right):
    return lax.dot_general(left, right, NT, preferred_element_type=f32)


def iota(shape, dim):
    return lax.broadcasted_iota(jnp.int32, shape, dim)


def one_hot(row, codes):
    entry = jnp.broadcast_to(row.astype(f32), (16, row.shape[1])).astype(bf16)
    entry = jnp.concatenate([entry] * (codes.shape[0] // 16), 0)
    pieces = [
        jnp.where(codes == entry[:, start : start + LANES], bf16(1), bf16(0))
        for start in range(0, row.shape[1], LANES)
    ]
    return jnp.concatenate(pieces, 1)


def row_codes(count):
    return iota((count, LANES), 0).astype(f32).astype(bf16)


def split_two(value):
    high = value.astype(bf16).astype(f32)
    return high, value - high


def coord_rows(coords, gain):
    high, low = split_two(coords)
    return jnp.concatenate([high, gain, low, jnp.zeros_like(gain)], 0)


def eye(count):
    return (iota((count, count), 0) == iota((count, count), 1)).astype(bf16)


def fetch(sources, targets, landed):
    copies = [
        pltpu.make_async_copy(source, target, landed.at[place])
        for place, (source, target) in enumerate(zip(sources, targets))
    ]
    for copy in copies:
        copy.start()
    for copy in copies:
        copy.wait()


def tables_kernel(*refs):
    own_ref, right_ref, offered_ref, send_ref = refs[7:11]
    fetch(refs[:7], refs[11:17] + (send_ref,), refs[17])
    positions_ref, features_ref, species_ref, scale_ref, w_first_ref, w_second_ref = refs[11:17]
    channels = features_ref.shape[0]
    count = features_ref.shape[1]
    species = species_ref[...]
    gain = jnp.zeros((1, count), f32)
    for kind in range(scale_ref.shape[1]):
        scale = scale_ref[:, kind : kind + 1].astype(f32)
        gain = jnp.where(species == kind, scale, gain)
    positions = positions_ref[...]
    left = dot(w_first_ref[...], features_ref[...]).astype(bf16).astype(f32)
    right = dot(w_second_ref[...], features_ref[...]).astype(bf16).astype(f32)
    own_ref[0:channels, :] = 0.5 * left
    own_ref[channels:, :] = jnp.concatenate([positions, gain, jnp.zeros((EXTRA - 4, count), f32)], 0)
    column = jnp.concatenate([0.5 * right, coord_rows(positions, gain)], 0)
    groups = count // GROUP
    rows = channels + EXTRA
    table = jnp.concatenate([column[:, group * GROUP : (group + 1) * GROUP] for group in range(groups)], 0)
    spare = right_ref.shape[0] - groups * rows
    if spare:
        table = jnp.concatenate([table, jnp.zeros((spare, GROUP), f32)], 0)
    table = table.astype(bf16)
    right_ref[...] = table
    send = send_ref[...]
    picked = dot(table, one_hot(send & (GROUP - 1), row_codes(GROUP)))
    chosen = group_pick(picked, send // GROUP, rows, groups)
    chosen = jnp.concatenate([chosen, jnp.zeros((OFFERED - EXTRA, chosen.shape[1]), f32)], 0)
    offered_ref[...] = chosen.astype(bf16)


def weights_kernel(*refs):
    mats_ref, radial_ref, radial_t_ref, out_ref = refs[7:11]
    fetch(refs[:7], refs[14:18] + refs[11:14], refs[18])
    radial_w_ref, w_mid_ref, w_last_ref, w_out_ref = refs[14:18]
    channels = w_mid_ref.shape[0]
    unit = eye(channels)
    w_mid = w_mid_ref[...]
    w_last = w_last_ref[...]
    last_t = dot_nt(unit, w_last).astype(bf16)
    mid_t = dot_nt(unit, w_mid).astype(bf16)
    wide = QUAD * channels
    for place, matrix in enumerate((w_mid, w_last, last_t, mid_t)):
        mats_ref[place * wide : (place + 1) * wide, :] = (0.5 * diagonal_copies(matrix)).astype(bf16)
    bases = radial_w_ref.shape[0]
    high, low = split_two(radial_w_ref[...])
    high = high.astype(bf16)
    low = low.astype(bf16)
    spread = dot_nt(unit, jnp.concatenate([high, high, low, low], 0)).astype(bf16)
    radial_ref[...] = (0.5 * diagonal_copies(spread)).astype(bf16)
    radial_t_ref[...] = diagonal_copies(jnp.concatenate([high, low], 0)).astype(bf16)
    w_out = w_out_ref[...]
    diagonal = jnp.where(iota((channels, channels), 0) == iota((channels, channels), 1), w_out, 0.0)
    out_ref[...] = jnp.broadcast_to(jnp.sum(diagonal, axis=1, keepdims=True), (channels, LANES))


def diagonal_copies(matrix):
    high, wide = matrix.shape
    repeat = (iota((wide, QUAD * wide), 0) == iota((wide, QUAD * wide), 1) % wide).astype(bf16)
    row = dot(matrix, repeat)
    full = jnp.concatenate([row] * QUAD, 0)
    return jnp.where(iota(full.shape, 0) // high == iota(full.shape, 1) // wide, full, 0.0)


def group_pick(values, high, rows, groups):
    chosen = values[:rows]
    for group in range(1, groups):
        chosen = jnp.where(high == group, values[group * rows : (group + 1) * rows], chosen)
    return chosen


def spread_groups(values, high, groups):
    twice = jnp.concatenate([values, values], 0)
    second = iota(twice.shape, 0) // 4
    pieces = [jnp.where(high == second + group, twice, 0.0) for group in range(0, groups, 2)]
    return jnp.concatenate(pieces, 0)


def lane_pick(table_ref, row):
    rows, count = table_ref.shape
    lane = jnp.broadcast_to(row & (LANES - 1), (rows, LANES))
    high = row // LANES
    chosen = None
    for group in range(count // LANES):
        part = table_ref[:, group * LANES : (group + 1) * LANES]
        picked = jnp.take_along_axis(part, lane, axis=1, mode="promise_in_bounds")
        chosen = picked if chosen is None else jnp.where(high == group, picked, chosen)
    return chosen


def pair_body(
    per_step,
    first_row,
    row_count,
    own_groups,
    partner_groups,
    channels,
    bases,
    owner_ref,
    partner_ref,
    mask_ref,
    own_ref,
    right_ref,
    mats_ref,
    radial_ref,
    radial_t_ref,
    out_ref,
    sums,
    hot,
    hot_wide,
    slope_one,
    slope_two,
    codes_ref,
):
    rows = channels + EXTRA
    line = CHUNK // LANES
    block = QUAD * line
    wide = QUAD * channels
    steps = row_count // (per_step * block)
    w_out = jnp.concatenate([out_ref[...]] * line, 1)
    centers = iota((bases, CHUNK), 0).astype(f32) * (1.0 / (bases - 1))
    sub = iota((8, CHUNK), 0)
    quads = range(QUAD)
    codes_ref[...] = row_codes(GROUP)

    def matrix(place):
        return mats_ref[place * wide : (place + 1) * wide, :]

    def part(values, number, size=channels):
        return values[number * size : (number + 1) * size]

    def silu_pair(half):
        grow = jnp.tanh(half)
        plus = 1.0 + grow
        hidden = half * plus
        return hidden, plus + hidden * (1.0 - grow)

    def chunk(base, number):
        at = pl.multiple_of(base + number * block, block)
        owner_rows = owner_ref[pl.ds(at, block), :]
        partner_rows = partner_ref[pl.ds(at, block), :]
        live_rows = mask_ref[pl.ds(at, block), :].astype(f32)

        def row_of(values, quad):
            return jnp.concatenate(
                [values[quad * line + piece : quad * line + piece + 1, :] for piece in range(line)], 1
            )

        own_high, partner_high, projected, shifts, squares, weights, stacks, slopes = ([] for _ in range(8))
        for quad in quads:
            cols = slice(quad * CHUNK, (quad + 1) * CHUNK)
            owner = row_of(owner_rows, quad)
            partner = row_of(partner_rows, quad)
            own_high.append(owner // LANES)
            partner_high.append(partner // LANES)
            hot[number, 0:LANES, cols] = one_hot(owner & (LANES - 1), codes_ref[0:LANES, :])
            if hot_wide is None:
                hot[number, LANES:, cols] = one_hot(partner & (LANES - 1), codes_ref[0:LANES, :])
            else:
                both = one_hot(partner & (GROUP - 1), codes_ref[...])
                hot_wide[number, :, cols] = both
                hot[number, LANES:, cols] = both[0:LANES] + both[LANES:]
            yield
        for quad in quads:
            cols = slice(quad * CHUNK, (quad + 1) * CHUNK)
            pieces = []
            for piece in range(line):
                at_row = quad * line + piece
                pieces.append(lane_pick(own_ref, owner_rows[at_row : at_row + 1, :]))
            own_vals = jnp.concatenate(pieces, 1)
            if hot_wide is None:
                pieces = []
                for piece in range(line):
                    at_row = quad * line + piece
                    pieces.append(lane_pick(right_ref, partner_rows[at_row : at_row + 1, :]))
                partner_vals = jnp.concatenate(pieces, 1)
                partner_coords = partner_vals[channels:]
            else:
                wide_high = row_of(partner_rows, quad) // GROUP
                partner_vals = group_pick(
                    dot(right_ref[...], hot_wide[number, :, cols]), wide_high, rows, partner_groups * LANES // GROUP
                )
                extra = partner_vals[channels:]
                partner_coords = extra + jnp.concatenate([extra[4:], extra[:4]], 0)
            projected.append(own_vals[:channels] + partner_vals[:channels])
            own_coords = own_vals[channels:]
            shift = partner_coords - own_coords
            square = shift * shift
            squared = square[0:1] + square[1:2] + square[2:3]
            weights.append(row_of(live_rows, quad) * own_coords[3:4] * partner_coords[3:4])
            away = squared - centers
            basis = jnp.exp(-basis_width * (away * away))
            basis_high, basis_low = split_two(basis)
            stacks.append(jnp.concatenate([basis_high, basis_low, basis_high, basis_low], 0).astype(bf16))
            slopes.append((-2.0 * basis_width) * away * basis)
            shifts.append(shift)
            squares.append(squared)
            yield
        radial = dot(radial_ref[...], jnp.concatenate(stacks, 0))
        yield
        pieces = []
        for quad in quads:
            hidden, slope_one[number, quad] = silu_pair(projected[quad] + part(radial, quad))
            pieces.append(hidden.astype(bf16))
        yield
        half = dot(matrix(0), jnp.concatenate(pieces, 0))
        yield
        pieces = []
        for quad in quads:
            hidden, slope_two[number, quad] = silu_pair(part(half, quad))
            pieces.append(hidden.astype(bf16))
        yield
        half = dot(matrix(1), jnp.concatenate(pieces, 0))
        yield
        pieces = []
        readouts = []
        for quad in quads:
            hidden, slope = silu_pair(part(half, quad))
            readouts.append(jnp.sum(w_out * hidden, axis=0, keepdims=True))
            pieces.append(((0.5 * w_out) * slope).astype(bf16))
        yield
        back = dot(matrix(2), jnp.concatenate(pieces, 0))
        yield
        pieces = [(part(back, quad) * slope_two[number, quad]).astype(bf16) for quad in quads]
        back = dot(matrix(3), jnp.concatenate(pieces, 0))
        yield
        pieces = [(part(back, quad) * slope_one[number, quad]).astype(bf16) for quad in quads]
        back = dot(radial_t_ref[...], jnp.concatenate(pieces, 0))
        yield
        parts = []
        for quad in quads:
            two = part(back, quad, 2 * bases)
            readout_slope = jnp.sum((two[:bases] + two[bases:]) * slopes[quad], axis=0, keepdims=True)
            near = jnp.maximum(1.0 - squares[quad], 0.0)
            weight_near = weights[quad] * near
            energy = weight_near * near * readouts[quad]
            slope = weight_near * (near * readout_slope - 2.0 * readouts[quad])
            push = (2.0 * slope) * shifts[quad]
            values = jnp.where(sub == 3, energy, push)[:4]
            parts.append(
                jnp.concatenate(
                    [
                        spread_groups(values, own_high[quad], own_groups),
                        spread_groups(values, partner_high[quad], partner_groups),
                    ],
                    0,
                ).astype(bf16)
            )
        yield
        sums[...] += dot_nt(jnp.concatenate(parts, 1), hot[number])

    def step(index, unused):
        base = pl.multiple_of(first_row + index * (per_step * block), block)
        running = []
        waiting = [chunk(base, number) for number in range(per_step)]
        while running or waiting:
            if waiting:
                running.append(waiting.pop(0))
            for _ in range(2):
                running = [task for task in running if next(task, task) is not task]
        return unused

    lax.fori_loop(0, steps, step, 0)


def local_kernel(per_step, channels, bases, first_row, row_count, with_start, *refs):
    count = 10 + with_start
    owner, partner, mask, own, right, *weights = refs[:9]
    sums, hot, *scratch = refs[count:]
    sums[...] = refs[9][...] if with_start else jnp.zeros_like(sums)
    groups = own.shape[1] // LANES
    pair_body(
        per_step,
        first_row,
        row_count,
        groups,
        groups,
        channels,
        bases,
        owner,
        partner,
        mask,
        own,
        right,
        *weights,
        sums,
        hot,
        *scratch,
    )


def ghost_kernel(per_step, channels, bases, *refs):
    blocks = len(ghost_offsets)
    owner, partner, mask, own, *weights = refs[:8]
    sums_in = refs[8]
    arrived = refs[9 : 10 + len(PLANAR)]
    sums_out, upward, *level = refs[10 + len(PLANAR) : 12 + 2 * len(PLANAR)]
    table, sums, *scratch = refs[12 + 2 * len(PLANAR) :]
    groups = own.shape[1] // LANES
    partner_groups = blocks * GROUP // LANES
    sums[...] = jnp.zeros_like(sums)
    pieces = []
    for offset in ghost_offsets:
        if offset[:2] == (0, 0):
            source, start = arrived[0], 0
        else:
            source, start = arrived[1 + PLANAR.index(offset[:2])], offset[2] * (channels + OFFERED)
        extra = source[start + channels : start + channels + OFFERED, :].astype(f32)
        moved = jnp.concatenate(
            [extra[axis : axis + 1] + extra[axis + 4 : axis + 5] + domain_edge * offset[axis] for axis in range(3)], 0
        )
        pieces += [source[start : start + channels, :].astype(f32), coord_rows(moved, extra[3:4])]
    pieces.append(jnp.zeros((table.shape[0] - blocks * (channels + EXTRA), GROUP), f32))
    table[...] = jnp.concatenate(pieces, 0).astype(bf16)
    pair_body(
        per_step,
        0,
        owner.shape[0],
        groups,
        partner_groups,
        channels,
        bases,
        owner,
        partner,
        mask,
        own,
        table,
        *weights,
        sums,
        *scratch,
    )
    first = groups * 4
    sums_out[0:first, :] = sums_in[0:first, :] + sums[0:first, :]
    sums_out[first:, :] = sums_in[first:, :]
    for block, offset in enumerate(ghost_offsets):
        halves = []
        for half in range(GROUP // LANES):
            start = first + (block * (GROUP // LANES) + half) * 4
            halves.append(sums[start : start + 4, LANES:])
        force = -jnp.concatenate(halves, 1)
        force = jnp.concatenate([force, jnp.zeros_like(force)], 0)
        if offset[2]:
            place = 0 if offset[:2] == (0, 0) else 1 + PLANAR.index(offset[:2])
            upward[place * 8 : place * 8 + 8, :] = force
        else:
            level[PLANAR.index(offset[:2])][...] = force


def pair_kernel(offered_ref, from_z_ref, both_ref):
    count = offered_ref.shape[0]
    both_ref[0:count, :] = offered_ref[...]
    both_ref[count:, :] = from_z_ref[...]


def merge_kernel(*refs):
    upward, *level = refs[: 1 + len(PLANAR)]
    outs = refs[1 + len(PLANAR) :]
    outs[0][...] = upward[0:8, :]
    for place, part in enumerate(level):
        outs[1 + place][...] = part[...] + upward[8 * place + 8 : 8 * place + 16, :]


def final_kernel(*refs):
    sums_ref, send_ref, *arrived = refs[:-2]
    forces_ref, energy_ref = refs[-2:]
    incoming = arrived[0][...]
    for part in arrived[1:]:
        incoming = incoming + part[...]
    high, low = split_two(incoming[:4])
    send = send_ref[...]
    groups = sums_ref.shape[0] // 8
    hot = one_hot(send & (LANES - 1), row_codes(LANES))
    spread = [spread_groups(value, send // LANES, groups).astype(bf16) for value in (high, low)]
    back = dot_nt(jnp.concatenate(spread, 0), hot)
    back = back[: groups * 4] + back[groups * 4 :]
    for group in range(groups):
        own = sums_ref[group * 4 : group * 4 + 4, 0:LANES]
        partner = sums_ref[(groups + group) * 4 : (groups + group) * 4 + 4, LANES:]
        total = own - partner + back[group * 4 : group * 4 + 4]
        cols = slice(group * LANES, (group + 1) * LANES)
        forces_ref[:, cols] = total[0:3]
        energy_ref[:, cols] = own[3:4]


def whole(shape, dtype):
    return jax.ShapeDtypeStruct(shape, dtype)


def call(kernel, outs, name, scratch=(), specs=None, cost=None):
    more = {} if cost is None else dict(cost_estimate=cost)
    return pl.pallas_call(
        kernel,
        grid=(1,),
        in_specs=specs,
        out_specs=tuple(pl.BlockSpec(memory_space=pltpu.VMEM) for _ in outs),
        out_shape=outs,
        scratch_shapes=list(scratch),
        compiler_params=pltpu.CompilerParams(vmem_limit_bytes=VMEM_LIMIT),
        name=name,
        **more,
    )


def shifted(value, offset, sizes, sign):
    used = tuple(axis for axis, step in zip(sizes, offset) if step)
    dims = [size for name, size in used]
    pairs = []
    for flat in range(math.prod(dims)):
        place, rest = [], flat
        for size in reversed(dims):
            place.insert(0, rest % size)
            rest //= size
        target = 0
        for at, size in zip(place, dims):
            target = target * size + (at - sign) % size
        pairs.append((flat, target))
    return lax.ppermute(value, tuple(name for name, size in used), pairs)


def on_device(
    sizes,
    positions,
    features,
    species,
    species_scale,
    w_first,
    w_second,
    w_radial,
    w_mid,
    w_last,
    w_out,
    ghost_send,
    local_first,
    local_second,
    local_mask,
    ghost_owner,
    ghost_index,
    ghost_mask,
):
    channels, own_count = features.shape
    send_count = ghost_send.shape[0]
    bases = w_radial.shape[1]
    rows = channels + EXTRA
    groups = own_count // LANES
    blocks = len(ghost_offsets)
    whole_spec = pl.BlockSpec(memory_space=pltpu.VMEM)
    def tiles(value):
        return value.reshape(value.shape[0] // LANES, LANES)

    def fetching(kernel, name, outs, operands, kept):
        here = [pltpu.with_memory_space_constraint(value, pltpu.HBM) for value in operands]
        landing = operands[: len(operands) - kept]
        return call(
            kernel,
            outs + tuple(whole(value.shape, value.dtype) for value in operands[len(landing) :]),
            name,
            [pltpu.VMEM(value.shape, value.dtype) for value in landing]
            + [pltpu.SemaphoreType.DMA((len(operands),))],
            [pl.BlockSpec(memory_space=pltpu.HBM)] * len(operands),
        )(*here)

    own, right, offered, send = fetching(
        tables_kernel,
        "tables",
        (
            whole((rows, own_count), f32),
            whole((-(-own_count // GROUP * rows // 16) * 16, GROUP), bf16),
            whole((channels + OFFERED, send_count), bf16),
        ),
        (
            positions,
            features,
            species.reshape(1, own_count),
            species_scale.reshape(1, species_scale.shape[0]),
            w_first,
            w_second,
            ghost_send.reshape(1, send_count),
        ),
        1,
    )
    from_z = shifted(offered, (0, 0, 1), sizes, 1)
    *weights, local_first, local_second, local_mask = fetching(
        weights_kernel,
        "weights",
        (
            whole((4 * QUAD * channels, QUAD * channels), bf16),
            whole((QUAD * channels, QUAD * 4 * bases), bf16),
            whole((QUAD * 2 * bases, QUAD * channels), bf16),
            whole((channels, LANES), f32),
        ),
        (
            w_radial.T,
            w_mid,
            w_last,
            w_out.reshape(1, channels),
            tiles(local_first),
            tiles(local_second),
            tiles(local_mask),
        ),
        3,
    )
    local = (local_first, local_second, local_mask)
    (both,) = call(
        pair_kernel, (whole((2 * offered.shape[0], send_count), bf16),), "two_blocks", specs=[whole_spec] * 2
    )(offered, from_z)
    arrived = [from_z] + [shifted(both, (*step, 0), sizes, 1) for step in PLANAR]

    def scratch(per_step, hots):
        return [pltpu.VMEM((per_step, GROUP, QUAD * CHUNK), bf16) for _ in range(hots)] + [
            pltpu.VMEM((per_step, QUAD, channels, CHUNK), f32),
            pltpu.VMEM((per_step, QUAD, channels, CHUNK), f32),
            pltpu.VMEM((GROUP, LANES), bf16),
        ]

    def cost(slots):
        return pl.CostEstimate(flops=slots * 400000, bytes_accessed=slots * 12, transcendentals=slots * 200)

    parts = 2
    part_rows = local[0].shape[0] // parts
    local_step = part_rows * LANES // (QUAD * CHUNK)

    def local_call(part, start, after):
        operands = [*local, own, right, *weights, *start, after]
        (sums,) = call(
            functools.partial(
                local_kernel, local_step, channels, bases, part * part_rows, part_rows, len(start)
            ),
            (whole((groups * 8, GROUP), f32),),
            "local_pairs",
            scratch(local_step, 2),
            [whole_spec] * len(operands),
            cost(part_rows * LANES),
        )(*operands)
        return sums

    sums = local_call(0, (), both)
    ghost_lists = [tiles(value) for value in (ghost_owner, ghost_index, ghost_mask)]
    ghost_step = ghost_owner.shape[0] // (QUAD * CHUNK)
    partner_rows = blocks * GROUP // LANES * 4
    table_rows = -(-blocks * rows // 16) * 16
    force = whole((8, send_count), f32)
    sums, upward, *level = call(
        functools.partial(ghost_kernel, ghost_step, channels, bases),
        (whole((groups * 8, GROUP), f32), whole((8 + 8 * len(PLANAR), send_count), f32)) + (force,) * len(PLANAR),
        "ghost_pairs",
        [pltpu.VMEM((table_rows, GROUP), bf16), pltpu.VMEM((groups * 4 + partner_rows, GROUP), f32)]
        + scratch(ghost_step, 2),
        [whole_spec] * (9 + len(arrived)),
        cost(ghost_owner.shape[0]),
    )(*ghost_lists, own, *weights, sums, *arrived)
    upward = shifted(upward, (0, 0, 1), sizes, -1)
    mine, *level = call(
        merge_kernel, (force,) * (1 + len(PLANAR)), "forces_upward", specs=[whole_spec] * (1 + len(PLANAR))
    )(upward, *level)
    returned = [shifted(part, (*step, 0), sizes, -1) for part, step in zip(level, PLANAR)]
    sums = local_call(1, (sums,), mine)
    forces, energy = call(
        final_kernel,
        (whole((3, own_count), f32), whole((1, own_count), f32)),
        "totals",
        specs=[whole_spec] * (3 + len(returned)),
    )(sums, send, mine, *returned)
    return forces, energy.reshape(own_count)


def solution(mesh):
    names = ("gx", "gy", "gz")
    sizes = tuple((name, mesh.shape[name]) for name in names)
    split = P(names)
    cols = P(None, names)
    in_specs = (cols, cols, split) + (P(),) * 7 + (split,) * 7
    return jax.shard_map(
        functools.partial(on_device, sizes),
        mesh=mesh,
        in_specs=in_specs,
        out_specs=(cols, split),
        check_vma=False,
    )
```

```python
import functools
import math

import jax
import jax.numpy as jnp
from jax import lax
from jax.experimental import pallas as pl
from jax.experimental.pallas import tpu as pltpu
from jax.sharding import PartitionSpec as P

basis_width = 24.0
domain_edge = 1.0
ghost_offsets = ((1, 0, 0), (0, 1, 0), (0, 0, 1), (1, 1, 0), (1, 0, 1), (0, 1, 1), (1, 1, 1))

PLANAR = ((1, 0), (0, 1), (1, 1))
EXTRA = 8
OFFERED = 16
GROUP = 256
LANES = 128
CHUNK = 256
QUAD = 4
VMEM_LIMIT = 48 * 1024 * 1024

NT = (((1,), (1,)), ((), ()))
f32 = jnp.float32
bf16 = jnp.bfloat16


def dot(left, right):
    return jnp.dot(left, right, preferred_element_type=f32)


def dot_nt(left, right):
    return lax.dot_general(left, right, NT, preferred_element_type=f32)


def iota(shape, dim):
    return lax.broadcasted_iota(jnp.int32, shape, dim)


def one_hot(entry, codes):
    entry = entry.astype(f32)
    entry = jnp.concatenate([entry, entry], 0).astype(bf16)
    entry = jnp.concatenate([entry] * (codes.shape[0] // 16), 0)
    pieces = [
        jnp.where(codes == entry[:, start : start + LANES], bf16(1), bf16(0))
        for start in range(0, entry.shape[1], LANES)
    ]
    return jnp.concatenate(pieces, 1)


def row_codes(count):
    return iota((count, LANES), 0).astype(f32).astype(bf16)


def split_two(value):
    high = value.astype(bf16).astype(f32)
    return high, value - high


def coord_rows(coords, gain):
    high, low = split_two(coords)
    return jnp.concatenate([high, gain, low, jnp.zeros_like(gain)], 0)


def eye(count):
    return (iota((count, count), 0) == iota((count, count), 1)).astype(bf16)


def fetch(sources, targets, landed):
    copies = [
        pltpu.make_async_copy(source, target, landed.at[place])
        for place, (source, target) in enumerate(zip(sources, targets))
    ]
    for copy in copies:
        copy.start()
    for copy in copies:
        copy.wait()


def tables_kernel(*refs):
    own_ref, right_ref, offered_ref, send_ref = refs[7:11]
    fetch(refs[:7], refs[11:17] + (send_ref,), refs[17])
    positions_ref, features_ref, species_ref, scale_ref, w_first_ref, w_second_ref = refs[11:17]
    channels = features_ref.shape[0]
    count = features_ref.shape[1]
    species = species_ref[...]
    gain = jnp.zeros((1, count), f32)
    for kind in range(scale_ref.shape[1]):
        scale = scale_ref[:, kind : kind + 1].astype(f32)
        gain = jnp.where(species == kind, scale, gain)
    positions = positions_ref[...]
    left = dot(w_first_ref[...], features_ref[...]).astype(bf16).astype(f32)
    right = dot(w_second_ref[...], features_ref[...]).astype(bf16).astype(f32)
    own_ref[0:channels, :] = 0.5 * left
    own_ref[channels:, :] = jnp.concatenate([positions, gain, positions, gain], 0)
    column = jnp.concatenate([0.5 * right, coord_rows(positions, gain)], 0)
    groups = count // GROUP
    rows = channels + EXTRA
    table = jnp.concatenate([column[:, group * GROUP : (group + 1) * GROUP] for group in range(groups)], 0)
    spare = right_ref.shape[0] - groups * rows
    if spare:
        table = jnp.concatenate([table, jnp.zeros((spare, GROUP), f32)], 0)
    table = table.astype(bf16)
    right_ref[...] = table
    send = jnp.broadcast_to(send_ref[...], (8, send_ref.shape[1]))
    picked = dot(table, one_hot(send & (GROUP - 1), row_codes(GROUP)))
    chosen = group_pick(picked, send // GROUP, rows, groups)
    chosen = jnp.concatenate([chosen, jnp.zeros((OFFERED - EXTRA, chosen.shape[1]), f32)], 0)
    offered_ref[...] = chosen.astype(bf16)


def weights_kernel(*refs):
    mats_ref, radial_ref, radial_t_ref, out_ref = refs[7:11]
    fetch(refs[:7], refs[14:18] + refs[11:14], refs[18])
    radial_w_ref, w_mid_ref, w_last_ref, w_out_ref = refs[14:18]
    channels = w_mid_ref.shape[0]
    unit = eye(channels)
    w_mid = w_mid_ref[...]
    w_last = w_last_ref[...]
    last_t = dot_nt(unit, w_last).astype(bf16)
    mid_t = dot_nt(unit, w_mid).astype(bf16)
    wide = QUAD * channels
    for place, matrix in enumerate((w_mid, w_last, last_t, mid_t)):
        mats_ref[place * wide : (place + 1) * wide, :] = (0.5 * diagonal_copies(matrix)).astype(bf16)
    bases = radial_w_ref.shape[0]
    high, low = split_two(radial_w_ref[...])
    high = high.astype(bf16)
    low = low.astype(bf16)
    spread = dot_nt(unit, jnp.concatenate([high, high, low, low], 0)).astype(bf16)
    radial_ref[...] = (0.5 * diagonal_copies(spread)).astype(bf16)
    radial_t_ref[...] = diagonal_copies(jnp.concatenate([high, low], 0)).astype(bf16)
    w_out = w_out_ref[...]
    diagonal = jnp.where(iota((channels, channels), 0) == iota((channels, channels), 1), w_out, 0.0)
    out_ref[...] = jnp.broadcast_to(jnp.sum(diagonal, axis=1, keepdims=True), (channels, LANES))


def diagonal_copies(matrix):
    high, wide = matrix.shape
    repeat = (iota((wide, QUAD * wide), 0) == iota((wide, QUAD * wide), 1) % wide).astype(bf16)
    row = dot(matrix, repeat)
    full = jnp.concatenate([row] * QUAD, 0)
    return jnp.where(iota(full.shape, 0) // high == iota(full.shape, 1) // wide, full, 0.0)


def group_pick(values, high, rows, groups):
    high = jnp.concatenate([high] * (rows // 8), 0)
    chosen = values[:rows]
    for group in range(1, groups):
        chosen = jnp.where(high == group, values[group * rows : (group + 1) * rows], chosen)
    return chosen


def spread_groups(values, high, groups):
    second = iota(values.shape, 0) // 4
    pieces = [jnp.where(high == second + group, values, 0.0) for group in range(0, groups, 2)]
    return jnp.concatenate(pieces, 0)


def lane_pick(table_ref, place):
    rows, count = table_ref.shape
    lane = jnp.concatenate([place & (LANES - 1)] * (rows // 8), 0)
    high = jnp.concatenate([place // LANES] * (rows // 8), 0)
    chosen = None
    for group in range(count // LANES):
        part = table_ref[:, group * LANES : (group + 1) * LANES]
        picked = jnp.take_along_axis(part, lane, axis=1, mode="promise_in_bounds")
        chosen = picked if chosen is None else jnp.where(high == group, picked, chosen)
    return chosen


def sum_rows(values, steps):
    for step in steps:
        values = values + pltpu.roll(values, step, 0)
    return values


def pair_body(
    per_step,
    first_row,
    row_count,
    own_groups,
    partner_groups,
    channels,
    bases,
    owner_ref,
    partner_ref,
    mask_ref,
    own_ref,
    right_ref,
    mats_ref,
    radial_ref,
    radial_t_ref,
    out_ref,
    sums,
    hot,
    hot_wide,
    slope_one,
    slope_two,
    codes_ref,
):
    rows = channels + EXTRA
    line = CHUNK // LANES
    block = QUAD * line
    wide = QUAD * channels
    steps = row_count // (per_step * block)
    w_out = jnp.concatenate([out_ref[...]] * line, 1)
    centers = iota((bases, CHUNK), 0).astype(f32) * (1.0 / (bases - 1))
    last = iota((8, CHUNK), 0) % 4 == 3
    partner_bits = (partner_groups * LANES - 1).bit_length()
    quads = range(QUAD)
    codes_ref[...] = row_codes(GROUP)

    def matrix(place):
        return mats_ref[place * wide : (place + 1) * wide, :]

    def part(values, number, size=channels):
        return values[number * size : (number + 1) * size]

    def silu_pair(half):
        grow = jnp.tanh(half)
        plus = 1.0 + grow
        hidden = half * plus
        return hidden, plus + hidden * (1.0 - grow)

    def chunk(base, number):
        at = pl.multiple_of(base + number * block, block)
        code_rows = owner_ref[pl.ds(at, block), :] * 2**partner_bits + partner_ref[pl.ds(at, block), :]
        code_rows = code_rows * 2 + mask_ref[pl.ds(at, block), :]
        owners, partners, lives, projected, shifts, squares, weights, stacks, slopes = ([] for _ in range(9))
        for quad in quads:
            cols = slice(quad * CHUNK, (quad + 1) * CHUNK)
            code = jnp.concatenate(
                [
                    jnp.broadcast_to(code_rows[row : row + 1, :], (8, LANES))
                    for row in range(quad * line, (quad + 1) * line)
                ],
                1,
            )
            lives.append((code & 1).astype(f32))
            partner = (code >> 1) & (2**partner_bits - 1)
            owner = code >> (partner_bits + 1)
            owners.append(owner)
            partners.append(partner)
            hot[number, 0:LANES, cols] = one_hot(owner & (LANES - 1), codes_ref[0:LANES, :])
            wide = one_hot(partner & (GROUP - 1), codes_ref[...])
            hot_wide[number, :, cols] = wide
            hot[number, LANES:, cols] = wide[0:LANES] + wide[LANES:]
            yield
        for quad in quads:
            cols = slice(quad * CHUNK, (quad + 1) * CHUNK)
            own_vals = jnp.concatenate(
                [lane_pick(own_ref, owners[quad][:, start : start + LANES]) for start in range(0, CHUNK, LANES)], 1
            )
            partner_vals = group_pick(
                dot(right_ref[...], hot_wide[number, :, cols]),
                partners[quad] // GROUP,
                rows,
                partner_groups * LANES // GROUP,
            )
            projected.append(own_vals[:channels] + partner_vals[:channels])
            own_coords = own_vals[channels:]
            extra = partner_vals[channels:]
            partner_coords = extra + pltpu.roll(extra, 4, 0)
            shift = partner_coords - own_coords
            squared = sum_rows(jnp.where(last, 0.0, shift * shift), (2, 1))
            gain = sum_rows(jnp.where(last, own_coords * partner_coords, 0.0), (2, 1))
            weights.append(lives[quad] * gain)
            away = squared - centers
            basis = jnp.exp(-basis_width * (away * away))
            basis_high, basis_low = split_two(basis)
            stacks.append(jnp.concatenate([basis_high, basis_low, basis_high, basis_low], 0).astype(bf16))
            slopes.append((-2.0 * basis_width) * away * basis)
            shifts.append(shift)
            squares.append(squared)
            yield
        radial = dot(radial_ref[...], jnp.concatenate(stacks, 0))
        yield
        pieces = []
        for quad in quads:
            hidden, slope_one[number, quad] = silu_pair(projected[quad] + part(radial, quad))
            pieces.append(hidden.astype(bf16))
        yield
        half = dot(matrix(0), jnp.concatenate(pieces, 0))
        yield
        pieces = []
        for quad in quads:
            hidden, slope_two[number, quad] = silu_pair(part(half, quad))
            pieces.append(hidden.astype(bf16))
        yield
        half = dot(matrix(1), jnp.concatenate(pieces, 0))
        yield
        pieces = []
        readouts = []
        for quad in quads:
            hidden, slope = silu_pair(part(half, quad))
            terms = w_out * hidden
            terms = sum(terms[start : start + 8] for start in range(8, channels, 8)) + terms[:8]
            readouts.append(sum_rows(terms, (4, 2, 1)))
            pieces.append(((0.5 * w_out) * slope).astype(bf16))
        yield
        back = dot(matrix(2), jnp.concatenate(pieces, 0))
        yield
        pieces = [(part(back, quad) * slope_two[number, quad]).astype(bf16) for quad in quads]
        back = dot(matrix(3), jnp.concatenate(pieces, 0))
        yield
        pieces = [(part(back, quad) * slope_one[number, quad]).astype(bf16) for quad in quads]
        back = dot(radial_t_ref[...], jnp.concatenate(pieces, 0))
        yield
        parts = []
        for quad in quads:
            two = part(back, quad, 2 * bases)
            readout_slope = sum_rows((two[:bases] + two[bases:]) * slopes[quad], (4, 2, 1))
            near = jnp.maximum(1.0 - squares[quad], 0.0)
            weight_near = weights[quad] * near
            energy = weight_near * near * readouts[quad]
            slope = weight_near * (near * readout_slope - 2.0 * readouts[quad])
            push = (2.0 * slope) * shifts[quad]
            values = jnp.where(last, energy, push)
            parts.append(
                jnp.concatenate(
                    [
                        spread_groups(values, owners[quad] // LANES, own_groups),
                        spread_groups(values, partners[quad] // LANES, partner_groups),
                    ],
                    0,
                ).astype(bf16)
            )
        yield
        sums[...] += dot_nt(jnp.concatenate(parts, 1), hot[number])

    def step(index, unused):
        base = pl.multiple_of(first_row + index * (per_step * block), block)
        running = []
        waiting = [chunk(base, number) for number in range(per_step)]
        while running or waiting:
            if waiting:
                running.append(waiting.pop(0))
            for _ in range(2):
                running = [task for task in running if next(task, task) is not task]
        return unused

    lax.fori_loop(0, steps, step, 0)


def local_kernel(per_step, channels, bases, first_row, row_count, counts, *refs):
    count = 9 + sum(counts)
    owner, partner, mask, own, right, *weights = refs[:9]
    sums, hot, *scratch = refs[count:]
    sums[...] = refs[9][...] if counts[0] else jnp.zeros_like(sums)
    groups = own.shape[1] // LANES
    pair_body(
        per_step,
        first_row,
        row_count,
        groups,
        groups,
        channels,
        bases,
        owner,
        partner,
        mask,
        own,
        right,
        *weights,
        sums,
        hot,
        *scratch,
    )


def ghost_kernel(per_step, channels, bases, *refs):
    blocks = len(ghost_offsets)
    owner, partner, mask, own, *weights = refs[:8]
    sums_in = refs[8]
    arrived = refs[9 : 10 + len(PLANAR)]
    sums_out, upward, *level = refs[10 + len(PLANAR) : 12 + 2 * len(PLANAR)]
    table, sums, *scratch = refs[12 + 2 * len(PLANAR) :]
    groups = own.shape[1] // LANES
    partner_groups = blocks * GROUP // LANES
    sums[...] = jnp.zeros_like(sums)
    pieces = []
    for offset in ghost_offsets:
        if offset[:2] == (0, 0):
            source, start = arrived[0], 0
        else:
            source, start = arrived[1 + PLANAR.index(offset[:2])], offset[2] * (channels + OFFERED)
        extra = source[start + channels : start + channels + OFFERED, :].astype(f32)
        moved = jnp.concatenate(
            [extra[axis : axis + 1] + extra[axis + 4 : axis + 5] + domain_edge * offset[axis] for axis in range(3)], 0
        )
        pieces += [source[start : start + channels, :].astype(f32), coord_rows(moved, extra[3:4])]
    pieces.append(jnp.zeros((table.shape[0] - blocks * (channels + EXTRA), GROUP), f32))
    table[...] = jnp.concatenate(pieces, 0).astype(bf16)
    pair_body(
        per_step,
        0,
        owner.shape[0],
        groups,
        partner_groups,
        channels,
        bases,
        owner,
        partner,
        mask,
        own,
        table,
        *weights,
        sums,
        *scratch,
    )
    first = groups * 4
    sums_out[0:first, :] = sums_in[0:first, :] + sums[0:first, :]
    sums_out[first:, :] = sums_in[first:, :]
    for block, offset in enumerate(ghost_offsets):
        halves = []
        for half in range(GROUP // LANES):
            start = first + (block * (GROUP // LANES) + half) * 4
            halves.append(sums[start : start + 4, LANES:])
        force = -jnp.concatenate(halves, 1)
        force = jnp.concatenate([force, jnp.zeros_like(force)], 0)
        if offset[2]:
            place = 0 if offset[:2] == (0, 0) else 1 + PLANAR.index(offset[:2])
            upward[place * 8 : place * 8 + 8, :] = force
        else:
            level[PLANAR.index(offset[:2])][...] = force


def pair_kernel(offered_ref, from_z_ref, unused_ref, both_ref):
    count = offered_ref.shape[0]
    both_ref[0:count, :] = offered_ref[...]
    both_ref[count:, :] = from_z_ref[...]


def merge_kernel(*refs):
    upward, *level = refs[: 1 + len(PLANAR)]
    outs = refs[2 + len(PLANAR) :]
    outs[0][...] = upward[0:8, :]
    for place, part in enumerate(level):
        outs[1 + place][...] = part[...] + upward[8 * place + 8 : 8 * place + 16, :]


def final_kernel(*refs):
    sums_ref, send_ref, *arrived = refs[:-2]
    forces_ref, energy_ref = refs[-2:]
    incoming = arrived[0][...]
    for part in arrived[1:]:
        incoming = incoming + part[...]
    high, low = split_two(jnp.concatenate([incoming[:4], incoming[:4]], 0))
    send = jnp.broadcast_to(send_ref[...], (8, send_ref.shape[1]))
    groups = sums_ref.shape[0] // 8
    hot = one_hot(send & (LANES - 1), row_codes(LANES))
    spread = [spread_groups(value, send // LANES, groups).astype(bf16) for value in (high, low)]
    back = dot_nt(jnp.concatenate(spread, 0), hot)
    back = back[: groups * 4] + back[groups * 4 :]
    for group in range(groups):
        own = sums_ref[group * 4 : group * 4 + 4, 0:LANES]
        partner = sums_ref[(groups + group) * 4 : (groups + group) * 4 + 4, LANES:]
        total = own - partner + back[group * 4 : group * 4 + 4]
        cols = slice(group * LANES, (group + 1) * LANES)
        forces_ref[:, cols] = total[0:3]
        energy_ref[:, cols] = own[3:4]


def whole(shape, dtype):
    return jax.ShapeDtypeStruct(shape, dtype)


def call(kernel, outs, name, scratch=(), specs=None, cost=None):
    more = {} if cost is None else dict(cost_estimate=cost)
    return pl.pallas_call(
        kernel,
        grid=(1,),
        in_specs=specs,
        out_specs=tuple(pl.BlockSpec(memory_space=pltpu.VMEM) for _ in outs),
        out_shape=outs,
        scratch_shapes=list(scratch),
        compiler_params=pltpu.CompilerParams(vmem_limit_bytes=VMEM_LIMIT),
        name=name,
        **more,
    )


def shifted(value, offset, sizes, sign):
    used = tuple(axis for axis, step in zip(sizes, offset) if step)
    dims = [size for name, size in used]
    pairs = []
    for flat in range(math.prod(dims)):
        place, rest = [], flat
        for size in reversed(dims):
            place.insert(0, rest % size)
            rest //= size
        target = 0
        for at, size in zip(place, dims):
            target = target * size + (at - sign) % size
        pairs.append((flat, target))
    return lax.ppermute(value, tuple(name for name, size in used), pairs)


def on_device(
    sizes,
    positions,
    features,
    species,
    species_scale,
    w_first,
    w_second,
    w_radial,
    w_mid,
    w_last,
    w_out,
    ghost_send,
    local_first,
    local_second,
    local_mask,
    ghost_owner,
    ghost_index,
    ghost_mask,
):
    channels, own_count = features.shape
    send_count = ghost_send.shape[0]
    bases = w_radial.shape[1]
    rows = channels + EXTRA
    groups = own_count // LANES
    blocks = len(ghost_offsets)
    whole_spec = pl.BlockSpec(memory_space=pltpu.VMEM)
    def tiles(value):
        return value.reshape(value.shape[0] // LANES, LANES)

    def fetching(kernel, name, outs, operands, kept):
        here = [pltpu.with_memory_space_constraint(value, pltpu.HBM) for value in operands]
        landing = operands[: len(operands) - kept]
        return call(
            kernel,
            outs + tuple(whole(value.shape, value.dtype) for value in operands[len(landing) :]),
            name,
            [pltpu.VMEM(value.shape, value.dtype) for value in landing]
            + [pltpu.SemaphoreType.DMA((len(operands),))],
            [pl.BlockSpec(memory_space=pltpu.HBM)] * len(operands),
        )(*here)

    own, right, offered, send = fetching(
        tables_kernel,
        "tables",
        (
            whole((rows, own_count), f32),
            whole((-(-own_count // GROUP * rows // 16) * 16, GROUP), bf16),
            whole((channels + OFFERED, send_count), bf16),
        ),
        (
            positions,
            features,
            species.reshape(1, own_count),
            species_scale.reshape(1, species_scale.shape[0]),
            w_first,
            w_second,
            ghost_send.reshape(1, send_count),
        ),
        1,
    )
    from_z = shifted(offered, (0, 0, 1), sizes, 1)
    *weights, local_first, local_second, local_mask = fetching(
        weights_kernel,
        "weights",
        (
            whole((4 * QUAD * channels, QUAD * channels), bf16),
            whole((QUAD * channels, QUAD * 4 * bases), bf16),
            whole((QUAD * 2 * bases, QUAD * channels), bf16),
            whole((channels, LANES), f32),
        ),
        (
            w_radial.T,
            w_mid,
            w_last,
            w_out.reshape(1, channels),
            tiles(local_first),
            tiles(local_second),
            tiles(local_mask),
        ),
        3,
    )
    local = (local_first, local_second, local_mask)
    def scratch(per_step, hots):
        return [pltpu.VMEM((per_step, GROUP, QUAD * CHUNK), bf16) for _ in range(hots)] + [
            pltpu.VMEM((per_step, QUAD, channels, CHUNK), f32),
            pltpu.VMEM((per_step, QUAD, channels, CHUNK), f32),
            pltpu.VMEM((GROUP, LANES), bf16),
        ]

    def cost(slots):
        return pl.CostEstimate(flops=slots * 400000, bytes_accessed=slots * 12, transcendentals=slots * 200)

    parts = 4
    part_rows = local[0].shape[0] // parts
    local_step = part_rows * LANES // (QUAD * CHUNK)

    def local_call(part, start, after):
        operands = [*local, own, right, *weights, *start, *after]
        (sums,) = call(
            functools.partial(
                local_kernel, local_step, channels, bases, part * part_rows, part_rows, (len(start), len(after))
            ),
            (whole((groups * 8, GROUP), f32),),
            "local_pairs",
            scratch(local_step, 2),
            [whole_spec] * len(operands),
            cost(part_rows * LANES),
        )(*operands)
        return sums

    sums = local_call(0, (), ())
    (both,) = call(
        pair_kernel, (whole((2 * offered.shape[0], send_count), bf16),), "two_blocks", specs=[whole_spec] * 3
    )(offered, from_z, sums)
    arrived = [from_z] + [shifted(both, (*step, 0), sizes, 1) for step in PLANAR]
    sums = local_call(1, (sums,), (both,))
    ghost_lists = [tiles(value) for value in (ghost_owner, ghost_index, ghost_mask)]
    ghost_step = ghost_owner.shape[0] // (QUAD * CHUNK)
    partner_rows = blocks * GROUP // LANES * 4
    table_rows = -(-blocks * rows // 16) * 16
    force = whole((8, send_count), f32)
    sums, upward, *level = call(
        functools.partial(ghost_kernel, ghost_step, channels, bases),
        (whole((groups * 8, GROUP), f32), whole((8 + 8 * len(PLANAR), send_count), f32)) + (force,) * len(PLANAR),
        "ghost_pairs",
        [pltpu.VMEM((table_rows, GROUP), bf16), pltpu.VMEM((groups * 4 + partner_rows, GROUP), f32)]
        + scratch(ghost_step, 2),
        [whole_spec] * (9 + len(arrived)),
        cost(ghost_owner.shape[0]),
    )(*ghost_lists, own, *weights, sums, *arrived)
    upward = shifted(upward, (0, 0, 1), sizes, -1)
    sums = local_call(2, (sums,), ())
    mine, *level = call(
        merge_kernel, (force,) * (1 + len(PLANAR)), "forces_upward", specs=[whole_spec] * (2 + len(PLANAR))
    )(upward, *level, sums)
    returned = [shifted(part, (*step, 0), sizes, -1) for part, step in zip(level, PLANAR)]
    sums = local_call(3, (sums,), (mine,))
    forces, energy = call(
        final_kernel,
        (whole((3, own_count), f32), whole((1, own_count), f32)),
        "totals",
        specs=[whole_spec] * (3 + len(returned)),
    )(sums, send, mine, *returned)
    return forces, energy.reshape(own_count)


def solution(mesh):
    names = ("gx", "gy", "gz")
    sizes = tuple((name, mesh.shape[name]) for name in names)
    split = P(names)
    cols = P(None, names)
    in_specs = (cols, cols, split) + (P(),) * 7 + (split,) * 7
    return jax.shard_map(
        functools.partial(on_device, sizes),
        mesh=mesh,
        in_specs=in_specs,
        out_specs=(cols, split),
        check_vma=False,
    )
```

```python
import functools
import math

import jax
import jax.numpy as jnp
from jax import lax
from jax.experimental import pallas as pl
from jax.experimental.pallas import tpu as pltpu
from jax.sharding import PartitionSpec as P

basis_width = 24.0
domain_edge = 1.0
ghost_offsets = ((1, 0, 0), (0, 1, 0), (0, 0, 1), (1, 1, 0), (1, 0, 1), (0, 1, 1), (1, 1, 1))

PLANAR = ((1, 0), (0, 1), (1, 1))
EXTRA = 8
OFFERED = 16
GROUP = 256
LANES = 128
CHUNK = 256
QUAD = 4
VMEM_LIMIT = 48 * 1024 * 1024

NT = (((1,), (1,)), ((), ()))
f32 = jnp.float32
bf16 = jnp.bfloat16


def dot(left, right):
    return jnp.dot(left, right, preferred_element_type=f32)


def dot_nt(left, right):
    return lax.dot_general(left, right, NT, preferred_element_type=f32)


def iota(shape, dim):
    return lax.broadcasted_iota(jnp.int32, shape, dim)


def one_hot(entry, codes):
    entry = entry.astype(f32)
    entry = jnp.concatenate([entry, entry], 0).astype(bf16)
    entry = jnp.concatenate([entry] * (codes.shape[0] // 16), 0)
    pieces = [
        jnp.where(codes == entry[:, start : start + LANES], bf16(1), bf16(0))
        for start in range(0, entry.shape[1], LANES)
    ]
    return jnp.concatenate(pieces, 1)


def row_codes(count):
    return iota((count, LANES), 0).astype(f32).astype(bf16)


def split_two(value):
    high = value.astype(bf16).astype(f32)
    return high, value - high


def coord_rows(coords, gain):
    high, low = split_two(coords)
    return jnp.concatenate([high, gain, low, jnp.zeros_like(gain)], 0)


def eye(count):
    return (iota((count, count), 0) == iota((count, count), 1)).astype(bf16)


def fetch(sources, targets, landed):
    copies = [
        pltpu.make_async_copy(source, target, landed.at[place])
        for place, (source, target) in enumerate(zip(sources, targets))
    ]
    for copy in copies:
        copy.start()
    for copy in copies:
        copy.wait()


def tables_kernel(*refs):
    own_ref, right_ref, offered_ref, mats_ref, radial_ref, radial_t_ref, out_ref, list_ref, need_ref = refs[14:23]
    send_ref = refs[23]
    landing = refs[24:37]
    fetch(refs[:14], landing + (send_ref,), refs[37])
    positions_ref, features_ref, species_ref, scale_ref, w_first_ref, w_second_ref = landing[:6]
    radial_w_ref, w_mid_ref, w_last_ref, w_out_ref, first_ref, second_ref, mask_ref = landing[6:]
    channels = features_ref.shape[0]
    count = features_ref.shape[1]
    species = species_ref[...]
    gain = jnp.zeros((1, count), f32)
    for kind in range(scale_ref.shape[1]):
        scale = scale_ref[:, kind : kind + 1].astype(f32)
        gain = jnp.where(species == kind, scale, gain)
    positions = positions_ref[...]
    left = dot(w_first_ref[...], features_ref[...]).astype(bf16).astype(f32)
    right = dot(w_second_ref[...], features_ref[...]).astype(bf16).astype(f32)
    own_ref[0:channels, :] = 0.5 * left
    own_ref[channels:, :] = jnp.concatenate([positions, gain, positions, gain], 0)
    column = jnp.concatenate([0.5 * right, coord_rows(positions, gain)], 0)
    groups = count // GROUP
    rows = channels + EXTRA
    table = jnp.concatenate([column[:, group * GROUP : (group + 1) * GROUP] for group in range(groups)], 0)
    spare = right_ref.shape[0] - groups * rows
    if spare:
        table = jnp.concatenate([table, jnp.zeros((spare, GROUP), f32)], 0)
    table = table.astype(bf16)
    right_ref[...] = table
    send = jnp.broadcast_to(send_ref[...], (8, send_ref.shape[1]))
    picked = dot(table, one_hot(send & (GROUP - 1), row_codes(GROUP)))
    chosen = group_pick(picked, send // GROUP, rows, groups)
    chosen = jnp.concatenate([chosen, jnp.zeros((OFFERED - EXTRA, chosen.shape[1]), f32)], 0)
    offered_ref[...] = chosen.astype(bf16)

    unit = eye(channels)
    w_mid = w_mid_ref[...]
    w_last = w_last_ref[...]
    last_t = dot_nt(unit, w_last).astype(bf16)
    mid_t = dot_nt(unit, w_mid).astype(bf16)
    wide = QUAD * channels
    for place, matrix in enumerate((w_mid, w_last, last_t, mid_t)):
        mats_ref[place * wide : (place + 1) * wide, :] = (0.5 * diagonal_copies(matrix)).astype(bf16)
    bases = radial_w_ref.shape[0]
    high, low = split_two(radial_w_ref[...])
    high = high.astype(bf16)
    low = low.astype(bf16)
    spread = dot_nt(unit, jnp.concatenate([high, high, low, low], 0)).astype(bf16)
    radial_ref[...] = (0.5 * diagonal_copies(spread)).astype(bf16)
    radial_t_ref[...] = diagonal_copies(jnp.concatenate([high, low], 0)).astype(bf16)
    w_out = w_out_ref[...]
    diagonal = jnp.where(iota((channels, channels), 0) == iota((channels, channels), 1), w_out, 0.0)
    out_ref[...] = jnp.broadcast_to(jnp.sum(diagonal, axis=1, keepdims=True), (channels, LANES))
    bits = (count - 1).bit_length()
    codes = pack(first_ref[...], second_ref[...], mask_ref[...], bits)
    live = [codes[start : start + 8] & 1 for start in range(0, codes.shape[0], 8)]
    need_ref[...] = gather_live(codes, live, 2 * bits + 1, list_ref)


def pack(owner, partner, mask, partner_bits):
    return (owner * 2**partner_bits + partner) * 2 + mask


def gather_live(codes, live, bits, list_ref):
    tiles = len(live)
    sub = iota((8, LANES), 0)
    passed = jnp.zeros((8, LANES), jnp.int32)
    words = []
    for tile in range(tiles):
        dead = 1 - live[tile]
        for step in (1, 2, 4):
            dead = dead + jnp.where(sub >= step, pltpu.roll(dead, step, 0), 0)
        move = (passed + dead) * 2**bits + codes[tile * 8 : tile * 8 + 8]
        words.append(jnp.where(live[tile] != 0, move, 0))
        passed = passed + jnp.broadcast_to(dead[7:8], (8, LANES))
    none = jnp.zeros((8, LANES), jnp.int32)
    for power in range((tiles * 8).bit_length()):
        step = 2**power
        moving = [jnp.where((word & 2 ** (bits + power)) != 0, word, 0) for word in words]
        if step < 8:
            rolled = [pltpu.roll(word, 8 - step, 0) for word in moving] + [none]
            come = [jnp.where(sub < 8 - step, rolled[tile], rolled[tile + 1]) for tile in range(tiles)]
        else:
            come = (moving[step // 8 :] + [none] * tiles)[:tiles]
        words = [word - gone + new for word, gone, new in zip(words, moving, come)]
    for tile, word in enumerate(words):
        list_ref[tile * 8 : tile * 8 + 8, :] = word & (2**bits - 1)
    return tiles * 8 - passed


def diagonal_copies(matrix):
    high, wide = matrix.shape
    repeat = (iota((wide, QUAD * wide), 0) == iota((wide, QUAD * wide), 1) % wide).astype(bf16)
    row = dot(matrix, repeat)
    full = jnp.concatenate([row] * QUAD, 0)
    return jnp.where(iota(full.shape, 0) // high == iota(full.shape, 1) // wide, full, 0.0)


def group_pick(values, high, rows, groups):
    high = jnp.concatenate([high] * (rows // 8), 0)
    chosen = values[:rows]
    for group in range(1, groups):
        chosen = jnp.where(high == group, values[group * rows : (group + 1) * rows], chosen)
    return chosen


def spread_groups(values, high, groups):
    second = iota(values.shape, 0) // 4
    pieces = [jnp.where(high == second + group, values, 0.0) for group in range(0, groups, 2)]
    return jnp.concatenate(pieces, 0)


def lane_pick(table_ref, place, first=0):
    rows, count = table_ref.shape[0] - first, table_ref.shape[1]
    lane = jnp.concatenate([place & (LANES - 1)] * (rows // 8), 0)
    high = jnp.concatenate([place // LANES] * (rows // 8), 0)
    chosen = None
    for group in range(count // LANES):
        part = table_ref[first:, group * LANES : (group + 1) * LANES]
        picked = jnp.take_along_axis(part, lane, axis=1, mode="promise_in_bounds")
        chosen = picked if chosen is None else jnp.where(high == group, picked, chosen)
    return chosen


def sum_rows(values, steps):
    for step in steps:
        values = values + pltpu.roll(values, step, 0)
    return values


def pair_body(
    first_quad,
    quad_count,
    rest,
    own_groups,
    partner_groups,
    channels,
    bases,
    list_ref,
    own_ref,
    right_ref,
    mats_ref,
    radial_ref,
    radial_t_ref,
    out_ref,
    sums,
    hot,
    hot_wide,
    slope_one,
    slope_two,
    codes_ref,
):
    rows = channels + EXTRA
    line = CHUNK // LANES
    block = QUAD * line
    wide = QUAD * channels
    w_out = jnp.concatenate([out_ref[...]] * line, 1)
    centers = iota((bases, CHUNK), 0).astype(f32) * (1.0 / (bases - 1))
    last = iota((8, CHUNK), 0) % 4 == 3
    partner_bits = (partner_groups * LANES - 1).bit_length()
    quads = range(QUAD)
    codes_ref[...] = row_codes(GROUP)

    def matrix(place):
        return mats_ref[place * wide : (place + 1) * wide, :]

    def part(values, number, size=channels):
        return values[number * size : (number + 1) * size]

    def silu_pair(half):
        grow = jnp.tanh(half)
        plus = 1.0 + grow
        hidden = half * plus
        return hidden, plus + hidden * (1.0 - grow)

    def chunk(base, number):
        at = pl.multiple_of(base + number * block, block)
        code_rows = list_ref[pl.ds(at, block), :]
        owners, partners, lives, projected, shifts, squares, weights, stacks, slopes = ([] for _ in range(9))
        for quad in quads:
            cols = slice(quad * CHUNK, (quad + 1) * CHUNK)
            code = jnp.concatenate(
                [
                    jnp.broadcast_to(code_rows[row : row + 1, :], (8, LANES))
                    for row in range(quad * line, (quad + 1) * line)
                ],
                1,
            )
            lives.append((code & 1).astype(f32))
            partner = (code >> 1) & (2**partner_bits - 1)
            owner = code >> (partner_bits + 1)
            owners.append(owner)
            partners.append(partner)
            hot[number, 0:LANES, cols] = one_hot(owner & (LANES - 1), codes_ref[0:LANES, :])
            wide = one_hot(partner & (GROUP - 1), codes_ref[...])
            hot_wide[number, :, cols] = wide
            hot[number, LANES:, cols] = wide[0:LANES] + wide[LANES:]
            yield
        for quad in quads:
            cols = slice(quad * CHUNK, (quad + 1) * CHUNK)
            own_vals = jnp.concatenate(
                [lane_pick(own_ref, owners[quad][:, start : start + LANES]) for start in range(0, CHUNK, LANES)], 1
            )
            partner_vals = group_pick(
                dot(right_ref[...], hot_wide[number, :, cols]),
                partners[quad] // GROUP,
                rows,
                partner_groups * LANES // GROUP,
            )
            projected.append(own_vals[:channels] + partner_vals[:channels])
            own_coords = own_vals[channels:]
            extra = partner_vals[channels:]
            partner_coords = extra + pltpu.roll(extra, 4, 0)
            shift = partner_coords - own_coords
            squared = sum_rows(jnp.where(last, 0.0, shift * shift), (2, 1))
            gain = sum_rows(jnp.where(last, own_coords * partner_coords, 0.0), (2, 1))
            weights.append(lives[quad] * gain)
            away = squared - centers
            basis = jnp.exp(-basis_width * (away * away))
            basis_high, basis_low = split_two(basis)
            stacks.append(jnp.concatenate([basis_high, basis_low, basis_high, basis_low], 0).astype(bf16))
            slopes.append((-2.0 * basis_width) * away * basis)
            shifts.append(shift)
            squares.append(squared)
            yield
        radial = dot(radial_ref[...], jnp.concatenate(stacks, 0))
        yield
        pieces = []
        for quad in quads:
            hidden, slope_one[number, quad] = silu_pair(projected[quad] + part(radial, quad))
            pieces.append(hidden.astype(bf16))
        yield
        half = dot(matrix(0), jnp.concatenate(pieces, 0))
        yield
        pieces = []
        for quad in quads:
            hidden, slope_two[number, quad] = silu_pair(part(half, quad))
            pieces.append(hidden.astype(bf16))
        yield
        half = dot(matrix(1), jnp.concatenate(pieces, 0))
        yield
        pieces = []
        readouts = []
        for quad in quads:
            hidden, slope = silu_pair(part(half, quad))
            terms = w_out * hidden
            terms = sum(terms[start : start + 8] for start in range(8, channels, 8)) + terms[:8]
            readouts.append(sum_rows(terms, (4, 2, 1)))
            pieces.append(((0.5 * w_out) * slope).astype(bf16))
        yield
        back = dot(matrix(2), jnp.concatenate(pieces, 0))
        yield
        pieces = [(part(back, quad) * slope_two[number, quad]).astype(bf16) for quad in quads]
        back = dot(matrix(3), jnp.concatenate(pieces, 0))
        yield
        pieces = [(part(back, quad) * slope_one[number, quad]).astype(bf16) for quad in quads]
        back = dot(radial_t_ref[...], jnp.concatenate(pieces, 0))
        yield
        parts = []
        for quad in quads:
            two = part(back, quad, 2 * bases)
            readout_slope = sum_rows((two[:bases] + two[bases:]) * slopes[quad], (4, 2, 1))
            near = jnp.maximum(1.0 - squares[quad], 0.0)
            weight_near = weights[quad] * near
            energy = weight_near * near * readouts[quad]
            slope = weight_near * (near * readout_slope - 2.0 * readouts[quad])
            push = (2.0 * slope) * shifts[quad]
            values = jnp.where(last, energy, push)
            parts.append(
                jnp.concatenate(
                    [
                        spread_groups(values, owners[quad] // LANES, own_groups),
                        spread_groups(values, partners[quad] // LANES, partner_groups),
                    ],
                    0,
                ).astype(bf16)
            )
        yield
        sums[...] += dot_nt(jnp.concatenate(parts, 1), hot[number])

    def run(first, count):
        running = []
        waiting = [chunk(first * block, number) for number in range(count)]
        while running or waiting:
            if waiting:
                running.append(waiting.pop(0))
            for _ in range(2):
                running = [task for task in running if next(task, task) is not task]

    run(first_quad, quad_count)
    if rest is not None:
        steps, size = rest

        def step(index, unused):
            run(first_quad + quad_count + index * size, size)
            return unused

        lax.fori_loop(0, steps, step, 0)


def rest_of(need, done, total):
    left = total - done
    size = 2 if left % 2 == 0 else 1
    rows = QUAD * CHUNK // LANES
    return jnp.maximum(need - done * rows + size * rows - 1, 0) // (size * rows), size


def local_kernel(channels, bases, first_quad, quad_count, counts, *refs):
    count = 7 + sum(counts)
    codes, own, right, *weights = refs[:7]
    sums, hot, *scratch = refs[count:]
    sums[...] = refs[7][...] if counts[0] else jnp.zeros_like(sums)
    rest = None
    if counts[1]:
        rest = rest_of(
            jnp.max(refs[7 + counts[0]][...]), first_quad + quad_count, codes.shape[0] * LANES // (QUAD * CHUNK)
        )
    groups = own.shape[1] // LANES
    pair_body(
        first_quad,
        quad_count,
        rest,
        groups,
        groups,
        channels,
        bases,
        codes,
        own,
        right,
        *weights,
        sums,
        hot,
        *scratch,
    )


def near_ones(codes, bits, own_ref, channels, coords_ref):
    sub = iota((8, LANES), 0)
    found = []
    for start in range(0, codes.shape[0], 8):
        tile = codes[start : start + 8]
        squared = jnp.zeros((8, LANES), f32)
        for low in range(4):
            code = jnp.where(
                sub < 4,
                jnp.broadcast_to(tile[low : low + 1], (8, LANES)),
                jnp.broadcast_to(tile[low + 4 : low + 5], (8, LANES)),
            )
            shift = lane_pick(coords_ref, (code >> 1) & (2**bits - 1)) - lane_pick(own_ref, code >> (bits + 1), channels)
            square = shift * shift
            total = square + pltpu.roll(square, 7, 0) + pltpu.roll(square, 6, 0)
            if low:
                total = pltpu.roll(total, low, 0)
            squared = jnp.where(sub % 4 == low, total, squared)
        found.append(jnp.where(squared < 1.001, tile & 1, 0))
    return found


def ghost_kernel(quad_count, channels, bases, *refs):
    blocks = len(ghost_offsets)
    owner, partner, mask, own, *weights = refs[:8]
    sums_in = refs[8]
    arrived = refs[9 : 10 + len(PLANAR)]
    sums_out, upward, *level = refs[10 + len(PLANAR) : 12 + 2 * len(PLANAR)]
    table, sums, codes_ref, coords_ref, *scratch = refs[12 + 2 * len(PLANAR) :]
    groups = own.shape[1] // LANES
    partner_groups = blocks * GROUP // LANES
    sums[...] = jnp.zeros_like(sums)
    pieces = []
    for offset in ghost_offsets:
        if offset[:2] == (0, 0):
            source, start = arrived[0], 0
        else:
            source, start = arrived[1 + PLANAR.index(offset[:2])], offset[2] * (channels + OFFERED)
        extra = source[start + channels : start + channels + OFFERED, :].astype(f32)
        moved = jnp.concatenate(
            [extra[axis : axis + 1] + extra[axis + 4 : axis + 5] + domain_edge * offset[axis] for axis in range(3)], 0
        )
        pieces += [source[start : start + channels, :].astype(f32), coord_rows(moved, extra[3:4])]
        place = ghost_offsets.index(offset) * GROUP
        coords_ref[:, place : place + GROUP] = jnp.concatenate([moved, extra[3:4], moved, extra[3:4]], 0)
    pieces.append(jnp.zeros((table.shape[0] - blocks * (channels + EXTRA), GROUP), f32))
    table[...] = jnp.concatenate(pieces, 0).astype(bf16)
    bits = (partner_groups * LANES - 1).bit_length()
    codes = pack(owner[...], partner[...], mask[...], bits)
    live = near_ones(codes, bits, own, channels, coords_ref)
    need = gather_live(codes, live, bits + (own.shape[1] - 1).bit_length() + 1, codes_ref)
    pair_body(
        0,
        quad_count,
        rest_of(jnp.max(need), quad_count, owner.shape[0] * LANES // (QUAD * CHUNK)),
        groups,
        partner_groups,
        channels,
        bases,
        codes_ref,
        own,
        table,
        *weights,
        sums,
        *scratch,
    )
    first = groups * 4
    sums_out[0:first, :] = sums_in[0:first, :] + sums[0:first, :]
    sums_out[first:, :] = sums_in[first:, :]
    for block, offset in enumerate(ghost_offsets):
        halves = []
        for half in range(GROUP // LANES):
            start = first + (block * (GROUP // LANES) + half) * 4
            halves.append(sums[start : start + 4, LANES:])
        force = -jnp.concatenate(halves, 1)
        force = jnp.concatenate([force, jnp.zeros_like(force)], 0)
        if offset[2]:
            place = 0 if offset[:2] == (0, 0) else 1 + PLANAR.index(offset[:2])
            upward[place * 8 : place * 8 + 8, :] = force
        else:
            level[PLANAR.index(offset[:2])][...] = force


def pair_kernel(offered_ref, from_z_ref, unused_ref, both_ref):
    count = offered_ref.shape[0]
    both_ref[0:count, :] = offered_ref[...]
    both_ref[count:, :] = from_z_ref[...]


def merge_kernel(*refs):
    upward, *level = refs[: 1 + len(PLANAR)]
    outs = refs[2 + len(PLANAR) :]
    outs[0][...] = upward[0:8, :]
    for place, part in enumerate(level):
        outs[1 + place][...] = part[...] + upward[8 * place + 8 : 8 * place + 16, :]


def final_kernel(*refs):
    sums_ref, send_ref, *arrived = refs[:-2]
    forces_ref, energy_ref = refs[-2:]
    incoming = arrived[0][...]
    for part in arrived[1:]:
        incoming = incoming + part[...]
    high, low = split_two(jnp.concatenate([incoming[:4], incoming[:4]], 0))
    send = jnp.broadcast_to(send_ref[...], (8, send_ref.shape[1]))
    groups = sums_ref.shape[0] // 8
    hot = one_hot(send & (LANES - 1), row_codes(LANES))
    spread = [spread_groups(value, send // LANES, groups).astype(bf16) for value in (high, low)]
    back = dot_nt(jnp.concatenate(spread, 0), hot)
    back = back[: groups * 4] + back[groups * 4 :]
    for group in range(groups):
        own = sums_ref[group * 4 : group * 4 + 4, 0:LANES]
        partner = sums_ref[(groups + group) * 4 : (groups + group) * 4 + 4, LANES:]
        total = own - partner + back[group * 4 : group * 4 + 4]
        cols = slice(group * LANES, (group + 1) * LANES)
        forces_ref[:, cols] = total[0:3]
        energy_ref[:, cols] = own[3:4]


def whole(shape, dtype):
    return jax.ShapeDtypeStruct(shape, dtype)


def call(kernel, outs, name, scratch=(), specs=None, cost=None):
    more = {} if cost is None else dict(cost_estimate=cost)
    return pl.pallas_call(
        kernel,
        grid=(1,),
        in_specs=specs,
        out_specs=tuple(pl.BlockSpec(memory_space=pltpu.VMEM) for _ in outs),
        out_shape=outs,
        scratch_shapes=list(scratch),
        compiler_params=pltpu.CompilerParams(vmem_limit_bytes=VMEM_LIMIT),
        name=name,
        **more,
    )


def shifted(value, offset, sizes, sign):
    used = tuple(axis for axis, step in zip(sizes, offset) if step)
    dims = [size for name, size in used]
    pairs = []
    for flat in range(math.prod(dims)):
        place, rest = [], flat
        for size in reversed(dims):
            place.insert(0, rest % size)
            rest //= size
        target = 0
        for at, size in zip(place, dims):
            target = target * size + (at - sign) % size
        pairs.append((flat, target))
    return lax.ppermute(value, tuple(name for name, size in used), pairs)


def on_device(
    sizes,
    positions,
    features,
    species,
    species_scale,
    w_first,
    w_second,
    w_radial,
    w_mid,
    w_last,
    w_out,
    ghost_send,
    local_first,
    local_second,
    local_mask,
    ghost_owner,
    ghost_index,
    ghost_mask,
):
    channels, own_count = features.shape
    send_count = ghost_send.shape[0]
    bases = w_radial.shape[1]
    rows = channels + EXTRA
    groups = own_count // LANES
    blocks = len(ghost_offsets)
    whole_spec = pl.BlockSpec(memory_space=pltpu.VMEM)
    def tiles(value):
        return value.reshape(value.shape[0] // LANES, LANES)

    def fetching(kernel, name, outs, operands, kept):
        here = [pltpu.with_memory_space_constraint(value, pltpu.HBM) for value in operands]
        landing = operands[: len(operands) - kept]
        return call(
            kernel,
            outs + tuple(whole(value.shape, value.dtype) for value in operands[len(landing) :]),
            name,
            [pltpu.VMEM(value.shape, value.dtype) for value in landing]
            + [pltpu.SemaphoreType.DMA((len(operands),))],
            [pl.BlockSpec(memory_space=pltpu.HBM)] * len(operands),
        )(*here)

    own, right, offered, *weights, local, need, send = fetching(
        tables_kernel,
        "tables",
        (
            whole((rows, own_count), f32),
            whole((-(-own_count // GROUP * rows // 16) * 16, GROUP), bf16),
            whole((channels + OFFERED, send_count), bf16),
            whole((4 * QUAD * channels, QUAD * channels), bf16),
            whole((QUAD * channels, QUAD * 4 * bases), bf16),
            whole((QUAD * 2 * bases, QUAD * channels), bf16),
            whole((channels, LANES), f32),
            whole((local_first.shape[0] // LANES, LANES), jnp.int32),
            whole((8, LANES), jnp.int32),
        ),
        (
            positions,
            features,
            species.reshape(1, own_count),
            species_scale.reshape(1, species_scale.shape[0]),
            w_first,
            w_second,
            w_radial.T,
            w_mid,
            w_last,
            w_out.reshape(1, channels),
            tiles(local_first),
            tiles(local_second),
            tiles(local_mask),
            ghost_send.reshape(1, send_count),
        ),
        1,
    )
    from_z = shifted(offered, (0, 0, 1), sizes, 1)

    def scratch(per_step, hots):
        return [pltpu.VMEM((per_step, GROUP, QUAD * CHUNK), bf16) for _ in range(hots)] + [
            pltpu.VMEM((per_step, QUAD, channels, CHUNK), f32),
            pltpu.VMEM((per_step, QUAD, channels, CHUNK), f32),
            pltpu.VMEM((GROUP, LANES), bf16),
        ]

    def cost(slots):
        return pl.CostEstimate(flops=slots * 400000, bytes_accessed=slots * 12, transcendentals=slots * 200)

    quads = local.shape[0] * LANES // (QUAD * CHUNK)
    cuts = [0, quads // 4, quads * 9 // 20, quads * 13 // 20, quads * 9 // 10]

    def local_call(part, start, needed, after):
        operands = [local, own, right, *weights, *start, *needed, *after]
        size = cuts[part + 1] - cuts[part]
        (sums,) = call(
            functools.partial(
                local_kernel, channels, bases, cuts[part], size, (len(start), len(needed), len(after))
            ),
            (whole((groups * 8, GROUP), f32),),
            "local_pairs",
            scratch(size, 2),
            [whole_spec] * len(operands),
            cost(size * QUAD * CHUNK),
        )(*operands)
        return sums

    sums = local_call(0, (), (), ())
    (both,) = call(
        pair_kernel, (whole((2 * offered.shape[0], send_count), bf16),), "two_blocks", specs=[whole_spec] * 3
    )(offered, from_z, sums)
    arrived = [from_z] + [shifted(both, (*step, 0), sizes, 1) for step in PLANAR]
    sums = local_call(1, (sums,), (), (both,))
    ghost_lists = [tiles(value) for value in (ghost_owner, ghost_index, ghost_mask)]
    ghost_step = ghost_owner.shape[0] // (QUAD * CHUNK) // 3
    partner_rows = blocks * GROUP // LANES * 4
    table_rows = -(-blocks * rows // 16) * 16
    force = whole((8, send_count), f32)
    sums, upward, *level = call(
        functools.partial(ghost_kernel, ghost_step, channels, bases),
        (whole((groups * 8, GROUP), f32), whole((8 + 8 * len(PLANAR), send_count), f32)) + (force,) * len(PLANAR),
        "ghost_pairs",
        [
            pltpu.VMEM((table_rows, GROUP), bf16),
            pltpu.VMEM((groups * 4 + partner_rows, GROUP), f32),
            pltpu.VMEM((ghost_owner.shape[0] // LANES, LANES), jnp.int32),
            pltpu.VMEM((8, blocks * GROUP), f32),
        ]
        + scratch(ghost_step, 2),
        [whole_spec] * (9 + len(arrived)),
        cost(ghost_owner.shape[0]),
    )(*ghost_lists, own, *weights, sums, *arrived)
    upward = shifted(upward, (0, 0, 1), sizes, -1)
    sums = local_call(2, (sums,), (), ())
    mine, *level = call(
        merge_kernel, (force,) * (1 + len(PLANAR)), "forces_upward", specs=[whole_spec] * (2 + len(PLANAR))
    )(upward, *level, sums)
    returned = [shifted(part, (*step, 0), sizes, -1) for part, step in zip(level, PLANAR)]
    sums = local_call(3, (sums,), (need,), (mine,))
    forces, energy = call(
        final_kernel,
        (whole((3, own_count), f32), whole((1, own_count), f32)),
        "totals",
        specs=[whole_spec] * (3 + len(returned)),
    )(sums, send, mine, *returned)
    return forces, energy.reshape(own_count)


def solution(mesh):
    names = ("gx", "gy", "gz")
    sizes = tuple((name, mesh.shape[name]) for name in names)
    split = P(names)
    cols = P(None, names)
    in_specs = (cols, cols, split) + (P(),) * 7 + (split,) * 7
    return jax.shard_map(
        functools.partial(on_device, sizes),
        mesh=mesh,
        in_specs=in_specs,
        out_specs=(cols, split),
        check_vma=False,
    )
```

```python
import functools
import math

import jax
import jax.numpy as jnp
from jax import lax
from jax.experimental import pallas as pl
from jax.experimental.pallas import tpu as pltpu
from jax.sharding import PartitionSpec as P

basis_width = 24.0
domain_edge = 1.0
ghost_offsets = ((1, 0, 0), (0, 1, 0), (0, 0, 1), (1, 1, 0), (1, 0, 1), (0, 1, 1), (1, 1, 1))

PLANAR = ((1, 0), (0, 1), (1, 1))
EXTRA = 8
OFFERED = 16
GROUP = 256
LANES = 128
CHUNK = 256
QUAD = 4
VMEM_LIMIT = 48 * 1024 * 1024

NT = (((1,), (1,)), ((), ()))
f32 = jnp.float32
bf16 = jnp.bfloat16


def dot(left, right):
    return jnp.dot(left, right, preferred_element_type=f32)


def dot_nt(left, right):
    return lax.dot_general(left, right, NT, preferred_element_type=f32)


def iota(shape, dim):
    return lax.broadcasted_iota(jnp.int32, shape, dim)


def one_hot(entry, codes):
    entry = entry.astype(f32)
    entry = jnp.concatenate([entry, entry], 0).astype(bf16)
    entry = jnp.concatenate([entry] * (codes.shape[0] // 16), 0)
    pieces = [
        jnp.where(codes == entry[:, start : start + LANES], bf16(1), bf16(0))
        for start in range(0, entry.shape[1], LANES)
    ]
    return jnp.concatenate(pieces, 1)


def row_codes(count):
    return iota((count, LANES), 0).astype(f32).astype(bf16)


def split_two(value):
    high = value.astype(bf16).astype(f32)
    return high, value - high


def coord_rows(coords, gain):
    high, low = split_two(coords)
    return jnp.concatenate([high, gain, low, jnp.zeros_like(gain)], 0)


def eye(count):
    return (iota((count, count), 0) == iota((count, count), 1)).astype(bf16)


def fetch(sources, targets, landed):
    copies = [
        pltpu.make_async_copy(source, target, landed.at[place])
        for place, (source, target) in enumerate(zip(sources, targets))
    ]
    for copy in copies:
        copy.start()
    for copy in copies:
        copy.wait()


def tables_kernel(*refs):
    own_ref, right_ref, offered_ref, mats_ref, radial_ref, radial_t_ref, out_ref, list_ref, need_ref = refs[14:23]
    send_ref = refs[23]
    landing = refs[24:37]
    fetch(refs[:14], landing + (send_ref,), refs[37])
    positions_ref, features_ref, species_ref, scale_ref, w_first_ref, w_second_ref = landing[:6]
    radial_w_ref, w_mid_ref, w_last_ref, w_out_ref, first_ref, second_ref, mask_ref = landing[6:]
    channels = features_ref.shape[0]
    count = features_ref.shape[1]
    species = species_ref[...]
    gain = jnp.zeros((1, count), f32)
    for kind in range(scale_ref.shape[1]):
        scale = scale_ref[:, kind : kind + 1].astype(f32)
        gain = jnp.where(species == kind, scale, gain)
    positions = positions_ref[...]
    left = dot(w_first_ref[...], features_ref[...]).astype(bf16).astype(f32)
    right = dot(w_second_ref[...], features_ref[...]).astype(bf16).astype(f32)
    own_ref[0:channels, :] = 0.5 * left
    own_ref[channels:, :] = jnp.concatenate([positions, gain, positions, gain], 0)
    column = jnp.concatenate([0.5 * right, coord_rows(positions, gain)], 0)
    groups = count // GROUP
    rows = channels + EXTRA
    table = jnp.concatenate([column[:, group * GROUP : (group + 1) * GROUP] for group in range(groups)], 0)
    spare = right_ref.shape[0] - groups * rows
    if spare:
        table = jnp.concatenate([table, jnp.zeros((spare, GROUP), f32)], 0)
    table = table.astype(bf16)
    right_ref[...] = table
    send = jnp.broadcast_to(send_ref[...], (8, send_ref.shape[1]))
    picked = dot(table, one_hot(send & (GROUP - 1), row_codes(GROUP)))
    chosen = group_pick(picked, send // GROUP, rows, groups)
    chosen = jnp.concatenate([chosen, jnp.zeros((OFFERED - EXTRA, chosen.shape[1]), f32)], 0)
    offered_ref[...] = chosen.astype(bf16)

    unit = eye(channels)
    w_mid = w_mid_ref[...]
    w_last = w_last_ref[...]
    last_t = dot_nt(unit, w_last).astype(bf16)
    mid_t = dot_nt(unit, w_mid).astype(bf16)
    wide = QUAD * channels
    for place, matrix in enumerate((w_mid, w_last, last_t, mid_t)):
        mats_ref[place * wide : (place + 1) * wide, :] = (0.5 * diagonal_copies(matrix)).astype(bf16)
    bases = radial_w_ref.shape[0]
    high, low = split_two(radial_w_ref[...])
    high = high.astype(bf16)
    low = low.astype(bf16)
    spread = dot_nt(unit, jnp.concatenate([high, high, low, low], 0)).astype(bf16)
    radial_ref[...] = (0.5 * diagonal_copies(spread)).astype(bf16)
    radial_t_ref[...] = diagonal_copies(jnp.concatenate([high, low], 0)).astype(bf16)
    w_out = w_out_ref[...]
    diagonal = jnp.where(iota((channels, channels), 0) == iota((channels, channels), 1), w_out, 0.0)
    out_ref[...] = jnp.broadcast_to(jnp.sum(diagonal, axis=1, keepdims=True), (channels, LANES))
    bits = (count - 1).bit_length()
    codes = pack(first_ref[...], second_ref[...], mask_ref[...], bits)
    live = [codes[start : start + 8] & 1 for start in range(0, codes.shape[0], 8)]
    need_ref[...] = gather_live(codes, live, 2 * bits + 1, list_ref)


def pack(owner, partner, mask, partner_bits):
    return (owner * 2**partner_bits + partner) * 2 + mask


def gather_live(codes, live, bits, list_ref):
    tiles = len(live)
    sub = iota((8, LANES), 0)
    passed = jnp.zeros((8, LANES), jnp.int32)
    words = []
    for tile in range(tiles):
        dead = 1 - live[tile]
        for step in (1, 2, 4):
            dead = dead + jnp.where(sub >= step, pltpu.roll(dead, step, 0), 0)
        move = (passed + dead) * 2**bits + codes[tile * 8 : tile * 8 + 8]
        words.append(jnp.where(live[tile] != 0, move, 0))
        passed = passed + jnp.broadcast_to(dead[7:8], (8, LANES))
    none = jnp.zeros((8, LANES), jnp.int32)
    for power in range((tiles * 8).bit_length()):
        step = 2**power
        moving = [jnp.where((word & 2 ** (bits + power)) != 0, word, 0) for word in words]
        if step < 8:
            rolled = [pltpu.roll(word, 8 - step, 0) for word in moving] + [none]
            come = [jnp.where(sub < 8 - step, rolled[tile], rolled[tile + 1]) for tile in range(tiles)]
        else:
            come = (moving[step // 8 :] + [none] * tiles)[:tiles]
        words = [word - gone + new for word, gone, new in zip(words, moving, come)]
    for tile, word in enumerate(words):
        list_ref[tile * 8 : tile * 8 + 8, :] = word & (2**bits - 1)
    return tiles * 8 - passed


def diagonal_copies(matrix):
    high, wide = matrix.shape
    repeat = (iota((wide, QUAD * wide), 0) == iota((wide, QUAD * wide), 1) % wide).astype(bf16)
    row = dot(matrix, repeat)
    full = jnp.concatenate([row] * QUAD, 0)
    return jnp.where(iota(full.shape, 0) // high == iota(full.shape, 1) // wide, full, 0.0)


def group_pick(values, high, rows, groups):
    high = jnp.concatenate([high] * (rows // 8), 0)
    chosen = values[:rows]
    for group in range(1, groups):
        chosen = jnp.where(high == group, values[group * rows : (group + 1) * rows], chosen)
    return chosen


def spread_groups(values, high, groups):
    second = iota(values.shape, 0) // 4
    pieces = [jnp.where(high == second + group, values, 0.0) for group in range(0, groups, 2)]
    return jnp.concatenate(pieces, 0)


def lane_pick(table_ref, place, first=0):
    rows, count = table_ref.shape[0] - first, table_ref.shape[1]
    lane = jnp.concatenate([place & (LANES - 1)] * (rows // 8), 0)
    high = jnp.concatenate([place // LANES] * (rows // 8), 0)
    chosen = None
    for group in range(count // LANES):
        part = table_ref[first:, group * LANES : (group + 1) * LANES]
        picked = jnp.take_along_axis(part, lane, axis=1, mode="promise_in_bounds")
        chosen = picked if chosen is None else jnp.where(high == group, picked, chosen)
    return chosen


def sum_rows(values, steps):
    for step in steps:
        values = values + pltpu.roll(values, step, 0)
    return values


def pair_tasks(
    own_groups,
    partner_groups,
    channels,
    bases,
    list_ref,
    own_ref,
    right_ref,
    mats_ref,
    radial_ref,
    radial_t_ref,
    out_ref,
    sums,
    hot,
    hot_wide,
    slope_one,
    slope_two,
    codes_ref,
):
    rows = channels + EXTRA
    line = CHUNK // LANES
    block = QUAD * line
    wide = QUAD * channels
    w_out = jnp.concatenate([out_ref[...]] * line, 1)
    centers = iota((bases, CHUNK), 0).astype(f32) * (1.0 / (bases - 1))
    last = iota((8, CHUNK), 0) % 4 == 3
    partner_bits = (partner_groups * LANES - 1).bit_length()
    quads = range(QUAD)
    codes_ref[...] = row_codes(GROUP)

    def matrix(place):
        return mats_ref[place * wide : (place + 1) * wide, :]

    def part(values, number, size=channels):
        return values[number * size : (number + 1) * size]

    def silu_pair(half):
        grow = jnp.tanh(half)
        plus = 1.0 + grow
        hidden = half * plus
        return hidden, plus + hidden * (1.0 - grow)

    def task(first, number):
        at = pl.multiple_of(first * block, block)
        code_rows = list_ref[pl.ds(at, block), :]
        owners, partners, lives, projected, shifts, squares, weights, stacks, slopes = ([] for _ in range(9))
        for quad in quads:
            cols = slice(quad * CHUNK, (quad + 1) * CHUNK)
            code = jnp.concatenate(
                [
                    jnp.broadcast_to(code_rows[row : row + 1, :], (8, LANES))
                    for row in range(quad * line, (quad + 1) * line)
                ],
                1,
            )
            lives.append((code & 1).astype(f32))
            partner = (code >> 1) & (2**partner_bits - 1)
            owner = code >> (partner_bits + 1)
            owners.append(owner)
            partners.append(partner)
            hot[number, 0:LANES, cols] = one_hot(owner & (LANES - 1), codes_ref[0:LANES, :])
            wide = one_hot(partner & (GROUP - 1), codes_ref[...])
            hot_wide[number, :, cols] = wide
            hot[number, LANES:, cols] = wide[0:LANES] + wide[LANES:]
            yield
        for quad in quads:
            cols = slice(quad * CHUNK, (quad + 1) * CHUNK)
            own_vals = jnp.concatenate(
                [lane_pick(own_ref, owners[quad][:, start : start + LANES]) for start in range(0, CHUNK, LANES)], 1
            )
            partner_vals = group_pick(
                dot(right_ref[...], hot_wide[number, :, cols]),
                partners[quad] // GROUP,
                rows,
                partner_groups * LANES // GROUP,
            )
            projected.append(own_vals[:channels] + partner_vals[:channels])
            own_coords = own_vals[channels:]
            extra = partner_vals[channels:]
            partner_coords = extra + pltpu.roll(extra, 4, 0)
            shift = partner_coords - own_coords
            squared = sum_rows(jnp.where(last, 0.0, shift * shift), (2, 1))
            gain = sum_rows(jnp.where(last, own_coords * partner_coords, 0.0), (2, 1))
            weights.append(lives[quad] * gain)
            away = squared - centers
            basis = jnp.exp(-basis_width * (away * away))
            basis_high, basis_low = split_two(basis)
            stacks.append(jnp.concatenate([basis_high, basis_low, basis_high, basis_low], 0).astype(bf16))
            slopes.append((-2.0 * basis_width) * away * basis)
            shifts.append(shift)
            squares.append(squared)
            yield
        radial = dot(radial_ref[...], jnp.concatenate(stacks, 0))
        yield
        pieces = []
        for quad in quads:
            hidden, slope_one[number, quad] = silu_pair(projected[quad] + part(radial, quad))
            pieces.append(hidden.astype(bf16))
        yield
        half = dot(matrix(0), jnp.concatenate(pieces, 0))
        yield
        pieces = []
        for quad in quads:
            hidden, slope_two[number, quad] = silu_pair(part(half, quad))
            pieces.append(hidden.astype(bf16))
        yield
        half = dot(matrix(1), jnp.concatenate(pieces, 0))
        yield
        pieces = []
        readouts = []
        for quad in quads:
            hidden, slope = silu_pair(part(half, quad))
            terms = w_out * hidden
            terms = sum(terms[start : start + 8] for start in range(8, channels, 8)) + terms[:8]
            readouts.append(sum_rows(terms, (4, 2, 1)))
            pieces.append(((0.5 * w_out) * slope).astype(bf16))
        yield
        back = dot(matrix(2), jnp.concatenate(pieces, 0))
        yield
        pieces = [(part(back, quad) * slope_two[number, quad]).astype(bf16) for quad in quads]
        back = dot(matrix(3), jnp.concatenate(pieces, 0))
        yield
        pieces = [(part(back, quad) * slope_one[number, quad]).astype(bf16) for quad in quads]
        back = dot(radial_t_ref[...], jnp.concatenate(pieces, 0))
        yield
        parts = []
        for quad in quads:
            two = part(back, quad, 2 * bases)
            readout_slope = sum_rows((two[:bases] + two[bases:]) * slopes[quad], (4, 2, 1))
            near = jnp.maximum(1.0 - squares[quad], 0.0)
            weight_near = weights[quad] * near
            energy = weight_near * near * readouts[quad]
            slope = weight_near * (near * readout_slope - 2.0 * readouts[quad])
            push = (2.0 * slope) * shifts[quad]
            values = jnp.where(last, energy, push)
            parts.append(
                jnp.concatenate(
                    [
                        spread_groups(values, owners[quad] // LANES, own_groups),
                        spread_groups(values, partners[quad] // LANES, partner_groups),
                    ],
                    0,
                ).astype(bf16)
            )
        yield
        sums[...] += dot_nt(jnp.concatenate(parts, 1), hot[number])

    return task


def run(tasks, then=None, later=()):
    running, waiting = [], list(tasks)
    while running or waiting or then is not None:
        if waiting:
            running.append(waiting.pop(0))
        if then is not None and next(then, then) is then:
            then = None
            waiting += later
        for _ in range(2):
            running = [task for task in running if next(task, task) is not task]


def run_rest(task, done, rest):
    steps, size = rest

    def step(index, unused):
        run([task(done + index * size + number, number) for number in range(size)])
        return unused

    lax.fori_loop(0, steps, step, 0)


def rest_of(need, done, total):
    left = total - done
    size = 2 if left % 2 == 0 else 1
    rows = QUAD * CHUNK // LANES
    return jnp.maximum(need - done * rows + size * rows - 1, 0) // (size * rows), size


def local_kernel(channels, bases, first_quad, quad_count, counts, *refs):
    count = 7 + sum(counts)
    codes, own, right, *weights = refs[:7]
    sums, hot, *scratch = refs[count:]
    sums[...] = refs[7][...] if counts[0] else jnp.zeros_like(sums)
    groups = own.shape[1] // LANES
    task = pair_tasks(groups, groups, channels, bases, codes, own, right, *weights, sums, hot, *scratch)
    run([task(first_quad + number, number) for number in range(quad_count)])
    if counts[1]:
        done = first_quad + quad_count
        need = jnp.max(refs[7 + counts[0]][...])
        run_rest(task, done, rest_of(need, done, codes.shape[0] * LANES // (QUAD * CHUNK)))


def near_ones(codes, bits, own_ref, channels, coords_ref, found):
    sub = iota((8, LANES), 0)
    for start in range(0, codes.shape[0], 8):
        tile = codes[start : start + 8]
        squared = jnp.zeros((8, LANES), f32)
        for low in range(4):
            code = jnp.where(
                sub < 4,
                jnp.broadcast_to(tile[low : low + 1], (8, LANES)),
                jnp.broadcast_to(tile[low + 4 : low + 5], (8, LANES)),
            )
            shift = lane_pick(coords_ref, (code >> 1) & (2**bits - 1)) - lane_pick(own_ref, code >> (bits + 1), channels)
            square = shift * shift
            total = square + pltpu.roll(square, 7, 0) + pltpu.roll(square, 6, 0)
            if low:
                total = pltpu.roll(total, low, 0)
            squared = jnp.where(sub % 4 == low, total, squared)
        found.append(jnp.where(squared < 1.001, tile & 1, 0))
        yield


def ghost_kernel(quad_count, local_quads, channels, bases, *refs):
    blocks = len(ghost_offsets)
    owner, partner, mask, own, *weights = refs[:8]
    local, right, sums_in = refs[8:11]
    arrived = refs[11 : 12 + len(PLANAR)]
    sums_out, upward, *level = refs[12 + len(PLANAR) : 14 + 2 * len(PLANAR)]
    table, sums, codes_ref, coords_ref, *scratch = refs[14 + 2 * len(PLANAR) :]
    half = len(scratch) // 2
    groups = own.shape[1] // LANES
    partner_groups = blocks * GROUP // LANES
    sums[...] = jnp.zeros_like(sums)
    pieces = []
    for offset in ghost_offsets:
        if offset[:2] == (0, 0):
            source, start = arrived[0], 0
        else:
            source, start = arrived[1 + PLANAR.index(offset[:2])], offset[2] * (channels + OFFERED)
        extra = source[start + channels : start + channels + OFFERED, :].astype(f32)
        moved = jnp.concatenate(
            [extra[axis : axis + 1] + extra[axis + 4 : axis + 5] + domain_edge * offset[axis] for axis in range(3)], 0
        )
        pieces += [source[start : start + channels, :].astype(f32), coord_rows(moved, extra[3:4])]
        place = ghost_offsets.index(offset) * GROUP
        coords_ref[:, place : place + GROUP] = jnp.concatenate([moved, extra[3:4], moved, extra[3:4]], 0)
    pieces.append(jnp.zeros((table.shape[0] - blocks * (channels + EXTRA), GROUP), f32))
    table[...] = jnp.concatenate(pieces, 0).astype(bf16)
    bits = (partner_groups * LANES - 1).bit_length()
    codes = pack(owner[...], partner[...], mask[...], bits)
    sums_out[...] = sums_in[...]
    local_task = pair_tasks(
        groups, groups, channels, bases, local, own, right, *weights, sums_out, *scratch[:half]
    )
    task = pair_tasks(
        groups, partner_groups, channels, bases, codes_ref, own, table, *weights, sums, *scratch[half:]
    )
    need = []

    def search():
        live = []
        yield from near_ones(codes, bits, own, channels, coords_ref, live)
        need.append(gather_live(codes, live, bits + (own.shape[1] - 1).bit_length() + 1, codes_ref))
        yield

    run(
        [local_task(quad, quad - local_quads[0]) for quad in range(*local_quads)],
        search(),
        [task(number, number) for number in range(quad_count)],
    )
    total = owner.shape[0] * LANES // (QUAD * CHUNK)
    run_rest(task, quad_count, rest_of(jnp.max(need[0]), quad_count, total))
    first = groups * 4
    sums_out[0:first, :] += sums[0:first, :]
    for block, offset in enumerate(ghost_offsets):
        halves = []
        for half in range(GROUP // LANES):
            start = first + (block * (GROUP // LANES) + half) * 4
            halves.append(sums[start : start + 4, LANES:])
        force = -jnp.concatenate(halves, 1)
        force = jnp.concatenate([force, jnp.zeros_like(force)], 0)
        if offset[2]:
            place = 0 if offset[:2] == (0, 0) else 1 + PLANAR.index(offset[:2])
            upward[place * 8 : place * 8 + 8, :] = force
        else:
            level[PLANAR.index(offset[:2])][...] = force


def pair_kernel(offered_ref, from_z_ref, unused_ref, both_ref):
    count = offered_ref.shape[0]
    both_ref[0:count, :] = offered_ref[...]
    both_ref[count:, :] = from_z_ref[...]


def merge_kernel(*refs):
    upward, *level = refs[: 1 + len(PLANAR)]
    outs = refs[2 + len(PLANAR) :]
    outs[0][...] = upward[0:8, :]
    for place, part in enumerate(level):
        outs[1 + place][...] = part[...] + upward[8 * place + 8 : 8 * place + 16, :]


def final_kernel(*refs):
    sums_ref, send_ref, *arrived = refs[:-2]
    forces_ref, energy_ref = refs[-2:]
    incoming = arrived[0][...]
    for part in arrived[1:]:
        incoming = incoming + part[...]
    high, low = split_two(jnp.concatenate([incoming[:4], incoming[:4]], 0))
    send = jnp.broadcast_to(send_ref[...], (8, send_ref.shape[1]))
    groups = sums_ref.shape[0] // 8
    hot = one_hot(send & (LANES - 1), row_codes(LANES))
    spread = [spread_groups(value, send // LANES, groups).astype(bf16) for value in (high, low)]
    back = dot_nt(jnp.concatenate(spread, 0), hot)
    back = back[: groups * 4] + back[groups * 4 :]
    for group in range(groups):
        own = sums_ref[group * 4 : group * 4 + 4, 0:LANES]
        partner = sums_ref[(groups + group) * 4 : (groups + group) * 4 + 4, LANES:]
        total = own - partner + back[group * 4 : group * 4 + 4]
        cols = slice(group * LANES, (group + 1) * LANES)
        forces_ref[:, cols] = total[0:3]
        energy_ref[:, cols] = own[3:4]


def whole(shape, dtype):
    return jax.ShapeDtypeStruct(shape, dtype)


def call(kernel, outs, name, scratch=(), specs=None, cost=None):
    more = {} if cost is None else dict(cost_estimate=cost)
    return pl.pallas_call(
        kernel,
        grid=(1,),
        in_specs=specs,
        out_specs=tuple(pl.BlockSpec(memory_space=pltpu.VMEM) for _ in outs),
        out_shape=outs,
        scratch_shapes=list(scratch),
        compiler_params=pltpu.CompilerParams(vmem_limit_bytes=VMEM_LIMIT),
        name=name,
        **more,
    )


def shifted(value, offset, sizes, sign):
    used = tuple(axis for axis, step in zip(sizes, offset) if step)
    dims = [size for name, size in used]
    pairs = []
    for flat in range(math.prod(dims)):
        place, rest = [], flat
        for size in reversed(dims):
            place.insert(0, rest % size)
            rest //= size
        target = 0
        for at, size in zip(place, dims):
            target = target * size + (at - sign) % size
        pairs.append((flat, target))
    return lax.ppermute(value, tuple(name for name, size in used), pairs)


def on_device(
    sizes,
    positions,
    features,
    species,
    species_scale,
    w_first,
    w_second,
    w_radial,
    w_mid,
    w_last,
    w_out,
    ghost_send,
    local_first,
    local_second,
    local_mask,
    ghost_owner,
    ghost_index,
    ghost_mask,
):
    channels, own_count = features.shape
    send_count = ghost_send.shape[0]
    bases = w_radial.shape[1]
    rows = channels + EXTRA
    groups = own_count // LANES
    blocks = len(ghost_offsets)
    whole_spec = pl.BlockSpec(memory_space=pltpu.VMEM)
    def tiles(value):
        return value.reshape(value.shape[0] // LANES, LANES)

    def fetching(kernel, name, outs, operands, kept):
        here = [pltpu.with_memory_space_constraint(value, pltpu.HBM) for value in operands]
        landing = operands[: len(operands) - kept]
        return call(
            kernel,
            outs + tuple(whole(value.shape, value.dtype) for value in operands[len(landing) :]),
            name,
            [pltpu.VMEM(value.shape, value.dtype) for value in landing]
            + [pltpu.SemaphoreType.DMA((len(operands),))],
            [pl.BlockSpec(memory_space=pltpu.HBM)] * len(operands),
        )(*here)

    own, right, offered, *weights, local, need, send = fetching(
        tables_kernel,
        "tables",
        (
            whole((rows, own_count), f32),
            whole((-(-own_count // GROUP * rows // 16) * 16, GROUP), bf16),
            whole((channels + OFFERED, send_count), bf16),
            whole((4 * QUAD * channels, QUAD * channels), bf16),
            whole((QUAD * channels, QUAD * 4 * bases), bf16),
            whole((QUAD * 2 * bases, QUAD * channels), bf16),
            whole((channels, LANES), f32),
            whole((local_first.shape[0] // LANES, LANES), jnp.int32),
            whole((8, LANES), jnp.int32),
        ),
        (
            positions,
            features,
            species.reshape(1, own_count),
            species_scale.reshape(1, species_scale.shape[0]),
            w_first,
            w_second,
            w_radial.T,
            w_mid,
            w_last,
            w_out.reshape(1, channels),
            tiles(local_first),
            tiles(local_second),
            tiles(local_mask),
            ghost_send.reshape(1, send_count),
        ),
        1,
    )
    from_z = shifted(offered, (0, 0, 1), sizes, 1)

    def scratch(per_step, hots):
        return [pltpu.VMEM((per_step, GROUP, QUAD * CHUNK), bf16) for _ in range(hots)] + [
            pltpu.VMEM((per_step, QUAD, channels, CHUNK), f32),
            pltpu.VMEM((per_step, QUAD, channels, CHUNK), f32),
            pltpu.VMEM((GROUP, LANES), bf16),
        ]

    def cost(slots):
        return pl.CostEstimate(flops=slots * 400000, bytes_accessed=slots * 12, transcendentals=slots * 200)

    quads = local.shape[0] * LANES // (QUAD * CHUNK)
    cuts = [(0, quads // 4), (quads // 4, quads * 2 // 5), (quads * 3 // 5, quads * 4 // 5), (quads * 4 // 5, quads * 9 // 10)]
    beside = (cuts[1][1], cuts[2][0])

    def local_call(part, start, needed, after):
        operands = [local, own, right, *weights, *start, *needed, *after]
        first, end = cuts[part]
        size = end - first
        (sums,) = call(
            functools.partial(
                local_kernel, channels, bases, first, size, (len(start), len(needed), len(after))
            ),
            (whole((groups * 8, GROUP), f32),),
            "local_pairs",
            scratch(size, 2),
            [whole_spec] * len(operands),
            cost(size * QUAD * CHUNK),
        )(*operands)
        return sums

    sums = local_call(0, (), (), ())
    (both,) = call(
        pair_kernel, (whole((2 * offered.shape[0], send_count), bf16),), "two_blocks", specs=[whole_spec] * 3
    )(offered, from_z, sums)
    arrived = [from_z] + [shifted(both, (*step, 0), sizes, 1) for step in PLANAR]
    sums = local_call(1, (sums,), (), (both,))
    ghost_lists = [tiles(value) for value in (ghost_owner, ghost_index, ghost_mask)]
    ghost_step = ghost_owner.shape[0] // (QUAD * CHUNK) // 3
    partner_rows = blocks * GROUP // LANES * 4
    table_rows = -(-blocks * rows // 16) * 16
    force = whole((8, send_count), f32)
    sums, upward, *level = call(
        functools.partial(ghost_kernel, ghost_step, beside, channels, bases),
        (whole((groups * 8, GROUP), f32), whole((8 + 8 * len(PLANAR), send_count), f32)) + (force,) * len(PLANAR),
        "ghost_pairs",
        [
            pltpu.VMEM((table_rows, GROUP), bf16),
            pltpu.VMEM((groups * 4 + partner_rows, GROUP), f32),
            pltpu.VMEM((ghost_owner.shape[0] // LANES, LANES), jnp.int32),
            pltpu.VMEM((8, blocks * GROUP), f32),
        ]
        + scratch(beside[1] - beside[0], 2)
        + scratch(ghost_step, 2),
        [whole_spec] * (11 + len(arrived)),
        cost(ghost_owner.shape[0]),
    )(*ghost_lists, own, *weights, local, right, sums, *arrived)
    upward = shifted(upward, (0, 0, 1), sizes, -1)
    sums = local_call(2, (sums,), (), ())
    mine, *level = call(
        merge_kernel, (force,) * (1 + len(PLANAR)), "forces_upward", specs=[whole_spec] * (2 + len(PLANAR))
    )(upward, *level, sums)
    returned = [shifted(part, (*step, 0), sizes, -1) for part, step in zip(level, PLANAR)]
    sums = local_call(3, (sums,), (need,), (mine,))
    forces, energy = call(
        final_kernel,
        (whole((3, own_count), f32), whole((1, own_count), f32)),
        "totals",
        specs=[whole_spec] * (3 + len(returned)),
    )(sums, send, mine, *returned)
    return forces, energy.reshape(own_count)


def solution(mesh):
    names = ("gx", "gy", "gz")
    sizes = tuple((name, mesh.shape[name]) for name in names)
    split = P(names)
    cols = P(None, names)
    in_specs = (cols, cols, split) + (P(),) * 7 + (split,) * 7
    return jax.shard_map(
        functools.partial(on_device, sizes),
        mesh=mesh,
        in_specs=in_specs,
        out_specs=(cols, split),
        check_vma=False,
    )
```

```python
import functools
import math

import jax
import jax.numpy as jnp
from jax import lax
from jax.experimental import pallas as pl
from jax.experimental.pallas import tpu as pltpu
from jax.sharding import PartitionSpec as P

basis_width = 24.0
domain_edge = 1.0
ghost_offsets = ((1, 0, 0), (0, 1, 0), (0, 0, 1), (1, 1, 0), (1, 0, 1), (0, 1, 1), (1, 1, 1))

PLANAR = ((1, 0), (0, 1), (1, 1))
EXTRA = 8
OFFERED = 16
GROUP = 256
LANES = 128
CHUNK = 256
QUAD = 4
VMEM_LIMIT = 48 * 1024 * 1024

NT = (((1,), (1,)), ((), ()))
f32 = jnp.float32
bf16 = jnp.bfloat16


def dot(left, right):
    return jnp.dot(left, right, preferred_element_type=f32)


def dot_nt(left, right):
    return lax.dot_general(left, right, NT, preferred_element_type=f32)


def iota(shape, dim):
    return lax.broadcasted_iota(jnp.int32, shape, dim)


def one_hot(entry, codes):
    entry = entry.astype(f32)
    entry = jnp.concatenate([entry, entry], 0).astype(bf16)
    entry = jnp.concatenate([entry] * (codes.shape[0] // 16), 0)
    pieces = [
        jnp.where(codes == entry[:, start : start + LANES], bf16(1), bf16(0))
        for start in range(0, entry.shape[1], LANES)
    ]
    return jnp.concatenate(pieces, 1)


def row_codes(count):
    return iota((count, LANES), 0).astype(f32).astype(bf16)


def split_two(value):
    high = value.astype(bf16).astype(f32)
    return high, value - high


def coord_rows(coords, gain):
    high, low = split_two(coords)
    return jnp.concatenate([high, gain, low, jnp.zeros_like(gain)], 0)


def eye(count):
    return (iota((count, count), 0) == iota((count, count), 1)).astype(bf16)


def fetch(sources, targets, landed):
    copies = [
        pltpu.make_async_copy(source, target, landed.at[place])
        for place, (source, target) in enumerate(zip(sources, targets))
    ]
    for copy in copies:
        copy.start()
    for copy in copies:
        copy.wait()


def tables_kernel(*refs):
    own_ref, right_ref, offered_ref, mats_ref, radial_ref, radial_t_ref, out_ref, list_ref, need_ref = refs[14:23]
    send_ref = refs[23]
    landing = refs[24:37]
    fetch(refs[:14], landing + (send_ref,), refs[37])
    positions_ref, features_ref, species_ref, scale_ref, w_first_ref, w_second_ref = landing[:6]
    radial_w_ref, w_mid_ref, w_last_ref, w_out_ref, first_ref, second_ref, mask_ref = landing[6:]
    channels = features_ref.shape[0]
    count = features_ref.shape[1]
    species = species_ref[...]
    gain = jnp.zeros((1, count), f32)
    for kind in range(scale_ref.shape[1]):
        scale = scale_ref[:, kind : kind + 1].astype(f32)
        gain = jnp.where(species == kind, scale, gain)
    positions = positions_ref[...]
    left = dot(w_first_ref[...], features_ref[...]).astype(bf16).astype(f32)
    right = dot(w_second_ref[...], features_ref[...]).astype(bf16).astype(f32)
    own_ref[0:channels, :] = 0.5 * left
    own_ref[channels:, :] = jnp.concatenate([positions, gain, positions, gain], 0)
    column = jnp.concatenate([0.5 * right, coord_rows(positions, gain)], 0)
    groups = count // GROUP
    rows = channels + EXTRA
    table = jnp.concatenate([column[:, group * GROUP : (group + 1) * GROUP] for group in range(groups)], 0)
    spare = right_ref.shape[0] - groups * rows
    if spare:
        table = jnp.concatenate([table, jnp.zeros((spare, GROUP), f32)], 0)
    table = table.astype(bf16)
    right_ref[...] = table
    send = jnp.broadcast_to(send_ref[...], (8, send_ref.shape[1]))
    picked = dot(table, one_hot(send & (GROUP - 1), row_codes(GROUP)))
    chosen = group_pick(picked, send // GROUP, rows, groups)
    chosen = jnp.concatenate([chosen, jnp.zeros((OFFERED - EXTRA, chosen.shape[1]), f32)], 0)
    offered_ref[...] = chosen.astype(bf16)

    unit = eye(channels)
    w_mid = w_mid_ref[...]
    w_last = w_last_ref[...]
    last_t = dot_nt(unit, w_last).astype(bf16)
    mid_t = dot_nt(unit, w_mid).astype(bf16)
    wide = QUAD * channels
    for place, matrix in enumerate((w_mid, w_last, last_t, mid_t)):
        mats_ref[place * wide : (place + 1) * wide, :] = (0.5 * diagonal_copies(matrix)).astype(bf16)
    bases = radial_w_ref.shape[0]
    high, low = split_two(radial_w_ref[...])
    high = high.astype(bf16)
    low = low.astype(bf16)
    spread = dot_nt(unit, jnp.concatenate([high, high, low, low], 0)).astype(bf16)
    radial_ref[...] = (0.5 * diagonal_copies(spread)).astype(bf16)
    radial_t_ref[...] = diagonal_copies(jnp.concatenate([high, low], 0)).astype(bf16)
    w_out = w_out_ref[...]
    diagonal = jnp.where(iota((channels, channels), 0) == iota((channels, channels), 1), w_out, 0.0)
    out_ref[...] = jnp.broadcast_to(jnp.sum(diagonal, axis=1, keepdims=True), (channels, LANES))
    bits = (count - 1).bit_length()
    codes = pack(first_ref[...], second_ref[...], mask_ref[...], bits)
    live = [codes[start : start + 8] & 1 for start in range(0, codes.shape[0], 8)]
    need_ref[...] = gather_live(codes, live, 2 * bits + 1, list_ref)


def pack(owner, partner, mask, partner_bits):
    return (owner * 2**partner_bits + partner) * 2 + mask


def gather_live(codes, live, bits, list_ref):
    tiles = len(live)
    sub = iota((8, LANES), 0)
    passed = jnp.zeros((8, LANES), jnp.int32)
    words = []
    for tile in range(tiles):
        dead = 1 - live[tile]
        for step in (1, 2, 4):
            dead = dead + jnp.where(sub >= step, pltpu.roll(dead, step, 0), 0)
        move = (passed + dead) * 2**bits + codes[tile * 8 : tile * 8 + 8]
        words.append(jnp.where(live[tile] != 0, move, 0))
        passed = passed + jnp.broadcast_to(dead[7:8], (8, LANES))
    none = jnp.zeros((8, LANES), jnp.int32)
    for power in range((tiles * 8).bit_length()):
        step = 2**power
        moving = [jnp.where((word & 2 ** (bits + power)) != 0, word, 0) for word in words]
        if step < 8:
            rolled = [pltpu.roll(word, 8 - step, 0) for word in moving] + [none]
            come = [jnp.where(sub < 8 - step, rolled[tile], rolled[tile + 1]) for tile in range(tiles)]
        else:
            come = (moving[step // 8 :] + [none] * tiles)[:tiles]
        words = [word - gone + new for word, gone, new in zip(words, moving, come)]
    for tile, word in enumerate(words):
        list_ref[tile * 8 : tile * 8 + 8, :] = word & (2**bits - 1)
    return tiles * 8 - passed


def diagonal_copies(matrix):
    high, wide = matrix.shape
    repeat = (iota((wide, QUAD * wide), 0) == iota((wide, QUAD * wide), 1) % wide).astype(bf16)
    row = dot(matrix, repeat)
    full = jnp.concatenate([row] * QUAD, 0)
    return jnp.where(iota(full.shape, 0) // high == iota(full.shape, 1) // wide, full, 0.0)


def group_pick(values, high, rows, groups):
    high = jnp.concatenate([high] * (rows // 8), 0)
    chosen = values[:rows]
    for group in range(1, groups):
        chosen = jnp.where(high == group, values[group * rows : (group + 1) * rows], chosen)
    return chosen


def spread_groups(values, high, groups):
    second = iota(values.shape, 0) // 4
    pieces = [jnp.where(high == second + group, values, 0.0) for group in range(0, groups, 2)]
    return jnp.concatenate(pieces, 0)


def lane_pick(table_ref, place, first=0):
    rows, count = table_ref.shape[0] - first, table_ref.shape[1]
    lane = jnp.concatenate([place & (LANES - 1)] * (rows // 8), 0)
    high = jnp.concatenate([place // LANES] * (rows // 8), 0)
    chosen = None
    for group in range(count // LANES):
        part = table_ref[first:, group * LANES : (group + 1) * LANES]
        picked = jnp.take_along_axis(part, lane, axis=1, mode="promise_in_bounds")
        chosen = picked if chosen is None else jnp.where(high == group, picked, chosen)
    return chosen


def sum_rows(values, steps):
    for step in steps:
        values = values + pltpu.roll(values, step, 0)
    return values


def pair_tasks(
    own_groups,
    partner_groups,
    channels,
    bases,
    list_ref,
    own_ref,
    right_ref,
    mats_ref,
    radial_ref,
    radial_t_ref,
    out_ref,
    sums,
    hot,
    hot_wide,
    slope_one,
    slope_two,
    codes_ref,
):
    rows = channels + EXTRA
    line = CHUNK // LANES
    block = QUAD * line
    wide = QUAD * channels
    w_out = jnp.concatenate([out_ref[...]] * line, 1)
    centers = iota((bases, CHUNK), 0).astype(f32) * (1.0 / (bases - 1))
    last = iota((8, CHUNK), 0) % 4 == 3
    partner_bits = (partner_groups * LANES - 1).bit_length()
    quads = range(QUAD)
    codes_ref[...] = row_codes(GROUP)

    def matrix(place):
        return mats_ref[place * wide : (place + 1) * wide, :]

    def part(values, number, size=channels):
        return values[number * size : (number + 1) * size]

    def silu_pair(half):
        grow = jnp.tanh(half)
        plus = 1.0 + grow
        hidden = half * plus
        return hidden, plus + hidden * (1.0 - grow)

    def task(first, number):
        at = pl.multiple_of(first * block, block)
        code_rows = list_ref[pl.ds(at, block), :]
        owners, partners, lives, projected, shifts, squares, weights, stacks, slopes = ([] for _ in range(9))
        for quad in quads:
            cols = slice(quad * CHUNK, (quad + 1) * CHUNK)
            code = jnp.concatenate(
                [
                    jnp.broadcast_to(code_rows[row : row + 1, :], (8, LANES))
                    for row in range(quad * line, (quad + 1) * line)
                ],
                1,
            )
            lives.append((code & 1).astype(f32))
            partner = (code >> 1) & (2**partner_bits - 1)
            owner = code >> (partner_bits + 1)
            owners.append(owner)
            partners.append(partner)
            hot[number, 0:LANES, cols] = one_hot(owner & (LANES - 1), codes_ref[0:LANES, :])
            wide = one_hot(partner & (GROUP - 1), codes_ref[...])
            hot_wide[number, :, cols] = wide
            hot[number, LANES:, cols] = wide[0:LANES] + wide[LANES:]
            yield
        for quad in quads:
            cols = slice(quad * CHUNK, (quad + 1) * CHUNK)
            own_vals = jnp.concatenate(
                [lane_pick(own_ref, owners[quad][:, start : start + LANES]) for start in range(0, CHUNK, LANES)], 1
            )
            partner_vals = group_pick(
                dot(right_ref[...], hot_wide[number, :, cols]),
                partners[quad] // GROUP,
                rows,
                partner_groups * LANES // GROUP,
            )
            projected.append(own_vals[:channels] + partner_vals[:channels])
            own_coords = own_vals[channels:]
            extra = partner_vals[channels:]
            partner_coords = extra + pltpu.roll(extra, 4, 0)
            shift = partner_coords - own_coords
            squared = sum_rows(jnp.where(last, 0.0, shift * shift), (2, 1))
            gain = sum_rows(jnp.where(last, own_coords * partner_coords, 0.0), (2, 1))
            weights.append(lives[quad] * gain)
            away = squared - centers
            basis = jnp.exp(-basis_width * (away * away))
            basis_high, basis_low = split_two(basis)
            stacks.append(jnp.concatenate([basis_high, basis_low, basis_high, basis_low], 0).astype(bf16))
            slopes.append((-2.0 * basis_width) * away * basis)
            shifts.append(shift)
            squares.append(squared)
            yield
        radial = dot(radial_ref[...], jnp.concatenate(stacks, 0))
        yield
        pieces = []
        for quad in quads:
            hidden, slope_one[number, quad] = silu_pair(projected[quad] + part(radial, quad))
            pieces.append(hidden.astype(bf16))
        yield
        half = dot(matrix(0), jnp.concatenate(pieces, 0))
        yield
        pieces = []
        for quad in quads:
            hidden, slope_two[number, quad] = silu_pair(part(half, quad))
            pieces.append(hidden.astype(bf16))
        yield
        half = dot(matrix(1), jnp.concatenate(pieces, 0))
        yield
        pieces = []
        readouts = []
        for quad in quads:
            hidden, slope = silu_pair(part(half, quad))
            terms = w_out * hidden
            terms = sum(terms[start : start + 8] for start in range(8, channels, 8)) + terms[:8]
            readouts.append(sum_rows(terms, (4, 2, 1)))
            pieces.append(((0.5 * w_out) * slope).astype(bf16))
        yield
        back = dot(matrix(2), jnp.concatenate(pieces, 0))
        yield
        pieces = [(part(back, quad) * slope_two[number, quad]).astype(bf16) for quad in quads]
        back = dot(matrix(3), jnp.concatenate(pieces, 0))
        yield
        pieces = [(part(back, quad) * slope_one[number, quad]).astype(bf16) for quad in quads]
        back = dot(radial_t_ref[...], jnp.concatenate(pieces, 0))
        yield
        parts = []
        for quad in quads:
            two = part(back, quad, 2 * bases)
            readout_slope = sum_rows((two[:bases] + two[bases:]) * slopes[quad], (4, 2, 1))
            near = jnp.maximum(1.0 - squares[quad], 0.0)
            weight_near = weights[quad] * near
            energy = weight_near * near * readouts[quad]
            slope = weight_near * (near * readout_slope - 2.0 * readouts[quad])
            push = (2.0 * slope) * shifts[quad]
            values = jnp.where(last, energy, push)
            parts.append(
                jnp.concatenate(
                    [
                        spread_groups(values, owners[quad] // LANES, own_groups),
                        spread_groups(values, partners[quad] // LANES, partner_groups),
                    ],
                    0,
                ).astype(bf16)
            )
        yield
        sums[...] += dot_nt(jnp.concatenate(parts, 1), hot[number])

    return task


def run(tasks):
    running, waiting = [], list(tasks)
    while running or waiting:
        if waiting:
            running.append(waiting.pop(0))
        for _ in range(2):
            running = [task for task in running if next(task, task) is not task]


def run_rest(task, done, rest):
    steps, size = rest

    def step(index, unused):
        run([task(done + index * size + number, number) for number in range(size)])
        return unused

    lax.fori_loop(0, steps, step, 0)


def fold(list_ref, source, target, turns):
    rows = slice(target * 8, target * 8 + 8)
    spare = slice(source * 8, source * 8 + 8)
    kept = list_ref[rows, :]
    moving = pltpu.roll(list_ref[spare, :], 4, 0)
    for turn in range(turns):
        moving = pltpu.roll(moving, 1, 1)
        if turn % 4 == 3:
            moving = pltpu.roll(moving, 3, 0)
        placed = jnp.where(kept == 0, moving, 0)
        kept = kept + placed
        moving = moving - placed
    list_ref[rows, :] = kept
    list_ref[spare, :] = moving


def rest_of(list_ref, need, done, total):
    left = total - done
    size = next(size for size in (3, 2, 1) if left % size == 0)
    rows = QUAD * CHUNK // LANES
    found = jnp.max(list_ref[done * rows : total * rows, :])
    steps = jnp.maximum(jnp.max(need) - done * rows + size * rows - 1, 0) // (size * rows)
    return jnp.where(found > 0, steps, 0), size


def local_kernel(channels, bases, first_quad, quad_count, counts, *refs):
    count = 7 + sum(counts)
    codes, own, right, *weights = refs[:7]
    sums, hot, *scratch = refs[count:]
    sums[...] = refs[7][...] if counts[0] else jnp.zeros_like(sums)
    groups = own.shape[1] // LANES
    if counts[1]:
        tail, *scratch = scratch
        tile = QUAD * CHUNK // LANES // 8
        tail[...] = codes[...]
        fold(tail, (first_quad + quad_count) * tile, (first_quad + quad_count) * tile - 1, 12)
        fold(tail, (first_quad + quad_count) * tile + 1, (first_quad + quad_count) * tile - 1, 8)
        codes = tail
    task = pair_tasks(groups, groups, channels, bases, codes, own, right, *weights, sums, hot, *scratch)
    run([task(first_quad + number, number) for number in range(quad_count)])
    if counts[1]:
        done = first_quad + quad_count
        total = codes.shape[0] * LANES // (QUAD * CHUNK)
        run_rest(task, done, rest_of(codes, refs[7 + counts[0]][...], done, total))


def near_ones(codes, bits, own_ref, channels, coords_ref):
    sub = iota((8, LANES), 0)
    found = []
    for start in range(0, codes.shape[0], 8):
        tile = codes[start : start + 8]
        squared = jnp.zeros((8, LANES), f32)
        for low in range(4):
            code = jnp.where(
                sub < 4,
                jnp.broadcast_to(tile[low : low + 1], (8, LANES)),
                jnp.broadcast_to(tile[low + 4 : low + 5], (8, LANES)),
            )
            shift = lane_pick(coords_ref, (code >> 1) & (2**bits - 1)) - lane_pick(own_ref, code >> (bits + 1), channels)
            square = shift * shift
            total = square + pltpu.roll(square, 7, 0) + pltpu.roll(square, 6, 0)
            if low:
                total = pltpu.roll(total, low, 0)
            squared = jnp.where(sub % 4 == low, total, squared)
        found.append(jnp.where(squared < 1.001, tile & 1, 0))
    return found


def ghost_kernel(quad_count, channels, bases, *refs):
    blocks = len(ghost_offsets)
    owner, partner, mask, own, *weights = refs[:8]
    sums_in = refs[8]
    arrived = refs[9 : 10 + len(PLANAR)]
    sums_out, upward, *level = refs[10 + len(PLANAR) : 12 + 2 * len(PLANAR)]
    table, sums, codes_ref, coords_ref, *scratch = refs[12 + 2 * len(PLANAR) :]
    groups = own.shape[1] // LANES
    partner_groups = blocks * GROUP // LANES
    sums[...] = jnp.zeros_like(sums)
    pieces = []
    for offset in ghost_offsets:
        if offset[:2] == (0, 0):
            source, start = arrived[0], 0
        else:
            source, start = arrived[1 + PLANAR.index(offset[:2])], offset[2] * (channels + OFFERED)
        extra = source[start + channels : start + channels + OFFERED, :].astype(f32)
        moved = jnp.concatenate(
            [extra[axis : axis + 1] + extra[axis + 4 : axis + 5] + domain_edge * offset[axis] for axis in range(3)], 0
        )
        pieces += [source[start : start + channels, :].astype(f32), coord_rows(moved, extra[3:4])]
        place = ghost_offsets.index(offset) * GROUP
        coords_ref[:, place : place + GROUP] = jnp.concatenate([moved, extra[3:4], moved, extra[3:4]], 0)
    pieces.append(jnp.zeros((table.shape[0] - blocks * (channels + EXTRA), GROUP), f32))
    table[...] = jnp.concatenate(pieces, 0).astype(bf16)
    bits = (partner_groups * LANES - 1).bit_length()
    codes = pack(owner[...], partner[...], mask[...], bits)
    live = near_ones(codes, bits, own, channels, coords_ref)
    need = gather_live(codes, live, bits + (own.shape[1] - 1).bit_length() + 1, codes_ref)
    tile = quad_count * QUAD * CHUNK // LANES // 8
    fold(codes_ref, tile, tile - 1, 8)
    task = pair_tasks(groups, partner_groups, channels, bases, codes_ref, own, table, *weights, sums, *scratch)
    run([task(number, number) for number in range(quad_count)])
    total = owner.shape[0] * LANES // (QUAD * CHUNK)
    run_rest(task, quad_count, rest_of(codes_ref, need, quad_count, total))
    first = groups * 4
    sums_out[0:first, :] = sums_in[0:first, :] + sums[0:first, :]
    sums_out[first:, :] = sums_in[first:, :]
    for block, offset in enumerate(ghost_offsets):
        halves = []
        for half in range(GROUP // LANES):
            start = first + (block * (GROUP // LANES) + half) * 4
            halves.append(sums[start : start + 4, LANES:])
        force = -jnp.concatenate(halves, 1)
        force = jnp.concatenate([force, jnp.zeros_like(force)], 0)
        if offset[2]:
            place = 0 if offset[:2] == (0, 0) else 1 + PLANAR.index(offset[:2])
            upward[place * 8 : place * 8 + 8, :] = force
        else:
            level[PLANAR.index(offset[:2])][...] = force


def pair_kernel(offered_ref, from_z_ref, unused_ref, both_ref):
    count = offered_ref.shape[0]
    both_ref[0:count, :] = offered_ref[...]
    both_ref[count:, :] = from_z_ref[...]


def merge_kernel(*refs):
    upward, *level = refs[: 1 + len(PLANAR)]
    outs = refs[2 + len(PLANAR) :]
    outs[0][...] = upward[0:8, :]
    for place, part in enumerate(level):
        outs[1 + place][...] = part[...] + upward[8 * place + 8 : 8 * place + 16, :]


def final_kernel(*refs):
    sums_ref, send_ref, *arrived = refs[:-2]
    forces_ref, energy_ref = refs[-2:]
    incoming = arrived[0][...]
    for part in arrived[1:]:
        incoming = incoming + part[...]
    high, low = split_two(jnp.concatenate([incoming[:4], incoming[:4]], 0))
    send = jnp.broadcast_to(send_ref[...], (8, send_ref.shape[1]))
    groups = sums_ref.shape[0] // 8
    hot = one_hot(send & (LANES - 1), row_codes(LANES))
    spread = [spread_groups(value, send // LANES, groups).astype(bf16) for value in (high, low)]
    back = dot_nt(jnp.concatenate(spread, 0), hot)
    back = back[: groups * 4] + back[groups * 4 :]
    for group in range(groups):
        own = sums_ref[group * 4 : group * 4 + 4, 0:LANES]
        partner = sums_ref[(groups + group) * 4 : (groups + group) * 4 + 4, LANES:]
        total = own - partner + back[group * 4 : group * 4 + 4]
        cols = slice(group * LANES, (group + 1) * LANES)
        forces_ref[:, cols] = total[0:3]
        energy_ref[:, cols] = own[3:4]


def whole(shape, dtype):
    return jax.ShapeDtypeStruct(shape, dtype)


def call(kernel, outs, name, scratch=(), specs=None, cost=None):
    more = {} if cost is None else dict(cost_estimate=cost)
    return pl.pallas_call(
        kernel,
        grid=(1,),
        in_specs=specs,
        out_specs=tuple(pl.BlockSpec(memory_space=pltpu.VMEM) for _ in outs),
        out_shape=outs,
        scratch_shapes=list(scratch),
        compiler_params=pltpu.CompilerParams(vmem_limit_bytes=VMEM_LIMIT),
        name=name,
        **more,
    )


def shifted(value, offset, sizes, sign):
    used = tuple(axis for axis, step in zip(sizes, offset) if step)
    dims = [size for name, size in used]
    pairs = []
    for flat in range(math.prod(dims)):
        place, rest = [], flat
        for size in reversed(dims):
            place.insert(0, rest % size)
            rest //= size
        target = 0
        for at, size in zip(place, dims):
            target = target * size + (at - sign) % size
        pairs.append((flat, target))
    return lax.ppermute(value, tuple(name for name, size in used), pairs)


def on_device(
    sizes,
    positions,
    features,
    species,
    species_scale,
    w_first,
    w_second,
    w_radial,
    w_mid,
    w_last,
    w_out,
    ghost_send,
    local_first,
    local_second,
    local_mask,
    ghost_owner,
    ghost_index,
    ghost_mask,
):
    channels, own_count = features.shape
    send_count = ghost_send.shape[0]
    bases = w_radial.shape[1]
    rows = channels + EXTRA
    groups = own_count // LANES
    blocks = len(ghost_offsets)
    whole_spec = pl.BlockSpec(memory_space=pltpu.VMEM)
    def tiles(value):
        return value.reshape(value.shape[0] // LANES, LANES)

    def fetching(kernel, name, outs, operands, kept):
        here = [pltpu.with_memory_space_constraint(value, pltpu.HBM) for value in operands]
        landing = operands[: len(operands) - kept]
        return call(
            kernel,
            outs + tuple(whole(value.shape, value.dtype) for value in operands[len(landing) :]),
            name,
            [pltpu.VMEM(value.shape, value.dtype) for value in landing]
            + [pltpu.SemaphoreType.DMA((len(operands),))],
            [pl.BlockSpec(memory_space=pltpu.HBM)] * len(operands),
        )(*here)

    own, right, offered, *weights, local, need, send = fetching(
        tables_kernel,
        "tables",
        (
            whole((rows, own_count), f32),
            whole((-(-own_count // GROUP * rows // 16) * 16, GROUP), bf16),
            whole((channels + OFFERED, send_count), bf16),
            whole((4 * QUAD * channels, QUAD * channels), bf16),
            whole((QUAD * channels, QUAD * 4 * bases), bf16),
            whole((QUAD * 2 * bases, QUAD * channels), bf16),
            whole((channels, LANES), f32),
            whole((local_first.shape[0] // LANES, LANES), jnp.int32),
            whole((8, LANES), jnp.int32),
        ),
        (
            positions,
            features,
            species.reshape(1, own_count),
            species_scale.reshape(1, species_scale.shape[0]),
            w_first,
            w_second,
            w_radial.T,
            w_mid,
            w_last,
            w_out.reshape(1, channels),
            tiles(local_first),
            tiles(local_second),
            tiles(local_mask),
            ghost_send.reshape(1, send_count),
        ),
        1,
    )
    from_z = shifted(offered, (0, 0, 1), sizes, 1)

    def scratch(per_step, hots, more=()):
        hot = [pltpu.VMEM((per_step, GROUP, QUAD * CHUNK), bf16) for _ in range(hots)]
        return hot[:1] + list(more) + hot[1:] + [
            pltpu.VMEM((per_step, QUAD, channels, CHUNK), f32),
            pltpu.VMEM((per_step, QUAD, channels, CHUNK), f32),
            pltpu.VMEM((GROUP, LANES), bf16),
        ]

    def cost(slots):
        return pl.CostEstimate(flops=slots * 400000, bytes_accessed=slots * 12, transcendentals=slots * 200)

    quads = local.shape[0] * LANES // (QUAD * CHUNK)
    cuts = [0, quads // 4, quads * 2 // 5, quads * 13 // 20, quads * 4 // 5]

    def local_call(part, start, needed, after):
        operands = [local, own, right, *weights, *start, *needed, *after]
        first = cuts[part]
        size = cuts[part + 1] - first
        (sums,) = call(
            functools.partial(
                local_kernel, channels, bases, first, size, (len(start), len(needed), len(after))
            ),
            (whole((groups * 8, GROUP), f32),),
            "local_pairs",
            scratch(size, 2, [pltpu.VMEM(local.shape, local.dtype)] if needed else []),
            [whole_spec] * len(operands),
            cost(size * QUAD * CHUNK),
        )(*operands)
        return sums

    sums = local_call(0, (), (), ())
    (both,) = call(
        pair_kernel, (whole((2 * offered.shape[0], send_count), bf16),), "two_blocks", specs=[whole_spec] * 3
    )(offered, from_z, sums)
    arrived = [from_z] + [shifted(both, (*step, 0), sizes, 1) for step in PLANAR]
    sums = local_call(1, (sums,), (), (both,))
    ghost_lists = [tiles(value) for value in (ghost_owner, ghost_index, ghost_mask)]
    ghost_step = ghost_owner.shape[0] // (QUAD * CHUNK) // 4
    partner_rows = blocks * GROUP // LANES * 4
    table_rows = -(-blocks * rows // 16) * 16
    force = whole((8, send_count), f32)
    sums, upward, *level = call(
        functools.partial(ghost_kernel, ghost_step, channels, bases),
        (whole((groups * 8, GROUP), f32), whole((8 + 8 * len(PLANAR), send_count), f32)) + (force,) * len(PLANAR),
        "ghost_pairs",
        [
            pltpu.VMEM((table_rows, GROUP), bf16),
            pltpu.VMEM((groups * 4 + partner_rows, GROUP), f32),
            pltpu.VMEM((ghost_owner.shape[0] // LANES, LANES), jnp.int32),
            pltpu.VMEM((8, blocks * GROUP), f32),
        ]
        + scratch(ghost_step, 2),
        [whole_spec] * (9 + len(arrived)),
        cost(ghost_owner.shape[0]),
    )(*ghost_lists, own, *weights, sums, *arrived)
    upward = shifted(upward, (0, 0, 1), sizes, -1)
    sums = local_call(2, (sums,), (), ())
    mine, *level = call(
        merge_kernel, (force,) * (1 + len(PLANAR)), "forces_upward", specs=[whole_spec] * (2 + len(PLANAR))
    )(upward, *level, sums)
    returned = [shifted(part, (*step, 0), sizes, -1) for part, step in zip(level, PLANAR)]
    sums = local_call(3, (sums,), (need,), (mine,))
    forces, energy = call(
        final_kernel,
        (whole((3, own_count), f32), whole((1, own_count), f32)),
        "totals",
        specs=[whole_spec] * (3 + len(returned)),
    )(sums, send, mine, *returned)
    return forces, energy.reshape(own_count)


def solution(mesh):
    names = ("gx", "gy", "gz")
    sizes = tuple((name, mesh.shape[name]) for name in names)
    split = P(names)
    cols = P(None, names)
    in_specs = (cols, cols, split) + (P(),) * 7 + (split,) * 7
    return jax.shard_map(
        functools.partial(on_device, sizes),
        mesh=mesh,
        in_specs=in_specs,
        out_specs=(cols, split),
        check_vma=False,
    )
```

```python
import functools
import math

import jax
import jax.numpy as jnp
from jax import lax
from jax.experimental import pallas as pl
from jax.experimental.pallas import tpu as pltpu
from jax.sharding import PartitionSpec as P

basis_width = 24.0
domain_edge = 1.0
ghost_offsets = ((1, 0, 0), (0, 1, 0), (0, 0, 1), (1, 1, 0), (1, 0, 1), (0, 1, 1), (1, 1, 1))

PLANAR = ((1, 0), (0, 1), (1, 1))
EXTRA = 8
OFFERED = 16
GROUP = 256
LANES = 128
CHUNK = 256
QUAD = 4
VMEM_LIMIT = 48 * 1024 * 1024

NT = (((1,), (1,)), ((), ()))
f32 = jnp.float32
bf16 = jnp.bfloat16


def dot(left, right):
    return jnp.dot(left, right, preferred_element_type=f32)


def dot_nt(left, right):
    return lax.dot_general(left, right, NT, preferred_element_type=f32)


def iota(shape, dim):
    return lax.broadcasted_iota(jnp.int32, shape, dim)


def one_hot(entry, codes):
    entry = entry.astype(f32)
    entry = jnp.concatenate([entry, entry], 0).astype(bf16)
    entry = jnp.concatenate([entry] * (codes.shape[0] // 16), 0)
    pieces = [
        jnp.where(codes == entry[:, start : start + LANES], bf16(1), bf16(0))
        for start in range(0, entry.shape[1], LANES)
    ]
    return jnp.concatenate(pieces, 1)


def row_codes(count):
    return iota((count, LANES), 0).astype(f32).astype(bf16)


def split_two(value):
    high = value.astype(bf16).astype(f32)
    return high, value - high


def coord_rows(coords, gain):
    high, low = split_two(coords)
    return jnp.concatenate([high, gain, low, jnp.zeros_like(gain)], 0)


def eye(count):
    return (iota((count, count), 0) == iota((count, count), 1)).astype(bf16)


def fetch(sources, targets, landed):
    copies = [
        pltpu.make_async_copy(source, target, landed.at[place])
        for place, (source, target) in enumerate(zip(sources, targets))
    ]
    for copy in copies:
        copy.start()
    for copy in copies:
        copy.wait()


def tables_kernel(*refs):
    own_ref, right_ref, offered_ref, mats_ref, radial_ref, radial_t_ref, out_ref, list_ref, need_ref = refs[14:23]
    send_ref = refs[23]
    landing = refs[24:37]
    fetch(refs[:14], landing + (send_ref,), refs[37])
    positions_ref, features_ref, species_ref, scale_ref, w_first_ref, w_second_ref = landing[:6]
    radial_w_ref, w_mid_ref, w_last_ref, w_out_ref, first_ref, second_ref, mask_ref = landing[6:]
    channels = features_ref.shape[0]
    count = features_ref.shape[1]
    species = species_ref[...]
    gain = jnp.zeros((1, count), f32)
    for kind in range(scale_ref.shape[1]):
        scale = scale_ref[:, kind : kind + 1].astype(f32)
        gain = jnp.where(species == kind, scale, gain)
    positions = positions_ref[...]
    left = dot(w_first_ref[...], features_ref[...]).astype(bf16).astype(f32)
    right = dot(w_second_ref[...], features_ref[...]).astype(bf16).astype(f32)
    own_ref[0:channels, :] = 0.5 * left
    own_ref[channels:, :] = jnp.concatenate([positions, gain, positions, gain], 0)
    column = jnp.concatenate([0.5 * right, coord_rows(positions, gain)], 0)
    groups = count // GROUP
    rows = channels + EXTRA
    table = jnp.concatenate([column[:, group * GROUP : (group + 1) * GROUP] for group in range(groups)], 0)
    spare = right_ref.shape[0] - groups * rows
    if spare:
        table = jnp.concatenate([table, jnp.zeros((spare, GROUP), f32)], 0)
    table = table.astype(bf16)
    right_ref[...] = table
    send = jnp.broadcast_to(send_ref[...], (8, send_ref.shape[1]))
    picked = dot(table, one_hot(send & (GROUP - 1), row_codes(GROUP)))
    chosen = group_pick(picked, send // GROUP, rows, groups)
    chosen = jnp.concatenate([chosen, jnp.zeros((OFFERED - EXTRA, chosen.shape[1]), f32)], 0)
    offered_ref[...] = chosen.astype(bf16)

    unit = eye(channels)
    w_mid = w_mid_ref[...]
    w_last = w_last_ref[...]
    last_t = dot_nt(unit, w_last).astype(bf16)
    mid_t = dot_nt(unit, w_mid).astype(bf16)
    wide = QUAD * channels
    for place, matrix in enumerate((w_mid, w_last, last_t, mid_t)):
        mats_ref[place * wide : (place + 1) * wide, :] = (0.5 * diagonal_copies(matrix)).astype(bf16)
    bases = radial_w_ref.shape[0]
    high, low = split_two(radial_w_ref[...])
    high = high.astype(bf16)
    low = low.astype(bf16)
    spread = dot_nt(unit, jnp.concatenate([high, high, low, low], 0)).astype(bf16)
    radial_ref[...] = (0.5 * diagonal_copies(spread)).astype(bf16)
    radial_t_ref[...] = diagonal_copies(jnp.concatenate([high, low], 0)).astype(bf16)
    w_out = w_out_ref[...]
    diagonal = jnp.where(iota((channels, channels), 0) == iota((channels, channels), 1), w_out, 0.0)
    out_ref[...] = jnp.broadcast_to(jnp.sum(diagonal, axis=1, keepdims=True), (channels, LANES))
    bits = (count - 1).bit_length()
    codes = pack(first_ref[...], second_ref[...], mask_ref[...], bits)
    live = [codes[start : start + 8] & 1 for start in range(0, codes.shape[0], 8)]
    need_ref[...] = gather_live(codes, live, 2 * bits + 1, list_ref)


def pack(owner, partner, mask, partner_bits):
    return (owner * 2**partner_bits + partner) * 2 + mask


def gather_live(codes, live, bits, list_ref):
    tiles = len(live)
    sub = iota((8, LANES), 0)
    passed = jnp.zeros((8, LANES), jnp.int32)
    words = []
    for tile in range(tiles):
        dead = 1 - live[tile]
        for step in (1, 2, 4):
            dead = dead + jnp.where(sub >= step, pltpu.roll(dead, step, 0), 0)
        move = (passed + dead) * 2**bits + codes[tile * 8 : tile * 8 + 8]
        words.append(jnp.where(live[tile] != 0, move, 0))
        passed = passed + jnp.broadcast_to(dead[7:8], (8, LANES))
    none = jnp.zeros((8, LANES), jnp.int32)
    for power in range((tiles * 8).bit_length()):
        step = 2**power
        moving = [jnp.where((word & 2 ** (bits + power)) != 0, word, 0) for word in words]
        if step < 8:
            rolled = [pltpu.roll(word, 8 - step, 0) for word in moving] + [none]
            come = [jnp.where(sub < 8 - step, rolled[tile], rolled[tile + 1]) for tile in range(tiles)]
        else:
            come = (moving[step // 8 :] + [none] * tiles)[:tiles]
        words = [word - gone + new for word, gone, new in zip(words, moving, come)]
    for tile, word in enumerate(words):
        list_ref[tile * 8 : tile * 8 + 8, :] = word & (2**bits - 1)
    return tiles * 8 - passed


def diagonal_copies(matrix):
    high, wide = matrix.shape
    repeat = (iota((wide, QUAD * wide), 0) == iota((wide, QUAD * wide), 1) % wide).astype(bf16)
    row = dot(matrix, repeat)
    full = jnp.concatenate([row] * QUAD, 0)
    return jnp.where(iota(full.shape, 0) // high == iota(full.shape, 1) // wide, full, 0.0)


def group_pick(values, high, rows, groups):
    high = jnp.concatenate([high] * (rows // 8), 0)
    chosen = values[:rows]
    for group in range(1, groups):
        chosen = jnp.where(high == group, values[group * rows : (group + 1) * rows], chosen)
    return chosen


def spread_groups(values, high, groups):
    second = iota(values.shape, 0) // 4
    pieces = [jnp.where(high == second + group, values, 0.0) for group in range(0, groups, 2)]
    return jnp.concatenate(pieces, 0)


def lane_pick(table_ref, place, first=0):
    rows, count = table_ref.shape[0] - first, table_ref.shape[1]
    lane = jnp.concatenate([place & (LANES - 1)] * (rows // 8), 0)
    high = jnp.concatenate([place // LANES] * (rows // 8), 0)
    chosen = None
    for group in range(count // LANES):
        part = table_ref[first:, group * LANES : (group + 1) * LANES]
        picked = jnp.take_along_axis(part, lane, axis=1, mode="promise_in_bounds")
        chosen = picked if chosen is None else jnp.where(high == group, picked, chosen)
    return chosen


def sum_rows(values, steps):
    for step in steps:
        values = values + pltpu.roll(values, step, 0)
    return values


def pair_tasks(
    own_groups,
    partner_groups,
    channels,
    bases,
    list_ref,
    own_ref,
    right_ref,
    mats_ref,
    radial_ref,
    radial_t_ref,
    out_ref,
    sums,
    hot,
    hot_wide,
    slope_one,
    slope_two,
    codes_ref,
):
    rows = channels + EXTRA
    line = CHUNK // LANES
    block = QUAD * line
    wide = QUAD * channels
    w_out = jnp.concatenate([out_ref[...]] * line, 1)
    w_out_half = (0.5 * w_out).astype(bf16)
    centers = iota((bases, CHUNK), 0).astype(f32) * (1.0 / (bases - 1))
    last = iota((8, CHUNK), 0) % 4 == 3
    partner_bits = (partner_groups * LANES - 1).bit_length()
    quads = range(QUAD)
    codes_ref[...] = row_codes(GROUP)

    def matrix(place):
        return mats_ref[place * wide : (place + 1) * wide, :]

    def part(values, number, size=channels):
        return values[number * size : (number + 1) * size]

    def silu_pair(half):
        grow = jnp.tanh(half)
        hidden = half * (1 + grow)
        grow = grow.astype(bf16)
        rounded = hidden.astype(bf16)
        return hidden, rounded, (1 + grow) + rounded * (1 - grow)

    def task(first, number, source=list_ref):
        at = pl.multiple_of(first * block, block)
        code_rows = source[pl.ds(at, block), :]
        owners, partners, lives, projected, shifts, squares, weights, stacks, slopes = ([] for _ in range(9))
        for quad in quads:
            cols = slice(quad * CHUNK, (quad + 1) * CHUNK)
            code = jnp.concatenate(
                [
                    jnp.broadcast_to(code_rows[row : row + 1, :], (8, LANES))
                    for row in range(quad * line, (quad + 1) * line)
                ],
                1,
            )
            lives.append((code & 1).astype(f32))
            partner = (code >> 1) & (2**partner_bits - 1)
            owner = code >> (partner_bits + 1)
            owners.append(owner)
            partners.append(partner)
            hot[number, 0:LANES, cols] = one_hot(owner & (LANES - 1), codes_ref[0:LANES, :])
            wide = one_hot(partner & (GROUP - 1), codes_ref[...])
            hot_wide[number, :, cols] = wide
            hot[number, LANES:, cols] = wide[0:LANES] + wide[LANES:]
            yield
        for quad in quads:
            cols = slice(quad * CHUNK, (quad + 1) * CHUNK)
            own_vals = jnp.concatenate(
                [lane_pick(own_ref, owners[quad][:, start : start + LANES]) for start in range(0, CHUNK, LANES)], 1
            )
            partner_vals = group_pick(
                dot(right_ref[...], hot_wide[number, :, cols]),
                partners[quad] // GROUP,
                rows,
                partner_groups * LANES // GROUP,
            )
            projected.append(own_vals[:channels] + partner_vals[:channels])
            own_coords = own_vals[channels:]
            extra = partner_vals[channels:]
            partner_coords = extra + pltpu.roll(extra, 4, 0)
            shift = partner_coords - own_coords
            squared = sum_rows(jnp.where(last, 0.0, shift * shift), (2, 1))
            gain = sum_rows(jnp.where(last, own_coords * partner_coords, 0.0), (2, 1))
            weights.append(lives[quad] * gain)
            away = squared - centers
            basis = jnp.exp(-basis_width * (away * away))
            basis_high, basis_low = split_two(basis)
            stacks.append(jnp.concatenate([basis_high, basis_low, basis_high, basis_low], 0).astype(bf16))
            slopes.append((-2.0 * basis_width) * away * basis)
            shifts.append(shift)
            squares.append(squared)
            yield
        radial = dot(radial_ref[...], jnp.concatenate(stacks, 0))
        yield
        pieces = []
        for quad in quads:
            half = (projected[quad] + part(radial, quad)).astype(bf16)
            _, hidden, slope_one[number, quad] = silu_pair(half)
            pieces.append(hidden)
        yield
        half = dot(matrix(0), jnp.concatenate(pieces, 0))
        yield
        pieces = []
        for quad in quads:
            _, hidden, slope_two[number, quad] = silu_pair(part(half, quad).astype(bf16))
            pieces.append(hidden)
        yield
        half = dot(matrix(1), jnp.concatenate(pieces, 0))
        yield
        pieces = []
        readouts = []
        for quad in quads:
            hidden, _, slope = silu_pair(part(half, quad))
            terms = w_out * hidden
            terms = sum(terms[start : start + 8] for start in range(8, channels, 8)) + terms[:8]
            readouts.append(sum_rows(terms, (4, 2, 1)))
            pieces.append(w_out_half * slope)
        yield
        back = dot(matrix(2), jnp.concatenate(pieces, 0))
        yield
        pieces = [part(back, quad).astype(bf16) * slope_two[number, quad] for quad in quads]
        back = dot(matrix(3), jnp.concatenate(pieces, 0))
        yield
        pieces = [part(back, quad).astype(bf16) * slope_one[number, quad] for quad in quads]
        back = dot(radial_t_ref[...], jnp.concatenate(pieces, 0))
        yield
        parts = []
        for quad in quads:
            two = part(back, quad, 2 * bases)
            readout_slope = sum_rows((two[:bases] + two[bases:]) * slopes[quad], (4, 2, 1))
            near = jnp.maximum(1.0 - squares[quad], 0.0)
            weight_near = weights[quad] * near
            energy = weight_near * near * readouts[quad]
            slope = weight_near * (near * readout_slope - 2.0 * readouts[quad])
            push = (2.0 * slope) * shifts[quad]
            values = jnp.where(last, energy, push)
            parts.append(
                jnp.concatenate(
                    [
                        spread_groups(values, owners[quad] // LANES, own_groups),
                        spread_groups(values, partners[quad] // LANES, partner_groups),
                    ],
                    0,
                ).astype(bf16)
            )
        yield
        sums[...] += dot_nt(jnp.concatenate(parts, 1), hot[number])

    return task


def run(tasks):
    running, waiting = [], list(tasks)
    while running or waiting:
        if waiting:
            running.append(waiting.pop(0))
        for _ in range(2):
            running = [task for task in running if next(task, task) is not task]


def run_rest(task, done, rest):
    steps, size = rest

    def step(index, unused):
        run([task(done + index * size + number, number) for number in range(size)])
        return unused

    lax.fori_loop(0, steps, step, 0)


def fold(list_ref, source, target, turns):
    rows = slice(target * 8, target * 8 + 8)
    spare = slice(source * 8, source * 8 + 8)
    kept = list_ref[rows, :]
    moving = pltpu.roll(list_ref[spare, :], 4, 0)
    for turn in range(turns):
        moving = pltpu.roll(moving, 1, 1)
        if turn % 4 == 3:
            moving = pltpu.roll(moving, 3, 0)
        placed = jnp.where(kept == 0, moving, 0)
        kept = kept + placed
        moving = moving - placed
    list_ref[rows, :] = kept
    list_ref[spare, :] = moving


def rest_of(list_ref, need, done, total):
    left = total - done
    size = next(size for size in (3, 2, 1) if left % size == 0)
    rows = QUAD * CHUNK // LANES
    found = jnp.max(list_ref[done * rows : total * rows, :])
    steps = jnp.maximum(jnp.max(need) - done * rows + size * rows - 1, 0) // (size * rows)
    return jnp.where(found > 0, steps, 0), size


def local_kernel(channels, bases, first_quad, quad_count, counts, *refs):
    count = 7 + sum(counts)
    codes, own, right, *weights = refs[:7]
    sums, hot, *scratch = refs[count:]
    sums[...] = refs[7][...] if counts[0] else jnp.zeros_like(sums)
    groups = own.shape[1] // LANES
    task = pair_tasks(groups, groups, channels, bases, codes, own, right, *weights, sums, hot, *scratch[counts[1] :])
    end = first_quad + quad_count
    if not counts[1]:
        run([task(first_quad + number, number) for number in range(quad_count)])
        return
    tail = scratch[0]
    rows = QUAD * CHUNK // LANES
    start = (end - 1) * rows
    tail[...] = codes[start:, :]
    fold(tail, rows // 8, rows // 8 - 1, 10)
    fold(tail, rows // 8 + 1, rows // 8 - 1, 6)
    run([task(first_quad + number, number) for number in range(quad_count - 1)] + [task(0, quad_count - 1, tail)])
    left = codes.shape[0] // rows - end + 1
    need = refs[7 + counts[0]][...] - start
    run_rest(lambda quad, slot: task(quad, slot, tail), 1, rest_of(tail, need, 1, left))


def near_ones(codes, bits, own_ref, channels, coords_ref):
    sub = iota((8, LANES), 0)
    found = []
    for start in range(0, codes.shape[0], 8):
        tile = codes[start : start + 8]
        squared = jnp.zeros((8, LANES), f32)
        for low in range(4):
            code = jnp.where(
                sub < 4,
                jnp.broadcast_to(tile[low : low + 1], (8, LANES)),
                jnp.broadcast_to(tile[low + 4 : low + 5], (8, LANES)),
            )
            shift = lane_pick(coords_ref, (code >> 1) & (2**bits - 1)) - lane_pick(own_ref, code >> (bits + 1), channels)
            square = shift * shift
            total = square + pltpu.roll(square, 7, 0) + pltpu.roll(square, 6, 0)
            if low:
                total = pltpu.roll(total, low, 0)
            squared = jnp.where(sub % 4 == low, total, squared)
        found.append(jnp.where(squared < 1.001, tile & 1, 0))
    return found


def ghost_kernel(quad_count, channels, bases, *refs):
    blocks = len(ghost_offsets)
    owner, partner, mask, own, *weights = refs[:8]
    sums_in = refs[8]
    arrived = refs[9 : 10 + len(PLANAR)]
    sums_out, upward, *level = refs[10 + len(PLANAR) : 12 + 2 * len(PLANAR)]
    table, sums, codes_ref, coords_ref, *scratch = refs[12 + 2 * len(PLANAR) :]
    groups = own.shape[1] // LANES
    partner_groups = blocks * GROUP // LANES
    sums[...] = jnp.zeros_like(sums)
    pieces = []
    for offset in ghost_offsets:
        if offset[:2] == (0, 0):
            source, start = arrived[0], 0
        else:
            source, start = arrived[1 + PLANAR.index(offset[:2])], offset[2] * (channels + OFFERED)
        extra = source[start + channels : start + channels + OFFERED, :].astype(f32)
        moved = jnp.concatenate(
            [extra[axis : axis + 1] + extra[axis + 4 : axis + 5] + domain_edge * offset[axis] for axis in range(3)], 0
        )
        pieces += [source[start : start + channels, :].astype(f32), coord_rows(moved, extra[3:4])]
        place = ghost_offsets.index(offset) * GROUP
        coords_ref[:, place : place + GROUP] = jnp.concatenate([moved, extra[3:4], moved, extra[3:4]], 0)
    pieces.append(jnp.zeros((table.shape[0] - blocks * (channels + EXTRA), GROUP), f32))
    table[...] = jnp.concatenate(pieces, 0).astype(bf16)
    bits = (partner_groups * LANES - 1).bit_length()
    codes = pack(owner[...], partner[...], mask[...], bits)
    live = near_ones(codes, bits, own, channels, coords_ref)
    need = gather_live(codes, live, bits + (own.shape[1] - 1).bit_length() + 1, codes_ref)
    tile = quad_count * QUAD * CHUNK // LANES // 8
    fold(codes_ref, tile, tile - 1, 8)
    task = pair_tasks(groups, partner_groups, channels, bases, codes_ref, own, table, *weights, sums, *scratch)
    run([task(number, number) for number in range(quad_count)])
    total = owner.shape[0] * LANES // (QUAD * CHUNK)
    run_rest(task, quad_count, rest_of(codes_ref, need, quad_count, total))
    first = groups * 4
    sums_out[0:first, :] = sums_in[0:first, :] + sums[0:first, :]
    sums_out[first:, :] = sums_in[first:, :]
    for block, offset in enumerate(ghost_offsets):
        halves = []
        for half in range(GROUP // LANES):
            start = first + (block * (GROUP // LANES) + half) * 4
            halves.append(sums[start : start + 4, LANES:])
        force = -jnp.concatenate(halves, 1)
        force = jnp.concatenate([force, jnp.zeros_like(force)], 0)
        if offset[2]:
            place = 0 if offset[:2] == (0, 0) else 1 + PLANAR.index(offset[:2])
            upward[place * 8 : place * 8 + 8, :] = force
        else:
            level[PLANAR.index(offset[:2])][...] = force


def pair_kernel(offered_ref, from_z_ref, unused_ref, both_ref):
    count = offered_ref.shape[0]
    both_ref[0:count, :] = offered_ref[...]
    both_ref[count:, :] = from_z_ref[...]


def merge_kernel(*refs):
    upward, *level = refs[: 1 + len(PLANAR)]
    outs = refs[2 + len(PLANAR) :]
    outs[0][...] = upward[0:8, :]
    for place, part in enumerate(level):
        outs[1 + place][...] = part[...] + upward[8 * place + 8 : 8 * place + 16, :]


def final_kernel(*refs):
    sums_ref, send_ref, *arrived = refs[:-2]
    forces_ref, energy_ref = refs[-2:]
    incoming = arrived[0][...]
    for part in arrived[1:]:
        incoming = incoming + part[...]
    high, low = split_two(jnp.concatenate([incoming[:4], incoming[:4]], 0))
    send = jnp.broadcast_to(send_ref[...], (8, send_ref.shape[1]))
    groups = sums_ref.shape[0] // 8
    hot = one_hot(send & (LANES - 1), row_codes(LANES))
    spread = [spread_groups(value, send // LANES, groups).astype(bf16) for value in (high, low)]
    back = dot_nt(jnp.concatenate(spread, 0), hot)
    back = back[: groups * 4] + back[groups * 4 :]
    for group in range(groups):
        own = sums_ref[group * 4 : group * 4 + 4, 0:LANES]
        partner = sums_ref[(groups + group) * 4 : (groups + group) * 4 + 4, LANES:]
        total = own - partner + back[group * 4 : group * 4 + 4]
        cols = slice(group * LANES, (group + 1) * LANES)
        forces_ref[:, cols] = total[0:3]
        energy_ref[:, cols] = own[3:4]


def whole(shape, dtype):
    return jax.ShapeDtypeStruct(shape, dtype)


def call(kernel, outs, name, scratch=(), specs=None, cost=None):
    more = {} if cost is None else dict(cost_estimate=cost)
    return pl.pallas_call(
        kernel,
        grid=(1,),
        in_specs=specs,
        out_specs=tuple(pl.BlockSpec(memory_space=pltpu.VMEM) for _ in outs),
        out_shape=outs,
        scratch_shapes=list(scratch),
        compiler_params=pltpu.CompilerParams(vmem_limit_bytes=VMEM_LIMIT),
        name=name,
        **more,
    )


def shifted(value, offset, sizes, sign):
    used = tuple(axis for axis, step in zip(sizes, offset) if step)
    dims = [size for name, size in used]
    pairs = []
    for flat in range(math.prod(dims)):
        place, rest = [], flat
        for size in reversed(dims):
            place.insert(0, rest % size)
            rest //= size
        target = 0
        for at, size in zip(place, dims):
            target = target * size + (at - sign) % size
        pairs.append((flat, target))
    return lax.ppermute(value, tuple(name for name, size in used), pairs)


def on_device(
    sizes,
    positions,
    features,
    species,
    species_scale,
    w_first,
    w_second,
    w_radial,
    w_mid,
    w_last,
    w_out,
    ghost_send,
    local_first,
    local_second,
    local_mask,
    ghost_owner,
    ghost_index,
    ghost_mask,
):
    channels, own_count = features.shape
    send_count = ghost_send.shape[0]
    bases = w_radial.shape[1]
    rows = channels + EXTRA
    groups = own_count // LANES
    blocks = len(ghost_offsets)
    whole_spec = pl.BlockSpec(memory_space=pltpu.VMEM)
    def tiles(value):
        return value.reshape(value.shape[0] // LANES, LANES)

    def fetching(kernel, name, outs, operands, kept):
        here = [pltpu.with_memory_space_constraint(value, pltpu.HBM) for value in operands]
        landing = operands[: len(operands) - kept]
        return call(
            kernel,
            outs + tuple(whole(value.shape, value.dtype) for value in operands[len(landing) :]),
            name,
            [pltpu.VMEM(value.shape, value.dtype) for value in landing]
            + [pltpu.SemaphoreType.DMA((len(operands),))],
            [pl.BlockSpec(memory_space=pltpu.HBM)] * len(operands),
        )(*here)

    own, right, offered, *weights, local, need, send = fetching(
        tables_kernel,
        "tables",
        (
            whole((rows, own_count), f32),
            whole((-(-own_count // GROUP * rows // 16) * 16, GROUP), bf16),
            whole((channels + OFFERED, send_count), bf16),
            whole((4 * QUAD * channels, QUAD * channels), bf16),
            whole((QUAD * channels, QUAD * 4 * bases), bf16),
            whole((QUAD * 2 * bases, QUAD * channels), bf16),
            whole((channels, LANES), f32),
            whole((local_first.shape[0] // LANES, LANES), jnp.int32),
            whole((8, LANES), jnp.int32),
        ),
        (
            positions,
            features,
            species.reshape(1, own_count),
            species_scale.reshape(1, species_scale.shape[0]),
            w_first,
            w_second,
            w_radial.T,
            w_mid,
            w_last,
            w_out.reshape(1, channels),
            tiles(local_first),
            tiles(local_second),
            tiles(local_mask),
            ghost_send.reshape(1, send_count),
        ),
        1,
    )
    from_z = shifted(offered, (0, 0, 1), sizes, 1)

    def scratch(per_step, hots, more=()):
        hot = [pltpu.VMEM((per_step, GROUP, QUAD * CHUNK), bf16) for _ in range(hots)]
        return hot[:1] + list(more) + hot[1:] + [
            pltpu.VMEM((per_step, QUAD, channels, CHUNK), bf16),
            pltpu.VMEM((per_step, QUAD, channels, CHUNK), bf16),
            pltpu.VMEM((GROUP, LANES), bf16),
        ]

    def cost(slots):
        return pl.CostEstimate(flops=slots * 400000, bytes_accessed=slots * 12, transcendentals=slots * 200)

    quads = local.shape[0] * LANES // (QUAD * CHUNK)
    cuts = [0, quads // 4, quads * 2 // 5, quads * 13 // 20, quads * 4 // 5]
    tail = pltpu.VMEM((local.shape[0] - (cuts[4] - 1) * QUAD * CHUNK // LANES, LANES), local.dtype)

    def local_call(part, start, needed, after):
        operands = [local, own, right, *weights, *start, *needed, *after]
        first = cuts[part]
        size = cuts[part + 1] - first
        (sums,) = call(
            functools.partial(
                local_kernel, channels, bases, first, size, (len(start), len(needed), len(after))
            ),
            (whole((groups * 8, GROUP), f32),),
            "local_pairs",
            scratch(size, 2, [tail] if needed else []),
            [whole_spec] * len(operands),
            cost(size * QUAD * CHUNK),
        )(*operands)
        return sums

    sums = local_call(0, (), (), ())
    (both,) = call(
        pair_kernel, (whole((2 * offered.shape[0], send_count), bf16),), "two_blocks", specs=[whole_spec] * 3
    )(offered, from_z, sums)
    arrived = [from_z] + [shifted(both, (*step, 0), sizes, 1) for step in PLANAR]
    sums = local_call(1, (sums,), (), (both,))
    ghost_lists = [tiles(value) for value in (ghost_owner, ghost_index, ghost_mask)]
    ghost_step = ghost_owner.shape[0] // (QUAD * CHUNK) // 4
    partner_rows = blocks * GROUP // LANES * 4
    table_rows = -(-blocks * rows // 16) * 16
    force = whole((8, send_count), f32)
    sums, upward, *level = call(
        functools.partial(ghost_kernel, ghost_step, channels, bases),
        (whole((groups * 8, GROUP), f32), whole((8 + 8 * len(PLANAR), send_count), f32)) + (force,) * len(PLANAR),
        "ghost_pairs",
        [
            pltpu.VMEM((table_rows, GROUP), bf16),
            pltpu.VMEM((groups * 4 + partner_rows, GROUP), f32),
            pltpu.VMEM((ghost_owner.shape[0] // LANES, LANES), jnp.int32),
            pltpu.VMEM((8, blocks * GROUP), f32),
        ]
        + scratch(ghost_step, 2),
        [whole_spec] * (9 + len(arrived)),
        cost(ghost_owner.shape[0]),
    )(*ghost_lists, own, *weights, sums, *arrived)
    upward = shifted(upward, (0, 0, 1), sizes, -1)
    sums = local_call(2, (sums,), (), ())
    mine, *level = call(
        merge_kernel, (force,) * (1 + len(PLANAR)), "forces_upward", specs=[whole_spec] * (2 + len(PLANAR))
    )(upward, *level, sums)
    returned = [shifted(part, (*step, 0), sizes, -1) for part, step in zip(level, PLANAR)]
    sums = local_call(3, (sums,), (need,), (mine,))
    forces, energy = call(
        final_kernel,
        (whole((3, own_count), f32), whole((1, own_count), f32)),
        "totals",
        specs=[whole_spec] * (3 + len(returned)),
    )(sums, send, mine, *returned)
    return forces, energy.reshape(own_count)


def solution(mesh):
    names = ("gx", "gy", "gz")
    sizes = tuple((name, mesh.shape[name]) for name in names)
    split = P(names)
    cols = P(None, names)
    in_specs = (cols, cols, split) + (P(),) * 7 + (split,) * 7
    return jax.shard_map(
        functools.partial(on_device, sizes),
        mesh=mesh,
        in_specs=in_specs,
        out_specs=(cols, split),
        check_vma=False,
    )
```

```python
import functools
import math

import jax
import jax.numpy as jnp
from jax import lax
from jax.experimental import pallas as pl
from jax.experimental.pallas import tpu as pltpu
from jax.sharding import PartitionSpec as P

basis_width = 24.0
domain_edge = 1.0
ghost_offsets = ((1, 0, 0), (0, 1, 0), (0, 0, 1), (1, 1, 0), (1, 0, 1), (0, 1, 1), (1, 1, 1))

PLANAR = ((1, 0), (0, 1), (1, 1))
EXTRA = 8
OFFERED = 16
GROUP = 256
LANES = 128
CHUNK = 256
QUAD = 4
VMEM_LIMIT = 48 * 1024 * 1024

NT = (((1,), (1,)), ((), ()))
f32 = jnp.float32
bf16 = jnp.bfloat16


def dot(left, right):
    return jnp.dot(left, right, preferred_element_type=f32)


def dot_nt(left, right):
    return lax.dot_general(left, right, NT, preferred_element_type=f32)


def iota(shape, dim):
    return lax.broadcasted_iota(jnp.int32, shape, dim)


def one_hot(entry, codes):
    entry = entry.astype(f32)
    entry = jnp.concatenate([entry, entry], 0).astype(bf16)
    entry = jnp.concatenate([entry] * (codes.shape[0] // 16), 0)
    pieces = [
        jnp.where(codes == entry[:, start : start + LANES], bf16(1), bf16(0))
        for start in range(0, entry.shape[1], LANES)
    ]
    return jnp.concatenate(pieces, 1)


def row_codes(count):
    return iota((count, LANES), 0).astype(f32).astype(bf16)


def split_two(value):
    high = value.astype(bf16).astype(f32)
    return high, value - high


def coord_rows(coords, gain):
    high, low = split_two(coords)
    return jnp.concatenate([high, gain, low, jnp.zeros_like(gain)], 0)


def eye(count):
    return (iota((count, count), 0) == iota((count, count), 1)).astype(bf16)


def fetch(sources, targets, landed):
    copies = [
        pltpu.make_async_copy(source, target, landed.at[place])
        for place, (source, target) in enumerate(zip(sources, targets))
    ]
    for copy in copies:
        copy.start()
    for copy in copies:
        copy.wait()


def tables_kernel(*refs):
    own_ref, right_ref, offered_ref, mats_ref, radial_ref, radial_t_ref, out_ref, list_ref, need_ref = refs[14:23]
    send_ref = refs[23]
    landing = refs[24:37]
    fetch(refs[:14], landing + (send_ref,), refs[37])
    positions_ref, features_ref, species_ref, scale_ref, w_first_ref, w_second_ref = landing[:6]
    radial_w_ref, w_mid_ref, w_last_ref, w_out_ref, first_ref, second_ref, mask_ref = landing[6:]
    channels = features_ref.shape[0]
    count = features_ref.shape[1]
    species = species_ref[...]
    gain = jnp.zeros((1, count), f32)
    for kind in range(scale_ref.shape[1]):
        scale = scale_ref[:, kind : kind + 1].astype(f32)
        gain = jnp.where(species == kind, scale, gain)
    positions = positions_ref[...]
    left = dot(w_first_ref[...], features_ref[...]).astype(bf16).astype(f32)
    right = dot(w_second_ref[...], features_ref[...]).astype(bf16).astype(f32)
    own_ref[0:channels, :] = 0.5 * left
    own_ref[channels:, :] = jnp.concatenate([positions, gain, positions, gain], 0)
    column = jnp.concatenate([0.5 * right, coord_rows(positions, gain)], 0)
    groups = count // GROUP
    rows = channels + EXTRA
    table = jnp.concatenate([column[:, group * GROUP : (group + 1) * GROUP] for group in range(groups)], 0)
    spare = right_ref.shape[0] - groups * rows
    if spare:
        table = jnp.concatenate([table, jnp.zeros((spare, GROUP), f32)], 0)
    table = table.astype(bf16)
    right_ref[...] = table
    send = jnp.broadcast_to(send_ref[...], (8, send_ref.shape[1]))
    picked = dot(table, one_hot(send & (GROUP - 1), row_codes(GROUP)))
    chosen = group_pick(picked, send // GROUP, rows, groups)
    chosen = jnp.concatenate([chosen, jnp.zeros((OFFERED - EXTRA, chosen.shape[1]), f32)], 0)
    offered_ref[...] = chosen.astype(bf16)

    unit = eye(channels)
    w_mid = w_mid_ref[...]
    w_last = w_last_ref[...]
    last_t = dot_nt(unit, w_last).astype(bf16)
    mid_t = dot_nt(unit, w_mid).astype(bf16)
    wide = QUAD * channels
    for place, matrix in enumerate((w_mid, w_last, last_t, mid_t)):
        mats_ref[place * wide : (place + 1) * wide, :] = (0.5 * diagonal_copies(matrix)).astype(bf16)
    bases = radial_w_ref.shape[0]
    high, low = split_two(radial_w_ref[...])
    high = high.astype(bf16)
    low = low.astype(bf16)
    spread = dot_nt(unit, jnp.concatenate([high, high, low, low], 0)).astype(bf16)
    radial_ref[...] = (0.5 * diagonal_copies(spread)).astype(bf16)
    radial_t_ref[...] = diagonal_copies(jnp.concatenate([high, low], 0)).astype(bf16)
    w_out = w_out_ref[...]
    diagonal = jnp.where(iota((channels, channels), 0) == iota((channels, channels), 1), w_out, 0.0)
    out_ref[...] = jnp.broadcast_to(jnp.sum(diagonal, axis=1, keepdims=True), (channels, LANES))
    bits = (count - 1).bit_length()
    codes = pack(first_ref[...], second_ref[...], mask_ref[...], bits)
    live = [codes[start : start + 8] & 1 for start in range(0, codes.shape[0], 8)]
    need_ref[...] = gather_live(codes, live, 2 * bits + 1, list_ref)


def pack(owner, partner, mask, partner_bits):
    return (owner * 2**partner_bits + partner) * 2 + mask


def gather_live(codes, live, bits, list_ref):
    tiles = len(live)
    sub = iota((8, LANES), 0)
    passed = jnp.zeros((8, LANES), jnp.int32)
    words = []
    for tile in range(tiles):
        dead = 1 - live[tile]
        for step in (1, 2, 4):
            dead = dead + jnp.where(sub >= step, pltpu.roll(dead, step, 0), 0)
        move = (passed + dead) * 2**bits + codes[tile * 8 : tile * 8 + 8]
        words.append(jnp.where(live[tile] != 0, move, 0))
        passed = passed + jnp.broadcast_to(dead[7:8], (8, LANES))
    none = jnp.zeros((8, LANES), jnp.int32)
    for power in range((tiles * 8).bit_length()):
        step = 2**power
        moving = [jnp.where((word & 2 ** (bits + power)) != 0, word, 0) for word in words]
        if step < 8:
            rolled = [pltpu.roll(word, 8 - step, 0) for word in moving] + [none]
            come = [jnp.where(sub < 8 - step, rolled[tile], rolled[tile + 1]) for tile in range(tiles)]
        else:
            come = (moving[step // 8 :] + [none] * tiles)[:tiles]
        words = [word - gone + new for word, gone, new in zip(words, moving, come)]
    for tile, word in enumerate(words):
        list_ref[tile * 8 : tile * 8 + 8, :] = word & (2**bits - 1)
    return tiles * 8 - passed


def diagonal_copies(matrix):
    high, wide = matrix.shape
    repeat = (iota((wide, QUAD * wide), 0) == iota((wide, QUAD * wide), 1) % wide).astype(bf16)
    row = dot(matrix, repeat)
    full = jnp.concatenate([row] * QUAD, 0)
    return jnp.where(iota(full.shape, 0) // high == iota(full.shape, 1) // wide, full, 0.0)


def group_pick(values, high, rows, groups):
    high = jnp.concatenate([high] * (rows // 8), 0)
    chosen = values[:rows]
    for group in range(1, groups):
        chosen = jnp.where(high == group, values[group * rows : (group + 1) * rows], chosen)
    return chosen


def spread_groups(values, high, groups):
    second = iota(values.shape, 0) // 4
    pieces = [jnp.where(high == second + group, values, 0.0) for group in range(0, groups, 2)]
    return jnp.concatenate(pieces, 0)


def lane_pick(table_ref, place, first=0):
    rows, count = table_ref.shape[0] - first, table_ref.shape[1]
    lane = jnp.concatenate([place & (LANES - 1)] * (rows // 8), 0)
    high = jnp.concatenate([place // LANES] * (rows // 8), 0)
    chosen = None
    for group in range(count // LANES):
        part = table_ref[first:, group * LANES : (group + 1) * LANES]
        picked = jnp.take_along_axis(part, lane, axis=1, mode="promise_in_bounds")
        chosen = picked if chosen is None else jnp.where(high == group, picked, chosen)
    return chosen


def sum_rows(values, steps):
    for step in steps:
        values = values + pltpu.roll(values, step, 0)
    return values


def pair_tasks(
    own_groups,
    partner_groups,
    channels,
    bases,
    list_ref,
    own_ref,
    right_ref,
    mats_ref,
    radial_ref,
    radial_t_ref,
    out_ref,
    sums,
    hot,
    hot_wide,
    slope_one,
    slope_two,
    codes_ref,
):
    rows = channels + EXTRA
    line = CHUNK // LANES
    block = QUAD * line
    wide = QUAD * channels
    w_out = jnp.concatenate([out_ref[...]] * line, 1)
    centers = iota((bases, CHUNK), 0).astype(f32) * (1.0 / (bases - 1))
    last = iota((8, CHUNK), 0) % 4 == 3
    partner_bits = (partner_groups * LANES - 1).bit_length()
    quads = range(QUAD)
    codes_ref[...] = row_codes(GROUP)

    def matrix(place):
        return mats_ref[place * wide : (place + 1) * wide, :]

    def part(values, number, size=channels):
        return values[number * size : (number + 1) * size]

    def silu_pair(half):
        grow = jnp.tanh(half)
        plus = 1.0 + grow
        hidden = half * plus
        return hidden, plus + hidden * (1.0 - grow)

    def task(first, number, source=list_ref):
        at = pl.multiple_of(first * block, block)
        code_rows = source[pl.ds(at, block), :]
        owners, partners, lives, projected, shifts, squares, weights, stacks, slopes = ([] for _ in range(9))
        for quad in quads:
            cols = slice(quad * CHUNK, (quad + 1) * CHUNK)
            code = jnp.concatenate(
                [
                    jnp.broadcast_to(code_rows[row : row + 1, :], (8, LANES))
                    for row in range(quad * line, (quad + 1) * line)
                ],
                1,
            )
            lives.append((code & 1).astype(f32))
            partner = (code >> 1) & (2**partner_bits - 1)
            owner = code >> (partner_bits + 1)
            owners.append(owner)
            partners.append(partner)
            hot[number, 0:LANES, cols] = one_hot(owner & (LANES - 1), codes_ref[0:LANES, :])
            wide = one_hot(partner & (GROUP - 1), codes_ref[...])
            hot_wide[number, :, cols] = wide
            hot[number, LANES:, cols] = wide[0:LANES] + wide[LANES:]
            yield
        for quad in quads:
            cols = slice(quad * CHUNK, (quad + 1) * CHUNK)
            own_vals = jnp.concatenate(
                [lane_pick(own_ref, owners[quad][:, start : start + LANES]) for start in range(0, CHUNK, LANES)], 1
            )
            partner_vals = group_pick(
                dot(right_ref[...], hot_wide[number, :, cols]),
                partners[quad] // GROUP,
                rows,
                partner_groups * LANES // GROUP,
            )
            projected.append(own_vals[:channels] + partner_vals[:channels])
            own_coords = own_vals[channels:]
            extra = partner_vals[channels:]
            partner_coords = extra + pltpu.roll(extra, 4, 0)
            shift = partner_coords - own_coords
            squared = sum_rows(jnp.where(last, 0.0, shift * shift), (2, 1))
            gain = sum_rows(jnp.where(last, own_coords * partner_coords, 0.0), (2, 1))
            weights.append(lives[quad] * gain)
            away = squared - centers
            basis = jnp.exp(-basis_width * (away * away))
            basis_high, basis_low = split_two(basis)
            stacks.append(jnp.concatenate([basis_high, basis_low, basis_high, basis_low], 0).astype(bf16))
            slopes.append((-2.0 * basis_width) * away * basis)
            shifts.append(shift)
            squares.append(squared)
            yield
        radial = dot(radial_ref[...], jnp.concatenate(stacks, 0))
        yield
        pieces = []
        for quad in quads:
            hidden, slope_one[number, quad] = silu_pair(projected[quad] + part(radial, quad))
            pieces.append(hidden.astype(bf16))
        yield
        half = dot(matrix(0), jnp.concatenate(pieces, 0))
        yield
        pieces = []
        for quad in quads:
            hidden, slope_two[number, quad] = silu_pair(part(half, quad))
            pieces.append(hidden.astype(bf16))
        yield
        half = dot(matrix(1), jnp.concatenate(pieces, 0))
        yield
        pieces = []
        readouts = []
        for quad in quads:
            hidden, slope = silu_pair(part(half, quad))
            terms = w_out * hidden
            terms = sum(terms[start : start + 8] for start in range(8, channels, 8)) + terms[:8]
            readouts.append(sum_rows(terms, (4, 2, 1)))
            pieces.append(((0.5 * w_out) * slope).astype(bf16))
        yield
        back = dot(matrix(2), jnp.concatenate(pieces, 0))
        yield
        pieces = [(part(back, quad) * slope_two[number, quad]).astype(bf16) for quad in quads]
        back = dot(matrix(3), jnp.concatenate(pieces, 0))
        yield
        pieces = [(part(back, quad) * slope_one[number, quad]).astype(bf16) for quad in quads]
        back = dot(radial_t_ref[...], jnp.concatenate(pieces, 0))
        yield
        parts = []
        for quad in quads:
            two = part(back, quad, 2 * bases)
            readout_slope = sum_rows((two[:bases] + two[bases:]) * slopes[quad], (4, 2, 1))
            near = jnp.maximum(1.0 - squares[quad], 0.0)
            weight_near = weights[quad] * near
            energy = weight_near * near * readouts[quad]
            slope = weight_near * (near * readout_slope - 2.0 * readouts[quad])
            push = (2.0 * slope) * shifts[quad]
            values = jnp.where(last, energy, push)
            parts.append(
                jnp.concatenate(
                    [
                        spread_groups(values, owners[quad] // LANES, own_groups),
                        spread_groups(values, partners[quad] // LANES, partner_groups),
                    ],
                    0,
                ).astype(bf16)
            )
        yield
        sums[...] += dot_nt(jnp.concatenate(parts, 1), hot[number])

    return task


def run(tasks, side=None, later=()):
    running, waiting = [], list(tasks)
    while running or waiting or side is not None:
        if waiting:
            running.append(waiting.pop(0))
        if side is not None and next(side, side) is side:
            side = None
            waiting += later
        for _ in range(2):
            running = [task for task in running if next(task, task) is not task]


def run_rest(task, done, rest):
    steps, size = rest

    def step(index, unused):
        run([task(done + index * size + number, number) for number in range(size)])
        return unused

    lax.fori_loop(0, steps, step, 0)


def fold(list_ref, source, target, turns):
    rows = slice(target * 8, target * 8 + 8)
    spare = slice(source * 8, source * 8 + 8)
    kept = list_ref[rows, :]
    moving = pltpu.roll(list_ref[spare, :], 4, 0)
    for turn in range(turns):
        moving = pltpu.roll(moving, 1, 1)
        if turn % 4 == 3:
            moving = pltpu.roll(moving, 3, 0)
        placed = jnp.where(kept == 0, moving, 0)
        kept = kept + placed
        moving = moving - placed
        if turn % 2:
            yield
    list_ref[rows, :] = kept
    list_ref[spare, :] = moving


def rest_of(list_ref, need, done, total):
    left = total - done
    size = next(size for size in (3, 2, 1) if left % size == 0)
    rows = QUAD * CHUNK // LANES
    found = jnp.max(list_ref[done * rows : total * rows, :])
    steps = jnp.maximum(jnp.max(need) - done * rows + size * rows - 1, 0) // (size * rows)
    return jnp.where(found > 0, steps, 0), size


def local_kernel(channels, bases, first_quad, quad_count, spare, counts, *refs):
    has_sums, has_tail, ordering = counts
    count = 7 + has_sums + 2 * has_tail + ordering
    codes, own, right, *weights = refs[:7]
    outs = 1 + (spare > 0)
    sums = refs[count]
    scratch = refs[count + outs :]
    sums[...] = refs[7][...] if has_sums else jnp.zeros_like(sums)
    groups = own.shape[1] // LANES
    task = pair_tasks(groups, groups, channels, bases, codes, own, right, *weights, sums, *scratch)
    rows = QUAD * CHUNK // LANES
    if has_tail:
        tail, need = refs[7 + has_sums : 9 + has_sums]
        end = first_quad + quad_count
        tasks = [task(first_quad + number, number) for number in range(quad_count - 1)]
        run([task(0, quad_count - 1, tail)] + tasks)
        needed = need[...] - (end - 1) * rows
        rest = rest_of(tail, needed, 1, tail.shape[0] // rows)
        run_rest(lambda quad, slot: task(quad, slot, tail), 1, rest)
        return
    side = None
    if spare:
        tail = refs[count + 1]
        tail[...] = codes[(spare - 1) * rows :, :]

        def folds():
            yield from fold(tail, rows // 8, rows // 8 - 1, 10)
            yield from fold(tail, rows // 8 + 1, rows // 8 - 1, 6)

        side = folds()
    run([task(first_quad + number, number) for number in range(quad_count)], side)


def near_ones(codes, bits, own_ref, channels, coords_ref):
    sub = iota((8, LANES), 0)
    found = []
    for start in range(0, codes.shape[0], 8):
        tile = codes[start : start + 8]
        squared = jnp.zeros((8, LANES), f32)
        for low in range(4):
            code = jnp.where(
                sub < 4,
                jnp.broadcast_to(tile[low : low + 1], (8, LANES)),
                jnp.broadcast_to(tile[low + 4 : low + 5], (8, LANES)),
            )
            shift = lane_pick(coords_ref, (code >> 1) & (2**bits - 1)) - lane_pick(own_ref, code >> (bits + 1), channels)
            square = shift * shift
            total = square + pltpu.roll(square, 7, 0) + pltpu.roll(square, 6, 0)
            if low:
                total = pltpu.roll(total, low, 0)
            squared = jnp.where(sub % 4 == low, total, squared)
        found.append(jnp.where(squared < 1.001, tile & 1, 0))
    return found


def ghost_kernel(quad_count, channels, bases, *refs):
    blocks = len(ghost_offsets)
    owner, partner, mask, own, *weights = refs[:8]
    sums_in = refs[8]
    arrived = refs[9 : 10 + len(PLANAR)]
    sums_out, upward, *level = refs[10 + len(PLANAR) : 12 + 2 * len(PLANAR)]
    table, sums, codes_ref, coords_ref, *scratch = refs[12 + 2 * len(PLANAR) :]
    groups = own.shape[1] // LANES
    partner_groups = blocks * GROUP // LANES
    sums[...] = jnp.zeros_like(sums)
    pieces = []
    for offset in ghost_offsets:
        if offset[:2] == (0, 0):
            source, start = arrived[0], 0
        else:
            source, start = arrived[1 + PLANAR.index(offset[:2])], offset[2] * (channels + OFFERED)
        extra = source[start + channels : start + channels + OFFERED, :].astype(f32)
        moved = jnp.concatenate(
            [extra[axis : axis + 1] + extra[axis + 4 : axis + 5] + domain_edge * offset[axis] for axis in range(3)], 0
        )
        pieces += [source[start : start + channels, :].astype(f32), coord_rows(moved, extra[3:4])]
        place = ghost_offsets.index(offset) * GROUP
        coords_ref[:, place : place + GROUP] = jnp.concatenate([moved, extra[3:4], moved, extra[3:4]], 0)
    pieces.append(jnp.zeros((table.shape[0] - blocks * (channels + EXTRA), GROUP), f32))
    table[...] = jnp.concatenate(pieces, 0).astype(bf16)
    bits = (partner_groups * LANES - 1).bit_length()
    codes = pack(owner[...], partner[...], mask[...], bits)
    live = near_ones(codes, bits, own, channels, coords_ref)
    need = gather_live(codes, live, bits + (own.shape[1] - 1).bit_length() + 1, codes_ref)
    tile = quad_count * QUAD * CHUNK // LANES // 8
    task = pair_tasks(groups, partner_groups, channels, bases, codes_ref, own, table, *weights, sums, *scratch)
    last = quad_count - 1
    run([task(number, number) for number in range(last)], fold(codes_ref, tile, tile - 1, 4), [task(last, last)])
    total = owner.shape[0] * LANES // (QUAD * CHUNK)
    run_rest(task, quad_count, rest_of(codes_ref, need, quad_count, total))
    first = groups * 4
    sums_out[0:first, :] = sums_in[0:first, :] + sums[0:first, :]
    sums_out[first:, :] = sums_in[first:, :]
    for block, offset in enumerate(ghost_offsets):
        halves = []
        for half in range(GROUP // LANES):
            start = first + (block * (GROUP // LANES) + half) * 4
            halves.append(sums[start : start + 4, LANES:])
        force = -jnp.concatenate(halves, 1)
        force = jnp.concatenate([force, jnp.zeros_like(force)], 0)
        if offset[2]:
            place = 0 if offset[:2] == (0, 0) else 1 + PLANAR.index(offset[:2])
            upward[place * 8 : place * 8 + 8, :] = force
        else:
            level[PLANAR.index(offset[:2])][...] = force


def pair_kernel(offered_ref, from_z_ref, unused_ref, both_ref):
    count = offered_ref.shape[0]
    both_ref[0:count, :] = offered_ref[...]
    both_ref[count:, :] = from_z_ref[...]


def merge_kernel(*refs):
    upward, *level = refs[: 1 + len(PLANAR)]
    outs = refs[2 + len(PLANAR) :]
    outs[0][...] = upward[0:8, :]
    for place, part in enumerate(level):
        outs[1 + place][...] = part[...] + upward[8 * place + 8 : 8 * place + 16, :]


def final_kernel(*refs):
    sums_ref, send_ref, *arrived = refs[:-2]
    forces_ref, energy_ref = refs[-2:]
    incoming = arrived[0][...]
    for part in arrived[1:]:
        incoming = incoming + part[...]
    high, low = split_two(jnp.concatenate([incoming[:4], incoming[:4]], 0))
    send = jnp.broadcast_to(send_ref[...], (8, send_ref.shape[1]))
    groups = sums_ref.shape[0] // 8
    hot = one_hot(send & (LANES - 1), row_codes(LANES))
    spread = [spread_groups(value, send // LANES, groups).astype(bf16) for value in (high, low)]
    back = dot_nt(jnp.concatenate(spread, 0), hot)
    back = back[: groups * 4] + back[groups * 4 :]
    for group in range(groups):
        own = sums_ref[group * 4 : group * 4 + 4, 0:LANES]
        partner = sums_ref[(groups + group) * 4 : (groups + group) * 4 + 4, LANES:]
        total = own - partner + back[group * 4 : group * 4 + 4]
        cols = slice(group * LANES, (group + 1) * LANES)
        forces_ref[:, cols] = total[0:3]
        energy_ref[:, cols] = own[3:4]


def whole(shape, dtype):
    return jax.ShapeDtypeStruct(shape, dtype)


def call(kernel, outs, name, scratch=(), specs=None, cost=None):
    more = {} if cost is None else dict(cost_estimate=cost)
    return pl.pallas_call(
        kernel,
        grid=(1,),
        in_specs=specs,
        out_specs=tuple(pl.BlockSpec(memory_space=pltpu.VMEM) for _ in outs),
        out_shape=outs,
        scratch_shapes=list(scratch),
        compiler_params=pltpu.CompilerParams(vmem_limit_bytes=VMEM_LIMIT),
        name=name,
        **more,
    )


def shifted(value, offset, sizes, sign):
    used = tuple(axis for axis, step in zip(sizes, offset) if step)
    dims = [size for name, size in used]
    pairs = []
    for flat in range(math.prod(dims)):
        place, rest = [], flat
        for size in reversed(dims):
            place.insert(0, rest % size)
            rest //= size
        target = 0
        for at, size in zip(place, dims):
            target = target * size + (at - sign) % size
        pairs.append((flat, target))
    return lax.ppermute(value, tuple(name for name, size in used), pairs)


def on_device(
    sizes,
    positions,
    features,
    species,
    species_scale,
    w_first,
    w_second,
    w_radial,
    w_mid,
    w_last,
    w_out,
    ghost_send,
    local_first,
    local_second,
    local_mask,
    ghost_owner,
    ghost_index,
    ghost_mask,
):
    channels, own_count = features.shape
    send_count = ghost_send.shape[0]
    bases = w_radial.shape[1]
    rows = channels + EXTRA
    groups = own_count // LANES
    blocks = len(ghost_offsets)
    whole_spec = pl.BlockSpec(memory_space=pltpu.VMEM)
    def tiles(value):
        return value.reshape(value.shape[0] // LANES, LANES)

    def fetching(kernel, name, outs, operands, kept):
        here = [pltpu.with_memory_space_constraint(value, pltpu.HBM) for value in operands]
        landing = operands[: len(operands) - kept]
        return call(
            kernel,
            outs + tuple(whole(value.shape, value.dtype) for value in operands[len(landing) :]),
            name,
            [pltpu.VMEM(value.shape, value.dtype) for value in landing]
            + [pltpu.SemaphoreType.DMA((len(operands),))],
            [pl.BlockSpec(memory_space=pltpu.HBM)] * len(operands),
        )(*here)

    own, right, offered, *weights, local, need, send = fetching(
        tables_kernel,
        "tables",
        (
            whole((rows, own_count), f32),
            whole((-(-own_count // GROUP * rows // 16) * 16, GROUP), bf16),
            whole((channels + OFFERED, send_count), bf16),
            whole((4 * QUAD * channels, QUAD * channels), bf16),
            whole((QUAD * channels, QUAD * 4 * bases), bf16),
            whole((QUAD * 2 * bases, QUAD * channels), bf16),
            whole((channels, LANES), f32),
            whole((local_first.shape[0] // LANES, LANES), jnp.int32),
            whole((8, LANES), jnp.int32),
        ),
        (
            positions,
            features,
            species.reshape(1, own_count),
            species_scale.reshape(1, species_scale.shape[0]),
            w_first,
            w_second,
            w_radial.T,
            w_mid,
            w_last,
            w_out.reshape(1, channels),
            tiles(local_first),
            tiles(local_second),
            tiles(local_mask),
            ghost_send.reshape(1, send_count),
        ),
        1,
    )
    from_z = shifted(offered, (0, 0, 1), sizes, 1)

    def scratch(per_step, hots):
        return [pltpu.VMEM((per_step, GROUP, QUAD * CHUNK), bf16) for _ in range(hots)] + [
            pltpu.VMEM((per_step, QUAD, channels, CHUNK), f32),
            pltpu.VMEM((per_step, QUAD, channels, CHUNK), f32),
            pltpu.VMEM((GROUP, LANES), bf16),
        ]

    def cost(slots):
        return pl.CostEstimate(flops=slots * 400000, bytes_accessed=slots * 12, transcendentals=slots * 200)

    quads = local.shape[0] * LANES // (QUAD * CHUNK)
    cuts = [0, quads // 5, quads * 2 // 5, quads * 7 // 10, quads * 4 // 5]
    tail_rows = local.shape[0] - (cuts[4] - 1) * QUAD * CHUNK // LANES

    def local_call(part, start, tail, after):
        operands = [local, own, right, *weights, *start, *tail, *after]
        first = cuts[part]
        size = cuts[part + 1] - first
        spare = cuts[4] if part == 2 else 0
        outs = (whole((groups * 8, GROUP), f32),) + ((whole((tail_rows, LANES), jnp.int32),) if spare else ())
        return call(
            functools.partial(
                local_kernel, channels, bases, first, size, spare, (len(start), len(tail) // 2, len(after))
            ),
            outs,
            "local_pairs",
            scratch(size, 2),
            [whole_spec] * len(operands),
            cost(size * QUAD * CHUNK),
        )(*operands)

    (sums,) = local_call(0, (), (), ())
    (both,) = call(
        pair_kernel, (whole((2 * offered.shape[0], send_count), bf16),), "two_blocks", specs=[whole_spec] * 3
    )(offered, from_z, sums)
    arrived = [from_z] + [shifted(both, (*step, 0), sizes, 1) for step in PLANAR]
    (sums,) = local_call(1, (sums,), (), (both,))
    ghost_lists = [tiles(value) for value in (ghost_owner, ghost_index, ghost_mask)]
    ghost_step = ghost_owner.shape[0] // (QUAD * CHUNK) // 4
    partner_rows = blocks * GROUP // LANES * 4
    table_rows = -(-blocks * rows // 16) * 16
    force = whole((8, send_count), f32)
    sums, upward, *level = call(
        functools.partial(ghost_kernel, ghost_step, channels, bases),
        (whole((groups * 8, GROUP), f32), whole((8 + 8 * len(PLANAR), send_count), f32)) + (force,) * len(PLANAR),
        "ghost_pairs",
        [
            pltpu.VMEM((table_rows, GROUP), bf16),
            pltpu.VMEM((groups * 4 + partner_rows, GROUP), f32),
            pltpu.VMEM((ghost_owner.shape[0] // LANES, LANES), jnp.int32),
            pltpu.VMEM((8, blocks * GROUP), f32),
        ]
        + scratch(ghost_step, 2),
        [whole_spec] * (9 + len(arrived)),
        cost(ghost_owner.shape[0]),
    )(*ghost_lists, own, *weights, sums, *arrived)
    upward = shifted(upward, (0, 0, 1), sizes, -1)
    sums, tail = local_call(2, (sums,), (), ())
    mine, *level = call(
        merge_kernel, (force,) * (1 + len(PLANAR)), "forces_upward", specs=[whole_spec] * (2 + len(PLANAR))
    )(upward, *level, sums)
    returned = [shifted(part, (*step, 0), sizes, -1) for part, step in zip(level, PLANAR)]
    (sums,) = local_call(3, (sums,), (tail, need), (mine,))
    forces, energy = call(
        final_kernel,
        (whole((3, own_count), f32), whole((1, own_count), f32)),
        "totals",
        specs=[whole_spec] * (3 + len(returned)),
    )(sums, send, mine, *returned)
    return forces, energy.reshape(own_count)


def solution(mesh):
    names = ("gx", "gy", "gz")
    sizes = tuple((name, mesh.shape[name]) for name in names)
    split = P(names)
    cols = P(None, names)
    in_specs = (cols, cols, split) + (P(),) * 7 + (split,) * 7
    return jax.shard_map(
        functools.partial(on_device, sizes),
        mesh=mesh,
        in_specs=in_specs,
        out_specs=(cols, split),
        check_vma=False,
    )
```

```python
import functools
import math

import jax
import jax.numpy as jnp
from jax import lax
from jax.experimental import pallas as pl
from jax.experimental.pallas import tpu as pltpu
from jax.sharding import PartitionSpec as P

basis_width = 24.0
domain_edge = 1.0
ghost_offsets = ((1, 0, 0), (0, 1, 0), (0, 0, 1), (1, 1, 0), (1, 0, 1), (0, 1, 1), (1, 1, 1))

PLANAR = ((1, 0), (0, 1), (1, 1))
EXTRA = 8
OFFERED = 16
GROUP = 256
LANES = 128
CHUNK = 256
QUAD = 4
VMEM_LIMIT = 48 * 1024 * 1024

NT = (((1,), (1,)), ((), ()))
f32 = jnp.float32
bf16 = jnp.bfloat16


def dot(left, right):
    return jnp.dot(left, right, preferred_element_type=f32)


def dot_nt(left, right):
    return lax.dot_general(left, right, NT, preferred_element_type=f32)


def iota(shape, dim):
    return lax.broadcasted_iota(jnp.int32, shape, dim)


def one_hot(entry, codes):
    entry = entry.astype(f32)
    entry = jnp.concatenate([entry, entry], 0).astype(bf16)
    entry = jnp.concatenate([entry] * (codes.shape[0] // 16), 0)
    pieces = [
        jnp.where(codes == entry[:, start : start + LANES], bf16(1), bf16(0))
        for start in range(0, entry.shape[1], LANES)
    ]
    return jnp.concatenate(pieces, 1)


def row_codes(count):
    return iota((count, LANES), 0).astype(f32).astype(bf16)


def split_two(value):
    high = value.astype(bf16).astype(f32)
    return high, value - high


def coord_rows(coords, gain):
    high, low = split_two(coords)
    return jnp.concatenate([high, gain, low, jnp.zeros_like(gain)], 0)


def eye(count):
    return (iota((count, count), 0) == iota((count, count), 1)).astype(bf16)


def fetch(sources, targets, landed):
    copies = [
        pltpu.make_async_copy(source, target, landed.at[place])
        for place, (source, target) in enumerate(zip(sources, targets))
    ]
    for copy in copies:
        copy.start()
    for copy in copies:
        copy.wait()


def tables_kernel(*refs):
    own_ref, right_ref, offered_ref, mats_ref, radial_ref, radial_t_ref, out_ref, list_ref, need_ref = refs[14:23]
    send_ref = refs[23]
    landing = refs[24:37]
    fetch(refs[:14], landing + (send_ref,), refs[37])
    positions_ref, features_ref, species_ref, scale_ref, w_first_ref, w_second_ref = landing[:6]
    radial_w_ref, w_mid_ref, w_last_ref, w_out_ref, first_ref, second_ref, mask_ref = landing[6:]
    channels = features_ref.shape[0]
    count = features_ref.shape[1]
    species = species_ref[...]
    gain = jnp.zeros((1, count), f32)
    for kind in range(scale_ref.shape[1]):
        scale = scale_ref[:, kind : kind + 1].astype(f32)
        gain = jnp.where(species == kind, scale, gain)
    positions = positions_ref[...]
    left = dot(w_first_ref[...], features_ref[...]).astype(bf16).astype(f32)
    right = dot(w_second_ref[...], features_ref[...]).astype(bf16).astype(f32)
    own_ref[0:channels, :] = 0.5 * left
    own_ref[channels:, :] = jnp.concatenate([positions, gain, positions, gain], 0)
    column = jnp.concatenate([0.5 * right, coord_rows(positions, gain)], 0)
    groups = count // GROUP
    rows = channels + EXTRA
    table = jnp.concatenate([column[:, group * GROUP : (group + 1) * GROUP] for group in range(groups)], 0)
    spare = right_ref.shape[0] - groups * rows
    if spare:
        table = jnp.concatenate([table, jnp.zeros((spare, GROUP), f32)], 0)
    table = table.astype(bf16)
    right_ref[...] = table
    send = jnp.broadcast_to(send_ref[...], (8, send_ref.shape[1]))
    picked = dot(table, one_hot(send & (GROUP - 1), row_codes(GROUP)))
    chosen = group_pick(picked, send // GROUP, rows, groups)
    chosen = jnp.concatenate([chosen, jnp.zeros((OFFERED - EXTRA, chosen.shape[1]), f32)], 0)
    offered_ref[...] = chosen.astype(bf16)

    unit = eye(channels)
    w_mid = w_mid_ref[...]
    w_last = w_last_ref[...]
    last_t = dot_nt(unit, w_last).astype(bf16)
    mid_t = dot_nt(unit, w_mid).astype(bf16)
    wide = QUAD * channels
    for place, matrix in enumerate((w_mid, w_last, last_t, mid_t)):
        mats_ref[place * wide : (place + 1) * wide, :] = (0.5 * diagonal_copies(matrix)).astype(bf16)
    bases = radial_w_ref.shape[0]
    high, low = split_two(radial_w_ref[...])
    high = high.astype(bf16)
    low = low.astype(bf16)
    spread = dot_nt(unit, jnp.concatenate([high, high, low, low], 0)).astype(bf16)
    radial_ref[...] = (0.5 * diagonal_copies(spread)).astype(bf16)
    radial_t_ref[...] = diagonal_copies(jnp.concatenate([high, low], 0)).astype(bf16)
    w_out = w_out_ref[...]
    diagonal = jnp.where(iota((channels, channels), 0) == iota((channels, channels), 1), w_out, 0.0)
    out_ref[...] = jnp.broadcast_to(jnp.sum(diagonal, axis=1, keepdims=True), (channels, LANES))
    bits = (count - 1).bit_length()
    codes = pack(first_ref[...], second_ref[...], mask_ref[...], bits)
    live = [codes[start : start + 8] & 1 for start in range(0, codes.shape[0], 8)]
    need_ref[...] = gather_live(codes, live, 2 * bits + 1, list_ref)


def pack(owner, partner, mask, partner_bits):
    return (owner * 2**partner_bits + partner) * 2 + mask


def gather_live(codes, live, bits, list_ref):
    tiles = len(live)
    sub = iota((8, LANES), 0)
    passed = jnp.zeros((8, LANES), jnp.int32)
    words = []
    for tile in range(tiles):
        dead = 1 - live[tile]
        for step in (1, 2, 4):
            dead = dead + jnp.where(sub >= step, pltpu.roll(dead, step, 0), 0)
        move = (passed + dead) * 2**bits + codes[tile * 8 : tile * 8 + 8]
        words.append(jnp.where(live[tile] != 0, move, 0))
        passed = passed + jnp.broadcast_to(dead[7:8], (8, LANES))
    none = jnp.zeros((8, LANES), jnp.int32)
    for power in range((tiles * 8).bit_length()):
        step = 2**power
        moving = [jnp.where((word & 2 ** (bits + power)) != 0, word, 0) for word in words]
        if step < 8:
            rolled = [pltpu.roll(word, 8 - step, 0) for word in moving] + [none]
            come = [jnp.where(sub < 8 - step, rolled[tile], rolled[tile + 1]) for tile in range(tiles)]
        else:
            come = (moving[step // 8 :] + [none] * tiles)[:tiles]
        words = [word - gone + new for word, gone, new in zip(words, moving, come)]
    for tile, word in enumerate(words):
        list_ref[tile * 8 : tile * 8 + 8, :] = word & (2**bits - 1)
    return tiles * 8 - passed


def diagonal_copies(matrix):
    high, wide = matrix.shape
    repeat = (iota((wide, QUAD * wide), 0) == iota((wide, QUAD * wide), 1) % wide).astype(bf16)
    row = dot(matrix, repeat)
    full = jnp.concatenate([row] * QUAD, 0)
    return jnp.where(iota(full.shape, 0) // high == iota(full.shape, 1) // wide, full, 0.0)


def group_pick(values, high, rows, groups):
    high = jnp.concatenate([high] * (rows // 8), 0)
    chosen = values[:rows]
    for group in range(1, groups):
        chosen = jnp.where(high == group, values[group * rows : (group + 1) * rows], chosen)
    return chosen


def spread_groups(values, high, groups):
    second = iota(values.shape, 0) // 4
    pieces = [jnp.where(high == second + group, values, 0.0) for group in range(0, groups, 2)]
    return jnp.concatenate(pieces, 0)


def lane_pick(table_ref, place, first=0):
    rows, count = table_ref.shape[0] - first, table_ref.shape[1]
    lane = jnp.concatenate([place & (LANES - 1)] * (rows // 8), 0)
    high = jnp.concatenate([place // LANES] * (rows // 8), 0)
    chosen = None
    for group in range(count // LANES):
        part = table_ref[first:, group * LANES : (group + 1) * LANES]
        picked = jnp.take_along_axis(part, lane, axis=1, mode="promise_in_bounds")
        chosen = picked if chosen is None else jnp.where(high == group, picked, chosen)
    return chosen


def sum_rows(values, steps):
    for step in steps:
        values = values + pltpu.roll(values, step, 0)
    return values


def pair_tasks(
    own_groups,
    partner_groups,
    channels,
    bases,
    list_ref,
    own_ref,
    right_ref,
    mats_ref,
    radial_ref,
    radial_t_ref,
    out_ref,
    sums,
    hot,
    hot_wide,
    slope_one,
    slope_two,
    codes_ref,
):
    rows = channels + EXTRA
    line = CHUNK // LANES
    block = QUAD * line
    wide = QUAD * channels
    w_out = jnp.concatenate([out_ref[...]] * line, 1)
    centers = iota((bases, CHUNK), 0).astype(f32) * (1.0 / (bases - 1))
    last = iota((8, CHUNK), 0) % 4 == 3
    partner_bits = (partner_groups * LANES - 1).bit_length()
    quads = range(QUAD)
    codes_ref[...] = row_codes(GROUP)

    def matrix(place):
        return mats_ref[place * wide : (place + 1) * wide, :]

    def part(values, number, size=channels):
        return values[number * size : (number + 1) * size]

    def silu_pair(half):
        grow = jnp.tanh(half)
        plus = 1.0 + grow
        hidden = half * plus
        return hidden, plus + hidden * (1.0 - grow)

    def task(first, number, source=list_ref):
        at = pl.multiple_of(first * block, block)
        code_rows = source[pl.ds(at, block), :]
        owners, partners, lives, projected, shifts, squares, weights, stacks, slopes = ([] for _ in range(9))
        for quad in quads:
            cols = slice(quad * CHUNK, (quad + 1) * CHUNK)
            code = jnp.concatenate(
                [
                    jnp.broadcast_to(code_rows[row : row + 1, :], (8, LANES))
                    for row in range(quad * line, (quad + 1) * line)
                ],
                1,
            )
            lives.append((code & 1).astype(f32))
            partner = (code >> 1) & (2**partner_bits - 1)
            owner = code >> (partner_bits + 1)
            owners.append(owner)
            partners.append(partner)
            hot[number, 0:LANES, cols] = one_hot(owner & (LANES - 1), codes_ref[0:LANES, :])
            wide = one_hot(partner & (GROUP - 1), codes_ref[...])
            hot_wide[number, :, cols] = wide
            hot[number, LANES:, cols] = wide[0:LANES] + wide[LANES:]
            yield
        for quad in quads:
            cols = slice(quad * CHUNK, (quad + 1) * CHUNK)
            own_vals = jnp.concatenate(
                [lane_pick(own_ref, owners[quad][:, start : start + LANES]) for start in range(0, CHUNK, LANES)], 1
            )
            partner_vals = group_pick(
                dot(right_ref[...], hot_wide[number, :, cols]),
                partners[quad] // GROUP,
                rows,
                partner_groups * LANES // GROUP,
            )
            projected.append(own_vals[:channels] + partner_vals[:channels])
            own_coords = own_vals[channels:]
            extra = partner_vals[channels:]
            partner_coords = extra + pltpu.roll(extra, 4, 0)
            shift = partner_coords - own_coords
            squared = sum_rows(jnp.where(last, 0.0, shift * shift), (2, 1))
            gain = sum_rows(jnp.where(last, own_coords * partner_coords, 0.0), (2, 1))
            weights.append(lives[quad] * gain)
            away = squared - centers
            basis = jnp.exp(-basis_width * (away * away))
            basis_high, basis_low = split_two(basis)
            stacks.append(jnp.concatenate([basis_high, basis_low, basis_high, basis_low], 0).astype(bf16))
            slopes.append((-2.0 * basis_width) * away * basis)
            shifts.append(shift)
            squares.append(squared)
            yield
        radial = dot(radial_ref[...], jnp.concatenate(stacks, 0))
        yield
        pieces = []
        for quad in quads:
            hidden, slope_one[number, quad] = silu_pair(projected[quad] + part(radial, quad))
            pieces.append(hidden.astype(bf16))
        yield
        half = dot(matrix(0), jnp.concatenate(pieces, 0))
        yield
        pieces = []
        for quad in quads:
            hidden, slope_two[number, quad] = silu_pair(part(half, quad))
            pieces.append(hidden.astype(bf16))
        yield
        half = dot(matrix(1), jnp.concatenate(pieces, 0))
        yield
        pieces = []
        readouts = []
        for quad in quads:
            hidden, slope = silu_pair(part(half, quad))
            terms = w_out * hidden
            terms = sum(terms[start : start + 8] for start in range(8, channels, 8)) + terms[:8]
            readouts.append(sum_rows(terms, (4, 2, 1)))
            pieces.append(((0.5 * w_out) * slope).astype(bf16))
        yield
        back = dot(matrix(2), jnp.concatenate(pieces, 0))
        yield
        pieces = [(part(back, quad) * slope_two[number, quad]).astype(bf16) for quad in quads]
        back = dot(matrix(3), jnp.concatenate(pieces, 0))
        yield
        pieces = [(part(back, quad) * slope_one[number, quad]).astype(bf16) for quad in quads]
        back = dot(radial_t_ref[...], jnp.concatenate(pieces, 0))
        yield
        parts = []
        for quad in quads:
            two = part(back, quad, 2 * bases)
            readout_slope = sum_rows((two[:bases] + two[bases:]) * slopes[quad], (4, 2, 1))
            near = jnp.maximum(1.0 - squares[quad], 0.0)
            weight_near = weights[quad] * near
            energy = weight_near * near * readouts[quad]
            slope = weight_near * (near * readout_slope - 2.0 * readouts[quad])
            push = (2.0 * slope) * shifts[quad]
            values = jnp.where(last, energy, push)
            parts.append(
                jnp.concatenate(
                    [
                        spread_groups(values, owners[quad] // LANES, own_groups),
                        spread_groups(values, partners[quad] // LANES, partner_groups),
                    ],
                    0,
                ).astype(bf16)
            )
        yield
        sums[...] += dot_nt(jnp.concatenate(parts, 1), hot[number])

    return task


def run(tasks, side=None, later=()):
    running, waiting = [], list(tasks)
    while running or waiting or side is not None:
        if waiting:
            running.append(waiting.pop(0))
        if side is not None and next(side, side) is side:
            side = None
            waiting += later
        running = [task for task in running if next(task, task) is not task]


def run_rest(task, done, rest):
    steps, size = rest

    def step(index, unused):
        run([task(done + index * size + number, number) for number in range(size)])
        return unused

    lax.fori_loop(0, steps, step, 0)


def fold(list_ref, source, target, turns):
    rows = slice(target * 8, target * 8 + 8)
    spare = slice(source * 8, source * 8 + 8)
    kept = list_ref[rows, :]
    moving = pltpu.roll(list_ref[spare, :], 4, 0)
    for turn in range(turns):
        moving = pltpu.roll(moving, 1, 1)
        if turn % 4 == 3:
            moving = pltpu.roll(moving, 3, 0)
        placed = jnp.where(kept == 0, moving, 0)
        kept = kept + placed
        moving = moving - placed
        if turn % 2:
            yield
    list_ref[rows, :] = kept
    list_ref[spare, :] = moving


def rest_of(list_ref, need, done, total):
    left = total - done
    size = next(size for size in (3, 2, 1) if left % size == 0)
    rows = QUAD * CHUNK // LANES
    found = jnp.max(list_ref[done * rows : total * rows, :])
    steps = jnp.maximum(jnp.max(need) - done * rows + size * rows - 1, 0) // (size * rows)
    return jnp.where(found > 0, steps, 0), size


def local_kernel(channels, bases, first_quad, quad_count, spare, counts, *refs):
    has_sums, has_tail, ordering = counts
    count = 7 + has_sums + 2 * has_tail + ordering
    codes, own, right, *weights = refs[:7]
    outs = 1 + (spare > 0)
    sums = refs[count]
    scratch = refs[count + outs :]
    sums[...] = refs[7][...] if has_sums else jnp.zeros_like(sums)
    groups = own.shape[1] // LANES
    task = pair_tasks(groups, groups, channels, bases, codes, own, right, *weights, sums, *scratch)
    rows = QUAD * CHUNK // LANES
    if has_tail:
        tail, need = refs[7 + has_sums : 9 + has_sums]
        end = first_quad + quad_count
        tasks = [task(first_quad + number, number) for number in range(quad_count - 1)]
        run([task(0, quad_count - 1, tail)] + tasks)
        needed = need[...] - (end - 1) * rows
        rest = rest_of(tail, needed, 1, tail.shape[0] // rows)
        run_rest(lambda quad, slot: task(quad, slot, tail), 1, rest)
        return
    side = None
    if spare:
        tail = refs[count + 1]
        tail[...] = codes[(spare - 1) * rows :, :]

        def folds():
            yield from fold(tail, rows // 8, rows // 8 - 1, 10)
            yield from fold(tail, rows // 8 + 1, rows // 8 - 1, 6)

        side = folds()
    run([task(first_quad + number, number) for number in range(quad_count)], side)


def near_ones(codes, bits, own_ref, channels, coords_ref):
    sub = iota((8, LANES), 0)
    found = []
    for start in range(0, codes.shape[0], 8):
        tile = codes[start : start + 8]
        squared = jnp.zeros((8, LANES), f32)
        for low in range(4):
            code = jnp.where(
                sub < 4,
                jnp.broadcast_to(tile[low : low + 1], (8, LANES)),
                jnp.broadcast_to(tile[low + 4 : low + 5], (8, LANES)),
            )
            shift = lane_pick(coords_ref, (code >> 1) & (2**bits - 1)) - lane_pick(own_ref, code >> (bits + 1), channels)
            square = shift * shift
            total = square + pltpu.roll(square, 7, 0) + pltpu.roll(square, 6, 0)
            if low:
                total = pltpu.roll(total, low, 0)
            squared = jnp.where(sub % 4 == low, total, squared)
        found.append(jnp.where(squared < 1.001, tile & 1, 0))
    return found


def ghost_kernel(quad_count, channels, bases, *refs):
    blocks = len(ghost_offsets)
    owner, partner, mask, own, *weights = refs[:8]
    sums_in = refs[8]
    arrived = refs[9 : 10 + len(PLANAR)]
    sums_out, upward, *level = refs[10 + len(PLANAR) : 12 + 2 * len(PLANAR)]
    table, sums, codes_ref, coords_ref, *scratch = refs[12 + 2 * len(PLANAR) :]
    groups = own.shape[1] // LANES
    partner_groups = blocks * GROUP // LANES
    sums[...] = jnp.zeros_like(sums)
    pieces = []
    for offset in ghost_offsets:
        if offset[:2] == (0, 0):
            source, start = arrived[0], 0
        else:
            source, start = arrived[1 + PLANAR.index(offset[:2])], offset[2] * (channels + OFFERED)
        extra = source[start + channels : start + channels + OFFERED, :].astype(f32)
        moved = jnp.concatenate(
            [extra[axis : axis + 1] + extra[axis + 4 : axis + 5] + domain_edge * offset[axis] for axis in range(3)], 0
        )
        pieces += [source[start : start + channels, :].astype(f32), coord_rows(moved, extra[3:4])]
        place = ghost_offsets.index(offset) * GROUP
        coords_ref[:, place : place + GROUP] = jnp.concatenate([moved, extra[3:4], moved, extra[3:4]], 0)
    pieces.append(jnp.zeros((table.shape[0] - blocks * (channels + EXTRA), GROUP), f32))
    table[...] = jnp.concatenate(pieces, 0).astype(bf16)
    bits = (partner_groups * LANES - 1).bit_length()
    codes = pack(owner[...], partner[...], mask[...], bits)
    live = near_ones(codes, bits, own, channels, coords_ref)
    need = gather_live(codes, live, bits + (own.shape[1] - 1).bit_length() + 1, codes_ref)
    tile = quad_count * QUAD * CHUNK // LANES // 8
    task = pair_tasks(groups, partner_groups, channels, bases, codes_ref, own, table, *weights, sums, *scratch)
    last = quad_count - 1
    run([task(number, number) for number in range(last)], fold(codes_ref, tile, tile - 1, 4), [task(last, last)])
    total = owner.shape[0] * LANES // (QUAD * CHUNK)
    run_rest(task, quad_count, rest_of(codes_ref, need, quad_count, total))
    first = groups * 4
    sums_out[0:first, :] = sums_in[0:first, :] + sums[0:first, :]
    sums_out[first:, :] = sums_in[first:, :]
    for block, offset in enumerate(ghost_offsets):
        halves = []
        for half in range(GROUP // LANES):
            start = first + (block * (GROUP // LANES) + half) * 4
            halves.append(sums[start : start + 4, LANES:])
        force = -jnp.concatenate(halves, 1)
        force = jnp.concatenate([force, jnp.zeros_like(force)], 0)
        if offset[2]:
            place = 0 if offset[:2] == (0, 0) else 1 + PLANAR.index(offset[:2])
            upward[place * 8 : place * 8 + 8, :] = force
        else:
            level[PLANAR.index(offset[:2])][...] = force


def pair_kernel(offered_ref, from_z_ref, unused_ref, both_ref):
    count = offered_ref.shape[0]
    both_ref[0:count, :] = offered_ref[...]
    both_ref[count:, :] = from_z_ref[...]


def merge_kernel(*refs):
    upward, *level = refs[: 1 + len(PLANAR)]
    outs = refs[2 + len(PLANAR) :]
    outs[0][...] = upward[0:8, :]
    for place, part in enumerate(level):
        outs[1 + place][...] = part[...] + upward[8 * place + 8 : 8 * place + 16, :]


def final_kernel(*refs):
    sums_ref, send_ref, *arrived = refs[:-2]
    forces_ref, energy_ref = refs[-2:]
    incoming = arrived[0][...]
    for part in arrived[1:]:
        incoming = incoming + part[...]
    high, low = split_two(jnp.concatenate([incoming[:4], incoming[:4]], 0))
    send = jnp.broadcast_to(send_ref[...], (8, send_ref.shape[1]))
    groups = sums_ref.shape[0] // 8
    hot = one_hot(send & (LANES - 1), row_codes(LANES))
    spread = [spread_groups(value, send // LANES, groups).astype(bf16) for value in (high, low)]
    back = dot_nt(jnp.concatenate(spread, 0), hot)
    back = back[: groups * 4] + back[groups * 4 :]
    for group in range(groups):
        own = sums_ref[group * 4 : group * 4 + 4, 0:LANES]
        partner = sums_ref[(groups + group) * 4 : (groups + group) * 4 + 4, LANES:]
        total = own - partner + back[group * 4 : group * 4 + 4]
        cols = slice(group * LANES, (group + 1) * LANES)
        forces_ref[:, cols] = total[0:3]
        energy_ref[:, cols] = own[3:4]


def whole(shape, dtype):
    return jax.ShapeDtypeStruct(shape, dtype)


def call(kernel, outs, name, scratch=(), specs=None, cost=None):
    more = {} if cost is None else dict(cost_estimate=cost)
    return pl.pallas_call(
        kernel,
        grid=(1,),
        in_specs=specs,
        out_specs=tuple(pl.BlockSpec(memory_space=pltpu.VMEM) for _ in outs),
        out_shape=outs,
        scratch_shapes=list(scratch),
        compiler_params=pltpu.CompilerParams(vmem_limit_bytes=VMEM_LIMIT),
        name=name,
        **more,
    )


def shifted(value, offset, sizes, sign):
    used = tuple(axis for axis, step in zip(sizes, offset) if step)
    dims = [size for name, size in used]
    pairs = []
    for flat in range(math.prod(dims)):
        place, rest = [], flat
        for size in reversed(dims):
            place.insert(0, rest % size)
            rest //= size
        target = 0
        for at, size in zip(place, dims):
            target = target * size + (at - sign) % size
        pairs.append((flat, target))
    return lax.ppermute(value, tuple(name for name, size in used), pairs)


def on_device(
    sizes,
    positions,
    features,
    species,
    species_scale,
    w_first,
    w_second,
    w_radial,
    w_mid,
    w_last,
    w_out,
    ghost_send,
    local_first,
    local_second,
    local_mask,
    ghost_owner,
    ghost_index,
    ghost_mask,
):
    channels, own_count = features.shape
    send_count = ghost_send.shape[0]
    bases = w_radial.shape[1]
    rows = channels + EXTRA
    groups = own_count // LANES
    blocks = len(ghost_offsets)
    whole_spec = pl.BlockSpec(memory_space=pltpu.VMEM)
    def tiles(value):
        return value.reshape(value.shape[0] // LANES, LANES)

    def fetching(kernel, name, outs, operands, kept):
        here = [pltpu.with_memory_space_constraint(value, pltpu.HBM) for value in operands]
        landing = operands[: len(operands) - kept]
        return call(
            kernel,
            outs + tuple(whole(value.shape, value.dtype) for value in operands[len(landing) :]),
            name,
            [pltpu.VMEM(value.shape, value.dtype) for value in landing]
            + [pltpu.SemaphoreType.DMA((len(operands),))],
            [pl.BlockSpec(memory_space=pltpu.HBM)] * len(operands),
        )(*here)

    own, right, offered, *weights, local, need, send = fetching(
        tables_kernel,
        "tables",
        (
            whole((rows, own_count), f32),
            whole((-(-own_count // GROUP * rows // 16) * 16, GROUP), bf16),
            whole((channels + OFFERED, send_count), bf16),
            whole((4 * QUAD * channels, QUAD * channels), bf16),
            whole((QUAD * channels, QUAD * 4 * bases), bf16),
            whole((QUAD * 2 * bases, QUAD * channels), bf16),
            whole((channels, LANES), f32),
            whole((local_first.shape[0] // LANES, LANES), jnp.int32),
            whole((8, LANES), jnp.int32),
        ),
        (
            positions,
            features,
            species.reshape(1, own_count),
            species_scale.reshape(1, species_scale.shape[0]),
            w_first,
            w_second,
            w_radial.T,
            w_mid,
            w_last,
            w_out.reshape(1, channels),
            tiles(local_first),
            tiles(local_second),
            tiles(local_mask),
            ghost_send.reshape(1, send_count),
        ),
        1,
    )
    from_z = shifted(offered, (0, 0, 1), sizes, 1)

    def scratch(per_step, hots):
        return [pltpu.VMEM((per_step, GROUP, QUAD * CHUNK), bf16) for _ in range(hots)] + [
            pltpu.VMEM((per_step, QUAD, channels, CHUNK), f32),
            pltpu.VMEM((per_step, QUAD, channels, CHUNK), f32),
            pltpu.VMEM((GROUP, LANES), bf16),
        ]

    def cost(slots):
        return pl.CostEstimate(flops=slots * 400000, bytes_accessed=slots * 12, transcendentals=slots * 200)

    quads = local.shape[0] * LANES // (QUAD * CHUNK)
    cuts = [0, quads // 5, quads * 2 // 5, quads * 7 // 10, quads * 4 // 5]
    tail_rows = local.shape[0] - (cuts[4] - 1) * QUAD * CHUNK // LANES

    def local_call(part, start, tail, after):
        operands = [local, own, right, *weights, *start, *tail, *after]
        first = cuts[part]
        size = cuts[part + 1] - first
        spare = cuts[4] if part == 2 else 0
        outs = (whole((groups * 8, GROUP), f32),) + ((whole((tail_rows, LANES), jnp.int32),) if spare else ())
        return call(
            functools.partial(
                local_kernel, channels, bases, first, size, spare, (len(start), len(tail) // 2, len(after))
            ),
            outs,
            "local_pairs",
            scratch(size, 2),
            [whole_spec] * len(operands),
            cost(size * QUAD * CHUNK),
        )(*operands)

    (sums,) = local_call(0, (), (), ())
    (both,) = call(
        pair_kernel, (whole((2 * offered.shape[0], send_count), bf16),), "two_blocks", specs=[whole_spec] * 3
    )(offered, from_z, sums)
    arrived = [from_z] + [shifted(both, (*step, 0), sizes, 1) for step in PLANAR]
    (sums,) = local_call(1, (sums,), (), (both,))
    ghost_lists = [tiles(value) for value in (ghost_owner, ghost_index, ghost_mask)]
    ghost_step = ghost_owner.shape[0] // (QUAD * CHUNK) // 4
    partner_rows = blocks * GROUP // LANES * 4
    table_rows = -(-blocks * rows // 16) * 16
    force = whole((8, send_count), f32)
    sums, upward, *level = call(
        functools.partial(ghost_kernel, ghost_step, channels, bases),
        (whole((groups * 8, GROUP), f32), whole((8 + 8 * len(PLANAR), send_count), f32)) + (force,) * len(PLANAR),
        "ghost_pairs",
        [
            pltpu.VMEM((table_rows, GROUP), bf16),
            pltpu.VMEM((groups * 4 + partner_rows, GROUP), f32),
            pltpu.VMEM((ghost_owner.shape[0] // LANES, LANES), jnp.int32),
            pltpu.VMEM((8, blocks * GROUP), f32),
        ]
        + scratch(ghost_step, 2),
        [whole_spec] * (9 + len(arrived)),
        cost(ghost_owner.shape[0]),
    )(*ghost_lists, own, *weights, sums, *arrived)
    upward = shifted(upward, (0, 0, 1), sizes, -1)
    sums, tail = local_call(2, (sums,), (), ())
    mine, *level = call(
        merge_kernel, (force,) * (1 + len(PLANAR)), "forces_upward", specs=[whole_spec] * (2 + len(PLANAR))
    )(upward, *level, sums)
    returned = [shifted(part, (*step, 0), sizes, -1) for part, step in zip(level, PLANAR)]
    (sums,) = local_call(3, (sums,), (tail, need), (mine,))
    forces, energy = call(
        final_kernel,
        (whole((3, own_count), f32), whole((1, own_count), f32)),
        "totals",
        specs=[whole_spec] * (3 + len(returned)),
    )(sums, send, mine, *returned)
    return forces, energy.reshape(own_count)


def solution(mesh):
    names = ("gx", "gy", "gz")
    sizes = tuple((name, mesh.shape[name]) for name in names)
    split = P(names)
    cols = P(None, names)
    in_specs = (cols, cols, split) + (P(),) * 7 + (split,) * 7
    return jax.shard_map(
        functools.partial(on_device, sizes),
        mesh=mesh,
        in_specs=in_specs,
        out_specs=(cols, split),
        check_vma=False,
    )
```

```python
import functools
import math

import jax
import jax.numpy as jnp
from jax import lax
from jax.experimental import pallas as pl
from jax.experimental.pallas import tpu as pltpu
from jax.sharding import PartitionSpec as P

basis_width = 24.0
domain_edge = 1.0
ghost_offsets = ((1, 0, 0), (0, 1, 0), (0, 0, 1), (1, 1, 0), (1, 0, 1), (0, 1, 1), (1, 1, 1))

PLANAR = ((1, 0), (0, 1), (1, 1))
EXTRA = 8
OFFERED = 16
GROUP = 256
LANES = 128
CHUNK = 256
QUAD = 4
VMEM_LIMIT = 48 * 1024 * 1024

NT = (((1,), (1,)), ((), ()))
f32 = jnp.float32
bf16 = jnp.bfloat16


def dot(left, right):
    return jnp.dot(left, right, preferred_element_type=f32)


def dot_nt(left, right):
    return lax.dot_general(left, right, NT, preferred_element_type=f32)


def iota(shape, dim):
    return lax.broadcasted_iota(jnp.int32, shape, dim)


def one_hot(entry, codes):
    entry = entry.astype(f32)
    entry = jnp.concatenate([entry, entry], 0).astype(bf16)
    entry = jnp.concatenate([entry] * (codes.shape[0] // 16), 0)
    pieces = [
        jnp.where(codes == entry[:, start : start + LANES], bf16(1), bf16(0))
        for start in range(0, entry.shape[1], LANES)
    ]
    return jnp.concatenate(pieces, 1)


def row_codes(count):
    return iota((count, LANES), 0).astype(f32).astype(bf16)


def split_two(value):
    high = value.astype(bf16).astype(f32)
    return high, value - high


def coord_rows(coords, gain):
    high, low = split_two(coords)
    return jnp.concatenate([high, gain, low, jnp.zeros_like(gain)], 0)


def eye(count):
    return (iota((count, count), 0) == iota((count, count), 1)).astype(bf16)


def fetch(sources, targets, landed):
    copies = [
        pltpu.make_async_copy(source, target, landed.at[place])
        for place, (source, target) in enumerate(zip(sources, targets))
    ]
    for copy in copies:
        copy.start()
    for copy in copies:
        copy.wait()


def tables_kernel(*refs):
    own_ref, right_ref, offered_ref, mats_ref, radial_ref, radial_t_ref, out_ref, list_ref, need_ref = refs[14:23]
    send_ref = refs[23]
    landing = refs[24:37]
    fetch(refs[:14], landing + (send_ref,), refs[37])
    positions_ref, features_ref, species_ref, scale_ref, w_first_ref, w_second_ref = landing[:6]
    radial_w_ref, w_mid_ref, w_last_ref, w_out_ref, first_ref, second_ref, mask_ref = landing[6:]
    channels = features_ref.shape[0]
    count = features_ref.shape[1]
    species = species_ref[...]
    gain = jnp.zeros((1, count), f32)
    for kind in range(scale_ref.shape[1]):
        scale = scale_ref[:, kind : kind + 1].astype(f32)
        gain = jnp.where(species == kind, scale, gain)
    positions = positions_ref[...]
    left = dot(w_first_ref[...], features_ref[...]).astype(bf16).astype(f32)
    right = dot(w_second_ref[...], features_ref[...]).astype(bf16).astype(f32)
    own_ref[0:channels, :] = 0.5 * left
    own_ref[channels:, :] = jnp.concatenate([positions, gain, positions, gain], 0)
    column = jnp.concatenate([0.5 * right, coord_rows(positions, gain)], 0)
    groups = count // GROUP
    rows = channels + EXTRA
    table = jnp.concatenate([column[:, group * GROUP : (group + 1) * GROUP] for group in range(groups)], 0)
    spare = right_ref.shape[0] - groups * rows
    if spare:
        table = jnp.concatenate([table, jnp.zeros((spare, GROUP), f32)], 0)
    table = table.astype(bf16)
    right_ref[...] = table
    send = jnp.broadcast_to(send_ref[...], (8, send_ref.shape[1]))
    picked = dot(table, one_hot(send & (GROUP - 1), row_codes(GROUP)))
    chosen = group_pick(picked, send // GROUP, rows, groups)
    chosen = jnp.concatenate([chosen, jnp.zeros((OFFERED - EXTRA, chosen.shape[1]), f32)], 0)
    offered_ref[...] = chosen.astype(bf16)

    unit = eye(channels)
    w_mid = w_mid_ref[...]
    w_last = w_last_ref[...]
    last_t = dot_nt(unit, w_last).astype(bf16)
    mid_t = dot_nt(unit, w_mid).astype(bf16)
    wide = QUAD * channels
    for place, matrix in enumerate((w_mid, w_last, last_t, mid_t)):
        mats_ref[place * wide : (place + 1) * wide, :] = (0.5 * diagonal_copies(matrix)).astype(bf16)
    bases = radial_w_ref.shape[0]
    high, low = split_two(radial_w_ref[...])
    high = high.astype(bf16)
    low = low.astype(bf16)
    spread = dot_nt(unit, jnp.concatenate([high, high, low, low], 0)).astype(bf16)
    radial_ref[...] = (0.5 * diagonal_copies(spread)).astype(bf16)
    radial_t_ref[...] = diagonal_copies(jnp.concatenate([high, low], 0)).astype(bf16)
    w_out = w_out_ref[...]
    diagonal = jnp.where(iota((channels, channels), 0) == iota((channels, channels), 1), w_out, 0.0)
    out_ref[...] = jnp.broadcast_to(jnp.sum(diagonal, axis=1, keepdims=True), (channels, LANES))
    bits = (count - 1).bit_length()
    codes = pack(first_ref[...], second_ref[...], mask_ref[...], bits)
    live = [codes[start : start + 8] & 1 for start in range(0, codes.shape[0], 8)]
    need_ref[...] = gather_live(codes, live, 2 * bits + 1, list_ref)


def pack(owner, partner, mask, partner_bits):
    return (owner * 2**partner_bits + partner) * 2 + mask


def gather_live(codes, live, bits, list_ref):
    tiles = len(live)
    sub = iota((8, LANES), 0)
    passed = jnp.zeros((8, LANES), jnp.int32)
    words = []
    for tile in range(tiles):
        dead = 1 - live[tile]
        for step in (1, 2, 4):
            dead = dead + jnp.where(sub >= step, pltpu.roll(dead, step, 0), 0)
        move = (passed + dead) * 2**bits + codes[tile * 8 : tile * 8 + 8]
        words.append(jnp.where(live[tile] != 0, move, 0))
        passed = passed + jnp.broadcast_to(dead[7:8], (8, LANES))
    none = jnp.zeros((8, LANES), jnp.int32)
    for power in range((tiles * 8).bit_length()):
        step = 2**power
        moving = [jnp.where((word & 2 ** (bits + power)) != 0, word, 0) for word in words]
        if step < 8:
            rolled = [pltpu.roll(word, 8 - step, 0) for word in moving] + [none]
            come = [jnp.where(sub < 8 - step, rolled[tile], rolled[tile + 1]) for tile in range(tiles)]
        else:
            come = (moving[step // 8 :] + [none] * tiles)[:tiles]
        words = [word - gone + new for word, gone, new in zip(words, moving, come)]
    for tile, word in enumerate(words):
        list_ref[tile * 8 : tile * 8 + 8, :] = word & (2**bits - 1)
    return tiles * 8 - passed


def diagonal_copies(matrix):
    high, wide = matrix.shape
    repeat = (iota((wide, QUAD * wide), 0) == iota((wide, QUAD * wide), 1) % wide).astype(bf16)
    row = dot(matrix, repeat)
    full = jnp.concatenate([row] * QUAD, 0)
    return jnp.where(iota(full.shape, 0) // high == iota(full.shape, 1) // wide, full, 0.0)


def group_pick(values, high, rows, groups):
    high = jnp.concatenate([high] * (rows // 8), 0)
    chosen = values[:rows]
    for group in range(1, groups):
        chosen = jnp.where(high == group, values[group * rows : (group + 1) * rows], chosen)
    return chosen


def spread_groups(values, high, groups):
    second = iota(values.shape, 0) // 4
    pieces = [jnp.where(high == second + group, values, 0.0) for group in range(0, groups, 2)]
    return jnp.concatenate(pieces, 0)


def lane_pick(table_ref, place, first=0):
    rows, count = table_ref.shape[0] - first, table_ref.shape[1]
    lane = jnp.concatenate([place & (LANES - 1)] * (rows // 8), 0)
    high = jnp.concatenate([place // LANES] * (rows // 8), 0)
    chosen = None
    for group in range(count // LANES):
        part = table_ref[first:, group * LANES : (group + 1) * LANES]
        picked = jnp.take_along_axis(part, lane, axis=1, mode="promise_in_bounds")
        chosen = picked if chosen is None else jnp.where(high == group, picked, chosen)
    return chosen


def sum_rows(values, steps):
    for step in steps:
        values = values + pltpu.roll(values, step, 0)
    return values


def pair_tasks(
    own_groups,
    partner_groups,
    channels,
    bases,
    list_ref,
    own_ref,
    right_ref,
    mats_ref,
    radial_ref,
    radial_t_ref,
    out_ref,
    sums,
    hot,
    hot_wide,
    slope_one,
    slope_two,
    codes_ref,
):
    rows = channels + EXTRA
    line = CHUNK // LANES
    block = QUAD * line
    wide = QUAD * channels
    w_out = jnp.concatenate([out_ref[...]] * line, 1)
    centers = iota((bases, CHUNK), 0).astype(f32) * (1.0 / (bases - 1))
    last = iota((8, CHUNK), 0) % 4 == 3
    partner_bits = (partner_groups * LANES - 1).bit_length()
    quads = range(QUAD)
    codes_ref[...] = row_codes(GROUP)

    def matrix(place):
        return mats_ref[place * wide : (place + 1) * wide, :]

    def part(values, number, size=channels):
        return values[number * size : (number + 1) * size]

    def silu_pair(half):
        grow = jnp.tanh(half)
        plus = 1.0 + grow
        hidden = half * plus
        return hidden, plus + hidden * (1.0 - grow)

    def task(first, number, source=list_ref):
        at = pl.multiple_of(first * block, block)
        code_rows = source[pl.ds(at, block), :]
        owners, partners, lives, projected, shifts, squares, weights, stacks, slopes = ([] for _ in range(9))
        for quad in quads:
            cols = slice(quad * CHUNK, (quad + 1) * CHUNK)
            code = jnp.concatenate(
                [
                    jnp.broadcast_to(code_rows[row : row + 1, :], (8, LANES))
                    for row in range(quad * line, (quad + 1) * line)
                ],
                1,
            )
            lives.append((code & 1).astype(f32))
            partner = (code >> 1) & (2**partner_bits - 1)
            owner = code >> (partner_bits + 1)
            owners.append(owner)
            partners.append(partner)
            hot[number, 0:LANES, cols] = one_hot(owner & (LANES - 1), codes_ref[0:LANES, :])
            wide = one_hot(partner & (GROUP - 1), codes_ref[...])
            hot_wide[number, :, cols] = wide
            hot[number, LANES:, cols] = wide[0:LANES] + wide[LANES:]
            yield
        for quad in quads:
            cols = slice(quad * CHUNK, (quad + 1) * CHUNK)
            own_vals = jnp.concatenate(
                [lane_pick(own_ref, owners[quad][:, start : start + LANES]) for start in range(0, CHUNK, LANES)], 1
            )
            partner_vals = group_pick(
                dot(right_ref[...], hot_wide[number, :, cols]),
                partners[quad] // GROUP,
                rows,
                partner_groups * LANES // GROUP,
            )
            projected.append(own_vals[:channels] + partner_vals[:channels])
            own_coords = own_vals[channels:]
            extra = partner_vals[channels:]
            partner_coords = extra + pltpu.roll(extra, 4, 0)
            shift = partner_coords - own_coords
            squared = sum_rows(jnp.where(last, 0.0, shift * shift), (2, 1))
            gain = sum_rows(jnp.where(last, own_coords * partner_coords, 0.0), (2, 1))
            weights.append(lives[quad] * gain)
            away = squared - centers
            basis = jnp.exp(-basis_width * (away * away))
            basis_high, basis_low = split_two(basis)
            stacks.append(jnp.concatenate([basis_high, basis_low, basis_high, basis_low], 0).astype(bf16))
            slopes.append((-2.0 * basis_width) * away * basis)
            shifts.append(shift)
            squares.append(squared)
            yield
        radial = dot(radial_ref[...], jnp.concatenate(stacks, 0))
        yield
        pieces = []
        for quad in quads:
            hidden, slope_one[number, quad] = silu_pair(projected[quad] + part(radial, quad))
            pieces.append(hidden.astype(bf16))
        yield
        half = dot(matrix(0), jnp.concatenate(pieces, 0))
        yield
        pieces = []
        for quad in quads:
            hidden, slope_two[number, quad] = silu_pair(part(half, quad))
            pieces.append(hidden.astype(bf16))
        yield
        half = dot(matrix(1), jnp.concatenate(pieces, 0))
        yield
        pieces = []
        readouts = []
        for quad in quads:
            hidden, slope = silu_pair(part(half, quad))
            terms = w_out * hidden
            terms = sum(terms[start : start + 8] for start in range(8, channels, 8)) + terms[:8]
            readouts.append(sum_rows(terms, (4, 2, 1)))
            pieces.append(((0.5 * w_out) * slope).astype(bf16))
        yield
        back = dot(matrix(2), jnp.concatenate(pieces, 0))
        yield
        pieces = [(part(back, quad) * slope_two[number, quad]).astype(bf16) for quad in quads]
        back = dot(matrix(3), jnp.concatenate(pieces, 0))
        yield
        pieces = [(part(back, quad) * slope_one[number, quad]).astype(bf16) for quad in quads]
        back = dot(radial_t_ref[...], jnp.concatenate(pieces, 0))
        yield
        parts = []
        for quad in quads:
            two = part(back, quad, 2 * bases)
            readout_slope = sum_rows((two[:bases] + two[bases:]) * slopes[quad], (4, 2, 1))
            near = jnp.maximum(1.0 - squares[quad], 0.0)
            weight_near = weights[quad] * near
            energy = weight_near * near * readouts[quad]
            slope = weight_near * (near * readout_slope - 2.0 * readouts[quad])
            push = (2.0 * slope) * shifts[quad]
            values = jnp.where(last, energy, push)
            parts.append(
                jnp.concatenate(
                    [
                        spread_groups(values, owners[quad] // LANES, own_groups),
                        spread_groups(values, partners[quad] // LANES, partner_groups),
                    ],
                    0,
                ).astype(bf16)
            )
        yield
        sums[...] += dot_nt(jnp.concatenate(parts, 1), hot[number])

    return task


def run(tasks, side=None, later=()):
    running, waiting = [], list(tasks)
    while running or waiting or side is not None:
        if waiting:
            running.append(waiting.pop(0))
        if side is not None and next(side, side) is side:
            side = None
            waiting += later
        for _ in range(3):
            running = [task for task in running if next(task, task) is not task]


def run_rest(task, done, rest):
    steps, size = rest

    def step(index, unused):
        run([task(done + index * size + number, number) for number in range(size)])
        return unused

    lax.fori_loop(0, steps, step, 0)


def fold(list_ref, source, target, turns):
    rows = slice(target * 8, target * 8 + 8)
    spare = slice(source * 8, source * 8 + 8)
    kept = list_ref[rows, :]
    moving = pltpu.roll(list_ref[spare, :], 4, 0)
    for turn in range(turns):
        moving = pltpu.roll(moving, 1, 1)
        if turn % 4 == 3:
            moving = pltpu.roll(moving, 3, 0)
        placed = jnp.where(kept == 0, moving, 0)
        kept = kept + placed
        moving = moving - placed
        if turn % 2:
            yield
    list_ref[rows, :] = kept
    list_ref[spare, :] = moving


def rest_of(list_ref, need, done, total):
    left = total - done
    size = next(size for size in (3, 2, 1) if left % size == 0)
    rows = QUAD * CHUNK // LANES
    found = jnp.max(list_ref[done * rows : total * rows, :])
    steps = jnp.maximum(jnp.max(need) - done * rows + size * rows - 1, 0) // (size * rows)
    return jnp.where(found > 0, steps, 0), size


def local_kernel(channels, bases, first_quad, quad_count, spare, counts, *refs):
    has_sums, has_tail, ordering = counts
    count = 7 + has_sums + 2 * has_tail + ordering
    codes, own, right, *weights = refs[:7]
    outs = 1 + (spare > 0)
    sums = refs[count]
    scratch = refs[count + outs :]
    sums[...] = refs[7][...] if has_sums else jnp.zeros_like(sums)
    groups = own.shape[1] // LANES
    task = pair_tasks(groups, groups, channels, bases, codes, own, right, *weights, sums, *scratch)
    rows = QUAD * CHUNK // LANES
    if has_tail:
        tail, need = refs[7 + has_sums : 9 + has_sums]
        end = first_quad + quad_count
        tasks = [task(first_quad + number, number) for number in range(quad_count - 1)]
        run([task(0, quad_count - 1, tail)] + tasks)
        needed = need[...] - (end - 1) * rows
        rest = rest_of(tail, needed, 1, tail.shape[0] // rows)
        run_rest(lambda quad, slot: task(quad, slot, tail), 1, rest)
        return
    side = None
    if spare:
        tail = refs[count + 1]
        tail[...] = codes[(spare - 1) * rows :, :]

        def folds():
            yield from fold(tail, rows // 8, rows // 8 - 1, 10)
            yield from fold(tail, rows // 8 + 1, rows // 8 - 1, 6)

        side = folds()
    run([task(first_quad + number, number) for number in range(quad_count)], side)


def near_ones(codes, bits, own_ref, channels, coords_ref):
    sub = iota((8, LANES), 0)
    found = []
    for start in range(0, codes.shape[0], 8):
        tile = codes[start : start + 8]
        squared = jnp.zeros((8, LANES), f32)
        for low in range(4):
            code = jnp.where(
                sub < 4,
                jnp.broadcast_to(tile[low : low + 1], (8, LANES)),
                jnp.broadcast_to(tile[low + 4 : low + 5], (8, LANES)),
            )
            shift = lane_pick(coords_ref, (code >> 1) & (2**bits - 1)) - lane_pick(own_ref, code >> (bits + 1), channels)
            square = shift * shift
            total = square + pltpu.roll(square, 7, 0) + pltpu.roll(square, 6, 0)
            if low:
                total = pltpu.roll(total, low, 0)
            squared = jnp.where(sub % 4 == low, total, squared)
        found.append(jnp.where(squared < 1.001, tile & 1, 0))
    return found


def ghost_kernel(quad_count, channels, bases, *refs):
    blocks = len(ghost_offsets)
    owner, partner, mask, own, *weights = refs[:8]
    sums_in = refs[8]
    arrived = refs[9 : 10 + len(PLANAR)]
    sums_out, upward, *level = refs[10 + len(PLANAR) : 12 + 2 * len(PLANAR)]
    table, sums, codes_ref, coords_ref, *scratch = refs[12 + 2 * len(PLANAR) :]
    groups = own.shape[1] // LANES
    partner_groups = blocks * GROUP // LANES
    sums[...] = jnp.zeros_like(sums)
    pieces = []
    for offset in ghost_offsets:
        if offset[:2] == (0, 0):
            source, start = arrived[0], 0
        else:
            source, start = arrived[1 + PLANAR.index(offset[:2])], offset[2] * (channels + OFFERED)
        extra = source[start + channels : start + channels + OFFERED, :].astype(f32)
        moved = jnp.concatenate(
            [extra[axis : axis + 1] + extra[axis + 4 : axis + 5] + domain_edge * offset[axis] for axis in range(3)], 0
        )
        pieces += [source[start : start + channels, :].astype(f32), coord_rows(moved, extra[3:4])]
        place = ghost_offsets.index(offset) * GROUP
        coords_ref[:, place : place + GROUP] = jnp.concatenate([moved, extra[3:4], moved, extra[3:4]], 0)
    pieces.append(jnp.zeros((table.shape[0] - blocks * (channels + EXTRA), GROUP), f32))
    table[...] = jnp.concatenate(pieces, 0).astype(bf16)
    bits = (partner_groups * LANES - 1).bit_length()
    codes = pack(owner[...], partner[...], mask[...], bits)
    live = near_ones(codes, bits, own, channels, coords_ref)
    need = gather_live(codes, live, bits + (own.shape[1] - 1).bit_length() + 1, codes_ref)
    tile = quad_count * QUAD * CHUNK // LANES // 8
    task = pair_tasks(groups, partner_groups, channels, bases, codes_ref, own, table, *weights, sums, *scratch)
    last = quad_count - 1
    run([task(number, number) for number in range(last)], fold(codes_ref, tile, tile - 1, 4), [task(last, last)])
    total = owner.shape[0] * LANES // (QUAD * CHUNK)
    run_rest(task, quad_count, rest_of(codes_ref, need, quad_count, total))
    first = groups * 4
    sums_out[0:first, :] = sums_in[0:first, :] + sums[0:first, :]
    sums_out[first:, :] = sums_in[first:, :]
    for block, offset in enumerate(ghost_offsets):
        halves = []
        for half in range(GROUP // LANES):
            start = first + (block * (GROUP // LANES) + half) * 4
            halves.append(sums[start : start + 4, LANES:])
        force = -jnp.concatenate(halves, 1)
        force = jnp.concatenate([force, jnp.zeros_like(force)], 0)
        if offset[2]:
            place = 0 if offset[:2] == (0, 0) else 1 + PLANAR.index(offset[:2])
            upward[place * 8 : place * 8 + 8, :] = force
        else:
            level[PLANAR.index(offset[:2])][...] = force


def pair_kernel(offered_ref, from_z_ref, unused_ref, both_ref):
    count = offered_ref.shape[0]
    both_ref[0:count, :] = offered_ref[...]
    both_ref[count:, :] = from_z_ref[...]


def merge_kernel(*refs):
    upward, *level = refs[: 1 + len(PLANAR)]
    outs = refs[2 + len(PLANAR) :]
    outs[0][...] = upward[0:8, :]
    for place, part in enumerate(level):
        outs[1 + place][...] = part[...] + upward[8 * place + 8 : 8 * place + 16, :]


def final_kernel(*refs):
    sums_ref, send_ref, *arrived = refs[:-2]
    forces_ref, energy_ref = refs[-2:]
    incoming = arrived[0][...]
    for part in arrived[1:]:
        incoming = incoming + part[...]
    high, low = split_two(jnp.concatenate([incoming[:4], incoming[:4]], 0))
    send = jnp.broadcast_to(send_ref[...], (8, send_ref.shape[1]))
    groups = sums_ref.shape[0] // 8
    hot = one_hot(send & (LANES - 1), row_codes(LANES))
    spread = [spread_groups(value, send // LANES, groups).astype(bf16) for value in (high, low)]
    back = dot_nt(jnp.concatenate(spread, 0), hot)
    back = back[: groups * 4] + back[groups * 4 :]
    for group in range(groups):
        own = sums_ref[group * 4 : group * 4 + 4, 0:LANES]
        partner = sums_ref[(groups + group) * 4 : (groups + group) * 4 + 4, LANES:]
        total = own - partner + back[group * 4 : group * 4 + 4]
        cols = slice(group * LANES, (group + 1) * LANES)
        forces_ref[:, cols] = total[0:3]
        energy_ref[:, cols] = own[3:4]


def whole(shape, dtype):
    return jax.ShapeDtypeStruct(shape, dtype)


def call(kernel, outs, name, scratch=(), specs=None, cost=None):
    more = {} if cost is None else dict(cost_estimate=cost)
    return pl.pallas_call(
        kernel,
        grid=(1,),
        in_specs=specs,
        out_specs=tuple(pl.BlockSpec(memory_space=pltpu.VMEM) for _ in outs),
        out_shape=outs,
        scratch_shapes=list(scratch),
        compiler_params=pltpu.CompilerParams(vmem_limit_bytes=VMEM_LIMIT),
        name=name,
        **more,
    )


def shifted(value, offset, sizes, sign):
    used = tuple(axis for axis, step in zip(sizes, offset) if step)
    dims = [size for name, size in used]
    pairs = []
    for flat in range(math.prod(dims)):
        place, rest = [], flat
        for size in reversed(dims):
            place.insert(0, rest % size)
            rest //= size
        target = 0
        for at, size in zip(place, dims):
            target = target * size + (at - sign) % size
        pairs.append((flat, target))
    return lax.ppermute(value, tuple(name for name, size in used), pairs)


def on_device(
    sizes,
    positions,
    features,
    species,
    species_scale,
    w_first,
    w_second,
    w_radial,
    w_mid,
    w_last,
    w_out,
    ghost_send,
    local_first,
    local_second,
    local_mask,
    ghost_owner,
    ghost_index,
    ghost_mask,
):
    channels, own_count = features.shape
    send_count = ghost_send.shape[0]
    bases = w_radial.shape[1]
    rows = channels + EXTRA
    groups = own_count // LANES
    blocks = len(ghost_offsets)
    whole_spec = pl.BlockSpec(memory_space=pltpu.VMEM)
    def tiles(value):
        return value.reshape(value.shape[0] // LANES, LANES)

    def fetching(kernel, name, outs, operands, kept):
        here = [pltpu.with_memory_space_constraint(value, pltpu.HBM) for value in operands]
        landing = operands[: len(operands) - kept]
        return call(
            kernel,
            outs + tuple(whole(value.shape, value.dtype) for value in operands[len(landing) :]),
            name,
            [pltpu.VMEM(value.shape, value.dtype) for value in landing]
            + [pltpu.SemaphoreType.DMA((len(operands),))],
            [pl.BlockSpec(memory_space=pltpu.HBM)] * len(operands),
        )(*here)

    own, right, offered, *weights, local, need, send = fetching(
        tables_kernel,
        "tables",
        (
            whole((rows, own_count), f32),
            whole((-(-own_count // GROUP * rows // 16) * 16, GROUP), bf16),
            whole((channels + OFFERED, send_count), bf16),
            whole((4 * QUAD * channels, QUAD * channels), bf16),
            whole((QUAD * channels, QUAD * 4 * bases), bf16),
            whole((QUAD * 2 * bases, QUAD * channels), bf16),
            whole((channels, LANES), f32),
            whole((local_first.shape[0] // LANES, LANES), jnp.int32),
            whole((8, LANES), jnp.int32),
        ),
        (
            positions,
            features,
            species.reshape(1, own_count),
            species_scale.reshape(1, species_scale.shape[0]),
            w_first,
            w_second,
            w_radial.T,
            w_mid,
            w_last,
            w_out.reshape(1, channels),
            tiles(local_first),
            tiles(local_second),
            tiles(local_mask),
            ghost_send.reshape(1, send_count),
        ),
        1,
    )
    from_z = shifted(offered, (0, 0, 1), sizes, 1)

    def scratch(per_step, hots):
        return [pltpu.VMEM((per_step, GROUP, QUAD * CHUNK), bf16) for _ in range(hots)] + [
            pltpu.VMEM((per_step, QUAD, channels, CHUNK), f32),
            pltpu.VMEM((per_step, QUAD, channels, CHUNK), f32),
            pltpu.VMEM((GROUP, LANES), bf16),
        ]

    def cost(slots):
        return pl.CostEstimate(flops=slots * 400000, bytes_accessed=slots * 12, transcendentals=slots * 200)

    quads = local.shape[0] * LANES // (QUAD * CHUNK)
    cuts = [0, quads // 5, quads * 2 // 5, quads * 7 // 10, quads * 4 // 5]
    tail_rows = local.shape[0] - (cuts[4] - 1) * QUAD * CHUNK // LANES

    def local_call(part, start, tail, after):
        operands = [local, own, right, *weights, *start, *tail, *after]
        first = cuts[part]
        size = cuts[part + 1] - first
        spare = cuts[4] if part == 2 else 0
        outs = (whole((groups * 8, GROUP), f32),) + ((whole((tail_rows, LANES), jnp.int32),) if spare else ())
        return call(
            functools.partial(
                local_kernel, channels, bases, first, size, spare, (len(start), len(tail) // 2, len(after))
            ),
            outs,
            "local_pairs",
            scratch(size, 2),
            [whole_spec] * len(operands),
            cost(size * QUAD * CHUNK),
        )(*operands)

    (sums,) = local_call(0, (), (), ())
    (both,) = call(
        pair_kernel, (whole((2 * offered.shape[0], send_count), bf16),), "two_blocks", specs=[whole_spec] * 3
    )(offered, from_z, sums)
    arrived = [from_z] + [shifted(both, (*step, 0), sizes, 1) for step in PLANAR]
    (sums,) = local_call(1, (sums,), (), (both,))
    ghost_lists = [tiles(value) for value in (ghost_owner, ghost_index, ghost_mask)]
    ghost_step = ghost_owner.shape[0] // (QUAD * CHUNK) // 4
    partner_rows = blocks * GROUP // LANES * 4
    table_rows = -(-blocks * rows // 16) * 16
    force = whole((8, send_count), f32)
    sums, upward, *level = call(
        functools.partial(ghost_kernel, ghost_step, channels, bases),
        (whole((groups * 8, GROUP), f32), whole((8 + 8 * len(PLANAR), send_count), f32)) + (force,) * len(PLANAR),
        "ghost_pairs",
        [
            pltpu.VMEM((table_rows, GROUP), bf16),
            pltpu.VMEM((groups * 4 + partner_rows, GROUP), f32),
            pltpu.VMEM((ghost_owner.shape[0] // LANES, LANES), jnp.int32),
            pltpu.VMEM((8, blocks * GROUP), f32),
        ]
        + scratch(ghost_step, 2),
        [whole_spec] * (9 + len(arrived)),
        cost(ghost_owner.shape[0]),
    )(*ghost_lists, own, *weights, sums, *arrived)
    upward = shifted(upward, (0, 0, 1), sizes, -1)
    sums, tail = local_call(2, (sums,), (), ())
    mine, *level = call(
        merge_kernel, (force,) * (1 + len(PLANAR)), "forces_upward", specs=[whole_spec] * (2 + len(PLANAR))
    )(upward, *level, sums)
    returned = [shifted(part, (*step, 0), sizes, -1) for part, step in zip(level, PLANAR)]
    (sums,) = local_call(3, (sums,), (tail, need), (mine,))
    forces, energy = call(
        final_kernel,
        (whole((3, own_count), f32), whole((1, own_count), f32)),
        "totals",
        specs=[whole_spec] * (3 + len(returned)),
    )(sums, send, mine, *returned)
    return forces, energy.reshape(own_count)


def solution(mesh):
    names = ("gx", "gy", "gz")
    sizes = tuple((name, mesh.shape[name]) for name in names)
    split = P(names)
    cols = P(None, names)
    in_specs = (cols, cols, split) + (P(),) * 7 + (split,) * 7
    return jax.shard_map(
        functools.partial(on_device, sizes),
        mesh=mesh,
        in_specs=in_specs,
        out_specs=(cols, split),
        check_vma=False,
    )
```
